32 devices in a mesh: ctx: 16 (over z, y, x), panel: 2 (over core).
Axes of the slice: x: 2, y: 2, z: 4, core: 2. Of those that a mesh axis runs over, the one named last changes fastest.
Arguments:
- se_streams: bfloat16 [3, 2304, 4096], P(None, 'ctx', 'panel'), may hold values from -6 to 6
- se_short: float32 [3, 3, 4096], P(None, None, 'panel'), may hold values from -2 to 2
- se_filter: float32 [7, 4096], P(None, 'panel'), may hold values from -2 to 2
- medium_projected_streams: bfloat16 [3, 2304, 4096], P(None, 'ctx', 'panel'), may hold values from -6 to 6
- mr_short: float32 [3, 3, 4096], P(None, None, 'panel'), may hold values from -2 to 2
- medium_filter_raw: float32 [128, 4096], P(None, 'panel'), may hold values from -0.9 to 0.9
- mr_decay: float32 [4096], P('panel'), may hold values from 0.003 to 0.1
- queries: bfloat16 [2304, 4096], P('ctx', 'panel'), may hold values from -180 to 180
- keys: bfloat16 [2304, 4096], P('ctx', 'panel'), may hold values from -6 to 6
- values: bfloat16 [2304, 4096], P('ctx', 'panel'), may hold values from -6 to 6
Outputs:
- se_out: bfloat16 [2304, 4096], P('ctx', 'panel')
- mr_out: bfloat16 [2304, 4096], P('ctx', 'panel')
- attn_out: bfloat16 [2304, 4096], P('ctx', 'panel')
The draws below stay inside these ranges and needn't reach their ends.
All inputs are finite; a program needn't handle non-finite values.
Results may differ from the reference program's by a relative error of at most 0.008.
Values may be sent and summed in bfloat16 or wider, within the bound.
No kernel may reach another device: no remote copies, remote signals or barrier semaphores. Data moves between devices by JAX's collectives and lax.ppermute only.
A program may use at most 64 MiB of HBM per device.

```python
import math
import jax
import jax.numpy as jnp
from jax import lax

CHANNEL_SHARD = 4096
HD = 128
TOKENS_PER_SHARD = 144
FEATURIZER_TAPS = 3
LSE = 7
MEDIUM_TAPS = 128
S = 2304
N_CTX = 16


def pair_draw(key):
    base = jax.random.fold_in(key, 11)
    key_q, key_k = jax.random.split(base)
    query_all = jax.random.truncated_normal(key_q, -6.0, 6.0, (S, CHANNEL_SHARD), jnp.float32)
    key_all = jax.random.truncated_normal(key_k, -6.0, 6.0, (S, CHANNEL_SHARD), jnp.float32)
    return (query_all, key_all)


def draw_queries(key, part):
    return pair_draw(key)[0].astype(jnp.bfloat16)


def draw_keys(key, part):
    return pair_draw(key)[1].astype(jnp.bfloat16)


def level_of(own_key, extent, pieces, low, high):
    loudness = 1.0
    for axis_at, shards_of in pieces:
        heights = jax.random.uniform(jax.random.fold_in(jax.random.fold_in(own_key, 6), axis_at), (shards_of,), jnp.float32, low / len(pieces), high / len(pieces))
        loudness = loudness * jnp.repeat(jnp.exp(heights), extent[axis_at] // shards_of).reshape((-1,) + (1,) * (len(extent) - 1 - axis_at))
    return loudness


def gaussian(own_key, dims, scale, reach, pieces=(), kind=jnp.bfloat16):
    array = scale * jax.random.normal(own_key, dims, jnp.float32)
    if pieces:
        array = array * level_of(own_key, dims, pieces, -0.22, 0.18)
    return jnp.clip(array, -reach, reach).astype(kind)


def setup_inputs(seed: int = 0) -> dict:
    key_list = jax.random.split(jax.random.key(seed), 11)
    se_streams = gaussian(key_list[0], (3, S, CHANNEL_SHARD), 1.0, 6.0, ((1, 16), (2, 2)))
    se_short = gaussian(key_list[1], (3, FEATURIZER_TAPS, CHANNEL_SHARD), 0.4, 2.0, ((2, 2),), jnp.float32)
    se_filter = gaussian(key_list[2], (LSE, CHANNEL_SHARD), 0.4, 2.0, ((1, 2),), jnp.float32)
    medium_projected_streams = gaussian(key_list[3], (3, S, CHANNEL_SHARD), 1.0, 6.0, ((1, 16), (2, 2)))
    mr_short = gaussian(key_list[4], (3, FEATURIZER_TAPS, CHANNEL_SHARD), 0.4, 2.0, ((2, 2),), jnp.float32)
    medium_filter_raw = gaussian(key_list[5], (MEDIUM_TAPS, CHANNEL_SHARD), 0.15, 0.9, ((1, 2),), jnp.float32)
    mr_decay = jnp.clip(jnp.exp(math.log(0.1) - 3.506558 * jax.random.uniform(key_list[6], (CHANNEL_SHARD,), jnp.float32) ** level_of(key_list[6], (CHANNEL_SHARD,), ((0, 2),), -0.2, 0.2)), 0.003, 0.1)
    queries = draw_queries(jax.random.fold_in(key_list[10], 71), 0)
    keys = draw_keys(jax.random.fold_in(key_list[10], 71), 0)
    values = gaussian(key_list[9], (S, CHANNEL_SHARD), 1.0, 6.0, ((0, 16), (1, 2)))
    return {"se_streams": se_streams, "se_short": se_short, "se_filter": se_filter, "medium_projected_streams": medium_projected_streams, "mr_short": mr_short, "medium_filter_raw": medium_filter_raw, "mr_decay": mr_decay, "queries": queries, "keys": keys, "values": values}


def featurize(ext, short):
    taps = short.shape[1]
    count = ext.shape[1]
    total = short[:, 0][:, None, :] * ext[:, taps - 1:count, :].astype(jnp.float32)
    for j in range(1, taps):
        total = total + short[:, j][:, None, :] * ext[:, taps - 1 - j:count - j, :].astype(jnp.float32)
    return total

def long_conv(product, filt):
    taps = filt.shape[0]
    count = product.shape[0]
    pf = product.astype(jnp.float32)
    total = filt[0][None, :] * pf[taps - 1:count]
    for j in range(1, taps):
        total = total + filt[j][None, :] * pf[taps - 1 - j:count - j]
    return total

def hyena_full(streams, short, filt):
    width = math.gcd(CHANNEL_SHARD, 256)
    nblk = CHANNEL_SHARD // width
    taps = filt.shape[0]
    blocks = streams.reshape(3, S, nblk, width).transpose(2, 0, 1, 3)
    shorts = short.reshape(3, FEATURIZER_TAPS, nblk, width).transpose(2, 0, 1, 3)
    filts = filt.reshape(taps, nblk, width).transpose(1, 0, 2)

    def one(args):
        block, sblk, fblk = args
        ext = jnp.concatenate([jnp.zeros((3, FEATURIZER_TAPS - 1, width), block.dtype), block], axis=1)
        feats = featurize(ext, sblk)
        product = (feats[1] * feats[2]).astype(jnp.bfloat16)
        padded = jnp.concatenate([jnp.zeros((taps - 1, width), jnp.bfloat16), product], axis=0)
        return feats[0] * long_conv(padded, fblk)
    out = lax.map(one, (blocks, shorts, filts))
    return out.transpose(1, 0, 2).reshape(S, CHANNEL_SHARD)

def normalize(mixed):
    scale = lax.rsqrt(lax.optimization_barrier(jnp.mean(mixed * mixed, axis=-1)) + 1e-06)
    return (mixed * scale[:, None]).astype(jnp.bfloat16)

def attend(qblk, kblk, value_block, qpos, kpos):
    heads = qblk.shape[1] // HD
    q3 = qblk.reshape(-1, heads, HD)
    k3 = kblk.reshape(-1, heads, HD)
    v3 = value_block.reshape(-1, heads, HD)
    scores = jnp.einsum('qhd,khd->hqk', q3.astype(jnp.float32), k3.astype(jnp.float32)) * (1.0 / math.sqrt(HD))
    valid = (kpos[None, :] >= 0) & (kpos[None, :] <= qpos[:, None])
    masked = jnp.where(valid[None], scores, -1e+30)
    top = lax.optimization_barrier(jnp.max(masked, axis=-1, keepdims=True))
    raw = jnp.exp(masked - top)
    total = lax.optimization_barrier(jnp.sum(raw, axis=-1))
    probs = raw.astype(jnp.bfloat16)
    out = jnp.einsum('hqk,khd->qhd', probs.astype(jnp.float32), v3.astype(jnp.float32))
    out = out / total.T[:, :, None]
    return out.reshape(qblk.shape[0], -1)

def reference(se_streams, se_short, se_filter, medium_projected_streams, mr_short, medium_filter_raw, mr_decay, queries, keys, values):
    step_index = jnp.arange(MEDIUM_TAPS, dtype=jnp.float32)
    mr_taps = medium_filter_raw * jnp.exp(-mr_decay[None, :] * step_index[:, None])
    se_out = normalize(hyena_full(se_streams, se_short, se_filter))
    mr_out = normalize(hyena_full(medium_projected_streams, mr_short, mr_taps))
    zeroed_rows = jnp.zeros((TOKENS_PER_SHARD, CHANNEL_SHARD), jnp.bfloat16)
    kpad = jnp.concatenate([zeroed_rows, keys], axis=0)
    value_padded = jnp.concatenate([zeroed_rows, values], axis=0)
    local = jnp.arange(TOKENS_PER_SHARD, dtype=jnp.int32)
    wide = jnp.arange(2 * TOKENS_PER_SHARD, dtype=jnp.int32)

    def block(index):
        start_offset = (index * TOKENS_PER_SHARD).astype(jnp.int32)
        qblk = lax.dynamic_slice_in_dim(queries, start_offset, TOKENS_PER_SHARD, 0)
        kblk = lax.dynamic_slice_in_dim(kpad, start_offset, 2 * TOKENS_PER_SHARD, 0)
        value_block = lax.dynamic_slice_in_dim(value_padded, start_offset, 2 * TOKENS_PER_SHARD, 0)
        return attend(qblk, kblk, value_block, start_offset + local, start_offset - TOKENS_PER_SHARD + wide)
    mixed = lax.map(block, jnp.arange(N_CTX, dtype=jnp.int32)).reshape(S, CHANNEL_SHARD)
    return (se_out, mr_out, normalize(mixed))
```

```python
import functools
import math

import jax
import jax.numpy as jnp
from jax import lax
from jax.experimental import pallas as pl
from jax.experimental.pallas import tpu as pltpu
from jax.sharding import PartitionSpec as P

CHANNELS = 4096
HD = 128
LSE = 7
MEDIUM_TAPS = 128
LANES = 128
F32 = jnp.float32
BF16 = jnp.bfloat16


def params():
    return pltpu.CompilerParams(
        dimension_semantics=("arbitrary",), vmem_limit_bytes=40 * 1024 * 1024
    )


def cost(flops, nbytes, trans=0):
    return pl.CostEstimate(flops=int(flops), bytes_accessed=int(nbytes), transcendentals=int(trans))


def roll(value, shift):
    shift = shift % value.shape[0]
    return pltpu.roll(value, shift, 0) if shift else value


def row_is(rows, at):
    return lax.broadcasted_iota(jnp.int32, (rows, LANES), 0) == at


def features(u, front, taps):
    ext = jnp.concatenate([front, u], axis=0)
    total = taps[0] * ext
    for j in range(1, len(taps)):
        total = total + taps[j] * roll(ext, j)
    return total[8:]


def tap_rows(ref, stream, lanes):
    return [ref[stream, j : j + 1, lanes] for j in range(ref.shape[1])]


def lane_block(k):
    return pl.ds(pl.multiple_of(k * LANES, LANES), LANES)


def write_taps(taps_ref, raw_ref, decay_ref, lanes):
    steps = lax.broadcasted_iota(jnp.int32, (MEDIUM_TAPS, LANES), 0).astype(F32)
    taps = raw_ref[:, lanes] * jnp.exp(-decay_ref[0:1, lanes] * steps)
    taps_ref[...] = taps
    return taps


def tap_tile(taps_ref, j):
    return jnp.broadcast_to(taps_ref[j : j + 1, :], (8, LANES))


def pack_kernel(per, m1_ref, m2_ref, m0t_ref, s0t_ref, s1t_ref, s2t_ref, mw_ref, sw_ref, out_ref, last_ref):
    step = pl.program_id(0)
    rows = m1_ref.shape[1]
    chunk = MEDIUM_TAPS + 16
    nothing = jnp.zeros((8, LANES), F32)

    @pl.when(step == 0)
    def _():
        last_ref[...] = jnp.zeros_like(last_ref)

    @pl.loop(0, per)
    def _(k):
        lanes = lane_block(k)
        block = step * per + k
        m1 = m1_ref[0, :, lanes].astype(F32)
        m2 = m2_ref[0, :, lanes].astype(F32)
        z1 = features(m1, nothing, tap_rows(mw_ref, 1, lanes))
        z2 = features(m2, nothing, tap_rows(mw_ref, 2, lanes))
        product = (z1 * z2)[rows - MEDIUM_TAPS :]
        tail_m0 = m0t_ref[0, :, lanes].astype(F32)[8:]
        tail_m1, tail_m2 = m1[rows - 8 :], m2[rows - 8 :]
        head = jnp.where(row_is(8, 0), roll(tail_m2, 2), product[:8])
        product = jnp.concatenate([head, product[8:]], axis=0)
        s0 = s0t_ref[0, :, lanes].astype(F32)[8:]
        s1 = s1t_ref[0, :, lanes].astype(F32)
        s2 = s2t_ref[0, :, lanes].astype(F32)
        y1 = features(s1, nothing, tap_rows(sw_ref, 1, lanes))[8:]
        y2 = features(s2, nothing, tap_rows(sw_ref, 2, lanes))[8:]
        at = lax.broadcasted_iota(jnp.int32, (8, LANES), 0)
        x1 = jnp.where(at < 2, roll(s0, 2), y1 * y2)
        x2 = jnp.where(
            at < 2,
            roll(s1[8:], 2),
            jnp.where(at < 4, roll(s2[8:], 4), jnp.where(at < 6, roll(tail_m0, 6), tail_m1)),
        )
        start = pl.multiple_of(block * chunk, 16)
        out_ref[pl.ds(start, MEDIUM_TAPS), :] = product.astype(BF16)
        out_ref[pl.ds(start + MEDIUM_TAPS, 16), :] = jnp.concatenate([x1, x2], axis=0).astype(BF16)
        last_ref[pl.ds(block, 1), :] = tail_m2[7:8]

    out_ref[out_ref.shape[0] - 16 :, :] = last_ref[...].astype(BF16)


def pack(se, mr, se_short, mr_short, per):
    _, rows, channels = se.shape
    blocks = channels // LANES
    total = blocks * (MEDIUM_TAPS + 16) + 16
    width = per * LANES
    whole = lambda s: pl.BlockSpec((1, rows, width), lambda i: (s, 0, i))
    tail = lambda s: pl.BlockSpec((1, 16, width), lambda i: (s, rows // 16 - 1, i))
    short = pl.BlockSpec((3, 3, width), lambda i: (0, 0, i))
    return pl.pallas_call(
        functools.partial(pack_kernel, per),
        grid=(blocks // per,),
        out_shape=jax.ShapeDtypeStruct((total, LANES), BF16),
        in_specs=[whole(1), whole(2), tail(0), tail(0), tail(1), tail(2), short, short],
        out_specs=pl.BlockSpec((total, LANES), lambda i: (0, 0)),
        scratch_shapes=[pltpu.VMEM((16, LANES), F32)],
        compiler_params=params(),
        cost_estimate=cost(20 * rows * channels, 6 * rows * channels),
        name="pack",
    )(mr, mr, mr, se, se, se, mr_short, se_short)


def own_kernel(per, m1_ref, m2_ref, mw_ref, raw_ref, decay_ref, out_ref, taps_ref):
    rows = m1_ref.shape[1]
    tiles = rows // 8
    nothing = jnp.zeros((8, LANES), F32)

    @pl.loop(0, per)
    def _(k):
        lanes = lane_block(k)
        write_taps(taps_ref, raw_ref, decay_ref, lanes)
        z1 = features(m1_ref[0, :, lanes].astype(F32), nothing, tap_rows(mw_ref, 1, lanes))
        z2 = features(m2_ref[0, :, lanes].astype(F32), nothing, tap_rows(mw_ref, 2, lanes))
        product = (z1 * z2).astype(BF16).astype(F32)
        at = lax.broadcasted_iota(jnp.int32, (8, LANES), 0)
        head = jnp.where(at < 2, 0.0, product[:8])
        ext = jnp.concatenate([nothing, head, product[8:]], axis=0)
        total = [None] * tiles
        for r in range(8):
            shifted = roll(ext, r)
            tap = [tap_tile(taps_ref, 8 * a + r) for a in range(MEDIUM_TAPS // 8)]
            for i in range(tiles):
                for a in range(min(i + 1, MEDIUM_TAPS // 8)):
                    at_tile = 8 * (i - a + 1)
                    term = tap[a] * shifted[at_tile : at_tile + 8]
                    total[i] = term if total[i] is None else total[i] + term
        out_ref[:, lanes] = jnp.concatenate(total, axis=0)


def own_convolution(mr, mr_short, raw, decay, per):
    _, rows, channels = mr.shape
    width = per * LANES
    whole = lambda s: pl.BlockSpec((1, rows, width), lambda i: (s, 0, i))
    flat = lambda n: pl.BlockSpec((n, width), lambda i: (0, i))
    return pl.pallas_call(
        functools.partial(own_kernel, per),
        grid=(channels // width,),
        out_shape=jax.ShapeDtypeStruct((rows, channels), F32),
        in_specs=[
            whole(1),
            whole(2),
            pl.BlockSpec((3, 3, width), lambda i: (0, 0, i)),
            flat(MEDIUM_TAPS),
            flat(1),
        ],
        out_specs=flat(rows),
        scratch_shapes=[pltpu.VMEM((MEDIUM_TAPS, LANES), F32)],
        compiler_params=params(),
        cost_estimate=cost(150 * rows * channels, 12 * rows * channels),
        name="own_convolution",
    )(mr, mr, mr_short, raw, decay)


def mix_kernel(
    per,
    packet_ref,
    own_ref,
    m_ref,
    s_ref,
    mw_ref,
    sw_ref,
    raw_ref,
    decay_ref,
    filter_ref,
    se_ref,
    mr_ref,
    square_ref,
    taps_ref,
    last_ref,
):
    step = pl.program_id(0)
    rows = m_ref.shape[1]
    tiles = rows // 8
    chunk = MEDIUM_TAPS + 16
    nothing = jnp.zeros((8, LANES), F32)
    last_ref[...] = packet_ref[packet_ref.shape[0] - 16 :, :].astype(F32)

    @pl.when(step == 0)
    def _():
        square_ref[...] = jnp.zeros_like(square_ref)

    @pl.loop(0, per)
    def _(k):
        lanes = lane_block(k)
        block = step * per + k
        start = pl.multiple_of(block * chunk, 16)
        before = packet_ref[pl.ds(start, MEDIUM_TAPS), :].astype(F32)
        x = packet_ref[pl.ds(start + MEDIUM_TAPS, 16), :].astype(F32)
        x1, x2 = x[:8], x[8:]
        last = last_ref[pl.ds(block, 1), :]

        s0 = features(s_ref[0, :, lanes].astype(F32), roll(x1, 6), tap_rows(sw_ref, 0, lanes))
        s1 = features(s_ref[1, :, lanes].astype(F32), roll(x2, 6), tap_rows(sw_ref, 1, lanes))
        s2 = features(s_ref[2, :, lanes].astype(F32), roll(x2, 4), tap_rows(sw_ref, 2, lanes))
        ext = jnp.concatenate([x1, (s1 * s2).astype(BF16).astype(F32)], axis=0)
        total = filter_ref[0:1, lanes] * ext
        for j in range(1, LSE):
            total = total + filter_ref[j : j + 1, lanes] * roll(ext, j)
        mixed = s0 * total[8:]
        se_ref[:, lanes] = mixed
        square_ref[0] += mixed * mixed

        taps = write_taps(taps_ref, raw_ref, decay_ref, lanes)
        z0 = features(m_ref[0, :, lanes].astype(F32), roll(x2, 2), tap_rows(mw_ref, 0, lanes))
        front2 = jnp.where(row_is(8, 7), last, roll(before[:8], 6))
        z1 = features(m_ref[1, :16, lanes].astype(F32), x2, tap_rows(mw_ref, 1, lanes))
        z2 = features(m_ref[2, :16, lanes].astype(F32), front2, tap_rows(mw_ref, 2, lanes))
        first = (z1[:8] * z2[:8]).astype(BF16).astype(F32)
        padded = jnp.concatenate([taps, jnp.zeros((rows - MEDIUM_TAPS, LANES), F32)], axis=0)
        base = own_ref[:, lanes] + padded * first[0:1] + roll(padded, 1) * first[1:2]
        total = [base[8 * i : 8 * i + 8] for i in range(tiles)]
        ext = jnp.concatenate([before, nothing], axis=0)
        count = MEDIUM_TAPS // 8
        for r in range(8):
            shifted = roll(ext, r)
            tap = [tap_tile(taps_ref, 8 * a + r) for a in range(count)]
            for i in range(count):
                for a in range(i if r else i + 1, count):
                    at_tile = 8 * (i - a + count)
                    total[i] = total[i] + tap[a] * shifted[at_tile : at_tile + 8]
        mixed = z0 * jnp.concatenate(total, axis=0)
        mr_ref[:, lanes] = mixed
        square_ref[1] += mixed * mixed


def mix(packet, own, mr, se, mr_short, se_short, raw, decay, se_filter, per):
    _, rows, channels = mr.shape
    width = per * LANES
    streams = pl.BlockSpec((3, rows, width), lambda i: (0, 0, i))
    short = pl.BlockSpec((3, 3, width), lambda i: (0, 0, i))
    flat = lambda n: pl.BlockSpec((n, width), lambda i: (0, i))
    mixed = jax.ShapeDtypeStruct((rows, channels), F32)
    return pl.pallas_call(
        functools.partial(mix_kernel, per),
        grid=(channels // width,),
        out_shape=(mixed, mixed, jax.ShapeDtypeStruct((2, rows, LANES), F32)),
        in_specs=[
            pl.BlockSpec(packet.shape, lambda i: (0, 0)),
            flat(rows),
            streams,
            streams,
            short,
            short,
            flat(MEDIUM_TAPS),
            flat(1),
            flat(LSE),
        ],
        out_specs=(flat(rows), flat(rows), pl.BlockSpec((2, rows, LANES), lambda i: (0, 0, 0))),
        scratch_shapes=[pltpu.VMEM((MEDIUM_TAPS, LANES), F32), pltpu.VMEM((16, LANES), F32)],
        compiler_params=params(),
        cost_estimate=cost(180 * rows * channels, 24 * rows * channels),
        name="mix",
    )(packet, own, mr, se, mr_short, se_short, raw, decay, se_filter)


def score_kernel(per, there_ref, q_ref, k_ref, before_ref, v_ref, probs_ref, out_ref):
    rows = q_ref.shape[0]
    at = lax.broadcasted_iota(jnp.int32, (rows, 2 * rows), 0)
    key = lax.broadcasted_iota(jnp.int32, (rows, 2 * rows), 1)
    valid = (key <= at + rows) & (key >= there_ref[0])
    factor = math.log2(math.e) / math.sqrt(HD)

    @pl.loop(0, per)
    def _(k):
        lanes = lane_block(k)
        both = jnp.concatenate([before_ref[:, lanes], k_ref[:, lanes]], axis=0)
        scores = lax.dot_general(
            q_ref[:, lanes], both, (((1,), (1,)), ((), ())), preferred_element_type=F32
        )
        scores = jnp.where(valid, scores, -1e30)
        top = jnp.max(scores, axis=-1, keepdims=True)
        raw = jnp.exp2((scores - top) * factor)
        probs = (raw * (1.0 / jnp.sum(raw, axis=-1, keepdims=True))).astype(BF16)
        probs_ref[k] = probs[:, :rows]
        own = jnp.concatenate([jnp.zeros((rows, LANES), BF16), v_ref[:, lanes]], axis=0)
        out_ref[:, lanes] = jnp.dot(probs, own, preferred_element_type=F32)


def score(there, queries, keys, before, values, per):
    rows, channels = queries.shape
    width = per * LANES
    flat = pl.BlockSpec((rows, width), lambda i: (0, i))
    return pl.pallas_call(
        functools.partial(score_kernel, per),
        grid=(channels // width,),
        out_shape=(
            jax.ShapeDtypeStruct((channels // HD, rows, rows), BF16),
            jax.ShapeDtypeStruct((rows, channels), F32),
        ),
        in_specs=[pl.BlockSpec(memory_space=pltpu.SMEM), flat, flat, flat, flat],
        out_specs=(pl.BlockSpec((per, rows, rows), lambda i: (i, 0, 0)), flat),
        compiler_params=params(),
        cost_estimate=cost(8 * rows * rows * channels, 14 * rows * channels, 4 * rows * rows * channels // HD),
        name="score",
    )(there, queries, keys, before, values)


def value_kernel(per, probs_ref, before_ref, own_ref, out_ref, square_ref):
    @pl.when(pl.program_id(0) == 0)
    def _():
        square_ref[...] = jnp.zeros_like(square_ref)

    for k in range(per):
        lanes = slice(k * LANES, (k + 1) * LANES)
        total = own_ref[:, lanes] + jnp.dot(
            probs_ref[k], before_ref[:, lanes], preferred_element_type=F32
        )
        out_ref[:, lanes] = total
        square_ref[...] += total * total


def value_mix(probs, before, own, per):
    rows, channels = own.shape
    width = per * LANES
    flat = pl.BlockSpec((rows, width), lambda i: (0, i))
    return pl.pallas_call(
        functools.partial(value_kernel, per),
        grid=(channels // width,),
        out_shape=(
            jax.ShapeDtypeStruct((rows, channels), F32),
            jax.ShapeDtypeStruct((rows, LANES), F32),
        ),
        in_specs=[pl.BlockSpec((per, rows, rows), lambda i: (i, 0, 0)), flat, flat],
        out_specs=(flat, pl.BlockSpec((rows, LANES), lambda i: (0, 0))),
        compiler_params=params(),
        cost_estimate=cost(2 * rows * rows * channels, 12 * rows * channels),
        name="value_mix",
    )(probs, before, own)


def normalize_kernel(count, *refs):
    square_refs, mixed_refs, out_refs = refs[:-2 * count], refs[-2 * count : -count], refs[-count:]
    for n in range(count):
        square = square_refs[0][n]
        for ref in square_refs[1:]:
            square = square + ref[n]
        scale = lax.rsqrt(jnp.sum(square, axis=-1, keepdims=True) * (1.0 / CHANNELS) + 1e-06)
        out_refs[n][...] = (mixed_refs[n][...] * scale).astype(BF16)


def normalize(squares, mixed, per):
    rows, channels = mixed[0].shape
    count = len(mixed)
    flat = pl.BlockSpec((rows, per * LANES), lambda i: (0, i))
    square = pl.BlockSpec((count, rows, LANES), lambda i: (0, 0, 0))
    return pl.pallas_call(
        functools.partial(normalize_kernel, count),
        grid=(channels // (per * LANES),),
        out_shape=(jax.ShapeDtypeStruct((rows, channels), BF16),) * count,
        in_specs=[square] * len(squares) + [flat] * count,
        out_specs=(flat,) * count,
        compiler_params=params(),
        cost_estimate=cost(4 * count * rows * channels, 6 * count * rows * channels),
        name="normalize",
    )(*squares, *mixed)


def from_behind(value):
    count = lax.axis_size("ctx")
    return lax.ppermute(value, "ctx", [(source, source + 1) for source in range(count - 1)])


def of_panels(square):
    count = lax.axis_size("panel")
    return [square] + [
        lax.ppermute(square, "panel", [(n, (n + shift) % count) for n in range(count)])
        for shift in range(1, count)
    ]


def body(se, se_short, se_filter, mr, mr_short, raw, decay, queries, keys, values):
    rows = queries.shape[0]
    decay = decay[None, :]
    packet = from_behind(pack(se, mr, se_short, mr_short, 4))
    key_before, value_before = from_behind(keys), from_behind(values)
    own = own_convolution(mr, mr_short, raw, decay, 4)
    se_mix, mr_mix, square = mix(packet, own, mr, se, mr_short, se_short, raw, decay, se_filter, 4)
    squares = of_panels(square)
    there = jnp.where(lax.axis_index("ctx") == 0, rows, 0).astype(jnp.int32)[None]
    probs, attended = score(there, queries, keys, key_before, values, 4)
    se_out, mr_out = normalize(squares, (se_mix, mr_mix), 4)
    attended, square = value_mix(probs, value_before, attended, 4)
    (attn_out,) = normalize(of_panels(square[None]), (attended,), 4)
    return se_out, mr_out, attn_out


def solution(mesh):
    placed = (
        P(None, "ctx", "panel"),
        P(None, None, "panel"),
        P(None, "panel"),
        P(None, "ctx", "panel"),
        P(None, None, "panel"),
        P(None, "panel"),
        P("panel"),
        P("ctx", "panel"),
        P("ctx", "panel"),
        P("ctx", "panel"),
    )
    return jax.shard_map(
        body,
        mesh=mesh,
        in_specs=placed,
        out_specs=(P("ctx", "panel"), P("ctx", "panel"), P("ctx", "panel")),
        check_vma=False,
    )
```

```python
import functools
import math

import jax
import jax.numpy as jnp
from jax import lax
from jax.experimental import pallas as pl
from jax.experimental.pallas import tpu as pltpu
from jax.sharding import PartitionSpec as P

CHANNELS = 4096
HD = 128
LSE = 7
MEDIUM_TAPS = 128
LANES = 128
F32 = jnp.float32
BF16 = jnp.bfloat16


def params(mebibytes=36):
    return pltpu.CompilerParams(vmem_limit_bytes=mebibytes * 1024 * 1024)


def in_vmem():
    return pl.BlockSpec(memory_space=pltpu.VMEM)


def cost(flops, nbytes, trans=0):
    return pl.CostEstimate(flops=int(flops), bytes_accessed=int(nbytes), transcendentals=int(trans))


def roll(value, shift):
    shift = shift % value.shape[0]
    return pltpu.roll(value, shift, 0) if shift else value


def row_is(rows, at):
    return lax.broadcasted_iota(jnp.int32, (rows, LANES), 0) == at


def features(u, front, taps):
    ext = jnp.concatenate([front, u], axis=0)
    total = taps[0] * ext
    for j in range(1, len(taps)):
        total = total + taps[j] * roll(ext, j)
    return total[8:]


def tap_rows(ref, stream, lanes):
    return [ref[stream, j : j + 1, lanes] for j in range(ref.shape[1])]


def lane_block(k):
    return pl.ds(pl.multiple_of(k * LANES, LANES), LANES)


def write_taps(taps_ref, raw_ref, decay_ref, lanes):
    steps = lax.broadcasted_iota(jnp.int32, (MEDIUM_TAPS, LANES), 0).astype(F32)
    taps = raw_ref[:, lanes] * jnp.exp(-decay_ref[0:1, lanes] * steps)
    taps_ref[...] = taps
    return taps


def tap_tile(taps_ref, j):
    return jnp.broadcast_to(taps_ref[j : j + 1, :], (8, LANES))


def pack_kernel(per, m1_ref, m2_ref, m0t_ref, s0t_ref, s1t_ref, s2t_ref, mw_ref, sw_ref, out_ref, last_ref):
    step = pl.program_id(0)
    rows = m1_ref.shape[1]
    chunk = MEDIUM_TAPS + 16
    nothing = jnp.zeros((8, LANES), F32)

    @pl.when(step == 0)
    def _():
        last_ref[...] = jnp.zeros_like(last_ref)

    @pl.loop(0, per)
    def _(k):
        lanes = lane_block(k)
        block = step * per + k
        m1 = m1_ref[0, :, lanes].astype(F32)
        m2 = m2_ref[0, :, lanes].astype(F32)
        z1 = features(m1, nothing, tap_rows(mw_ref, 1, lanes))
        z2 = features(m2, nothing, tap_rows(mw_ref, 2, lanes))
        product = (z1 * z2)[rows - MEDIUM_TAPS :]
        tail_m0 = m0t_ref[0, :, lanes].astype(F32)[8:]
        tail_m1, tail_m2 = m1[rows - 8 :], m2[rows - 8 :]
        head = jnp.where(row_is(8, 0), roll(tail_m2, 2), product[:8])
        product = jnp.concatenate([head, product[8:]], axis=0)
        s0 = s0t_ref[0, :, lanes].astype(F32)[8:]
        s1 = s1t_ref[0, :, lanes].astype(F32)
        s2 = s2t_ref[0, :, lanes].astype(F32)
        y1 = features(s1, nothing, tap_rows(sw_ref, 1, lanes))[8:]
        y2 = features(s2, nothing, tap_rows(sw_ref, 2, lanes))[8:]
        at = lax.broadcasted_iota(jnp.int32, (8, LANES), 0)
        x1 = jnp.where(at < 2, roll(s0, 2), y1 * y2)
        x2 = jnp.where(
            at < 2,
            roll(s1[8:], 2),
            jnp.where(at < 4, roll(s2[8:], 4), jnp.where(at < 6, roll(tail_m0, 6), tail_m1)),
        )
        start = pl.multiple_of(block * chunk, 16)
        out_ref[pl.ds(start, MEDIUM_TAPS), :] = product.astype(BF16)
        out_ref[pl.ds(start + MEDIUM_TAPS, 16), :] = jnp.concatenate([x1, x2], axis=0).astype(BF16)
        last_ref[pl.ds(block, 1), :] = tail_m2[7:8]

    out_ref[out_ref.shape[0] - 16 :, :] = last_ref[...].astype(BF16)


def pack(se, mr, se_short, mr_short, per):
    _, rows, channels = se.shape
    blocks = channels // LANES
    total = blocks * (MEDIUM_TAPS + 16) + 16
    width = per * LANES
    whole = lambda s: pl.BlockSpec((1, rows, width), lambda i: (s, 0, i))
    tail = lambda s: pl.BlockSpec((1, 16, width), lambda i: (s, rows // 16 - 1, i))
    short = pl.BlockSpec((3, 3, width), lambda i: (0, 0, i))
    return pl.pallas_call(
        functools.partial(pack_kernel, per),
        grid=(blocks // per,),
        out_shape=jax.ShapeDtypeStruct((total, LANES), BF16),
        in_specs=[whole(1), whole(2), tail(0), tail(0), tail(1), tail(2), short, short],
        out_specs=pl.BlockSpec((total, LANES), lambda i: (0, 0)),
        scratch_shapes=[pltpu.VMEM((16, LANES), F32)],
        compiler_params=params(60),
        cost_estimate=cost(20 * rows * channels, 6 * rows * channels),
        name="pack",
    )(mr, mr, mr, se, se, se, mr_short, se_short)


def own_kernel(m_ref, s_ref, mw_ref, sw_ref, raw_ref, decay_ref, filter_ref, own_ref, se_ref, square_ref, taps_ref):
    rows, channels = own_ref.shape
    tiles = rows // 8
    nothing = jnp.zeros((8, LANES), F32)
    square_ref[...] = jnp.zeros_like(square_ref)

    @pl.loop(0, channels // LANES)
    def _(k):
        lanes = lane_block(k)
        s = [features(s_ref[n, :, lanes].astype(F32), nothing, tap_rows(sw_ref, n, lanes)) for n in range(3)]
        ext = jnp.concatenate([nothing, (s[1] * s[2]).astype(BF16).astype(F32)], axis=0)
        total = filter_ref[0:1, lanes] * ext
        for j in range(1, LSE):
            total = total + filter_ref[j : j + 1, lanes] * roll(ext, j)
        mixed = s[0] * total[8:]
        se_ref[:, lanes] = mixed
        square_ref[8:, :] += mixed[8:] * mixed[8:]

        write_taps(taps_ref, raw_ref, decay_ref, lanes)
        z1 = features(m_ref[1, :, lanes].astype(F32), nothing, tap_rows(mw_ref, 1, lanes))
        z2 = features(m_ref[2, :, lanes].astype(F32), nothing, tap_rows(mw_ref, 2, lanes))
        product = (z1 * z2).astype(BF16).astype(F32)
        at = lax.broadcasted_iota(jnp.int32, (8, LANES), 0)
        head = jnp.where(at < 2, 0.0, product[:8])
        ext = jnp.concatenate([nothing, head, product[8:]], axis=0)
        total = [None] * tiles
        for r in range(8):
            shifted = roll(ext, r)
            tap = [tap_tile(taps_ref, 8 * a + r) for a in range(MEDIUM_TAPS // 8)]
            for i in range(tiles):
                for a in range(min(i + 1, MEDIUM_TAPS // 8)):
                    at_tile = 8 * (i - a + 1)
                    term = tap[a] * shifted[at_tile : at_tile + 8]
                    total[i] = term if total[i] is None else total[i] + term
        own_ref[:, lanes] = jnp.concatenate(total, axis=0)


def own_part(mr, se, mr_short, se_short, raw, decay, se_filter):
    _, rows, channels = mr.shape
    mixed = jax.ShapeDtypeStruct((rows, channels), F32)
    return pl.pallas_call(
        own_kernel,
        out_shape=(mixed, mixed, jax.ShapeDtypeStruct((rows, LANES), F32)),
        in_specs=[in_vmem()] * 7,
        out_specs=(in_vmem(),) * 3,
        scratch_shapes=[pltpu.VMEM((MEDIUM_TAPS, LANES), F32)],
        compiler_params=params(),
        cost_estimate=cost(180 * rows * channels, 24 * rows * channels),
        name="own_part",
    )(mr, se, mr_short, se_short, raw, decay, se_filter)


def mix_kernel(
    packet_ref,
    own_ref,
    se_square_ref,
    m_ref,
    s_ref,
    mw_ref,
    sw_ref,
    raw_ref,
    decay_ref,
    filter_ref,
    head_ref,
    mr_ref,
    square_ref,
    taps_ref,
    last_ref,
):
    rows, channels = own_ref.shape
    tiles = rows // 8
    chunk = MEDIUM_TAPS + 16
    nothing = jnp.zeros((8, LANES), F32)
    last_ref[...] = packet_ref[packet_ref.shape[0] - 16 :, :].astype(F32)
    square_ref[0] = se_square_ref[...]
    square_ref[1] = jnp.zeros((rows, LANES), F32)

    @pl.loop(0, channels // LANES)
    def _(k):
        lanes = lane_block(k)
        start = pl.multiple_of(k * chunk, 16)
        before = packet_ref[pl.ds(start, MEDIUM_TAPS), :].astype(F32)
        x = packet_ref[pl.ds(start + MEDIUM_TAPS, 16), :].astype(F32)
        x1, x2 = x[:8], x[8:]
        last = last_ref[pl.ds(k, 1), :]

        fronts = (roll(x1, 6), roll(x2, 6), roll(x2, 4))
        s = [
            features(s_ref[n, :16, lanes].astype(F32)[:8], fronts[n], tap_rows(sw_ref, n, lanes))
            for n in range(3)
        ]
        ext = jnp.concatenate([x1, (s[1] * s[2]).astype(BF16).astype(F32)], axis=0)
        total = filter_ref[0:1, lanes] * ext
        for j in range(1, LSE):
            total = total + filter_ref[j : j + 1, lanes] * roll(ext, j)
        mixed = s[0] * total[8:]
        head_ref[:, lanes] = mixed
        square_ref[0, :8, :] += mixed * mixed

        taps = write_taps(taps_ref, raw_ref, decay_ref, lanes)
        z0 = features(m_ref[0, :, lanes].astype(F32), roll(x2, 2), tap_rows(mw_ref, 0, lanes))
        front2 = jnp.where(row_is(8, 7), last, roll(before[:8], 6))
        z1 = features(m_ref[1, :16, lanes].astype(F32)[:8], x2, tap_rows(mw_ref, 1, lanes))
        z2 = features(m_ref[2, :16, lanes].astype(F32)[:8], front2, tap_rows(mw_ref, 2, lanes))
        first = (z1 * z2).astype(BF16).astype(F32)
        padded = jnp.concatenate([taps, jnp.zeros((rows - MEDIUM_TAPS, LANES), F32)], axis=0)
        base = own_ref[:, lanes] + padded * first[0:1] + roll(padded, 1) * first[1:2]
        total = [base[8 * i : 8 * i + 8] for i in range(tiles)]
        ext = jnp.concatenate([before, nothing], axis=0)
        count = MEDIUM_TAPS // 8
        for r in range(8):
            shifted = roll(ext, r)
            tap = [tap_tile(taps_ref, 8 * a + r) for a in range(count)]
            for i in range(count):
                for a in range(i if r else i + 1, count):
                    at_tile = 8 * (i - a + count)
                    total[i] = total[i] + tap[a] * shifted[at_tile : at_tile + 8]
        mixed = z0 * jnp.concatenate(total, axis=0)
        mr_ref[:, lanes] = mixed
        square_ref[1] += mixed * mixed


def mix(packet, own, se_square, mr, se, mr_short, se_short, raw, decay, se_filter):
    _, rows, channels = mr.shape
    return pl.pallas_call(
        mix_kernel,
        out_shape=(
            jax.ShapeDtypeStruct((8, channels), F32),
            jax.ShapeDtypeStruct((rows, channels), F32),
            jax.ShapeDtypeStruct((2, rows, LANES), F32),
        ),
        in_specs=[in_vmem()] * 10,
        out_specs=(in_vmem(),) * 3,
        scratch_shapes=[pltpu.VMEM((MEDIUM_TAPS, LANES), F32), pltpu.VMEM((16, LANES), F32)],
        compiler_params=params(),
        cost_estimate=cost(140 * rows * channels, 16 * rows * channels),
        name="mix",
    )(packet, own, se_square, mr, se, mr_short, se_short, raw, decay, se_filter)


def score_kernel(per, there_ref, q_ref, k_ref, before_ref, v_ref, probs_ref, out_ref, inverse_ref, bias_ref):
    rows, channels = q_ref.shape
    at = lax.broadcasted_iota(jnp.int32, (rows, 2 * rows), 0)
    key = lax.broadcasted_iota(jnp.int32, (rows, 2 * rows), 1)
    valid = (key <= at + rows) & (key >= there_ref[0])
    bias_ref[...] = jnp.where(valid, 0.0, -1e30)
    factor = math.log2(math.e) / math.sqrt(HD)
    zeros, ones = jnp.zeros((rows, LANES), BF16), jnp.ones((rows, LANES), BF16)

    @pl.loop(0, channels // (LANES * per))
    def _(group):
        for n in range(per):
            head = group * per + n
            lanes = lane_block(head)
            both = jnp.concatenate([before_ref[:, lanes], k_ref[:, lanes]], axis=0)
            scores = lax.dot_general(
                q_ref[:, lanes], both, (((1,), (1,)), ((), ())), preferred_element_type=F32
            )
            scores = scores + bias_ref[...]
            top = jnp.max(scores, axis=-1, keepdims=True)
            probs = jnp.exp2((scores - top) * factor).astype(BF16)
            probs_ref[head] = probs[:, :rows]
            own = jnp.concatenate(
                [
                    jnp.concatenate([zeros, v_ref[:, lanes]], axis=0),
                    jnp.concatenate([ones, ones], axis=0),
                ],
                axis=1,
            )
            total = jnp.dot(probs, own, preferred_element_type=F32)
            inverse = 1.0 / total[:, LANES:]
            inverse_ref[:, lanes] = inverse
            out_ref[:, lanes] = total[:, :LANES] * inverse


def score(there, queries, keys, before, values, per):
    rows, channels = queries.shape
    flat = jax.ShapeDtypeStruct((rows, channels), F32)
    return pl.pallas_call(
        functools.partial(score_kernel, per),
        out_shape=(jax.ShapeDtypeStruct((channels // HD, rows, rows), BF16), flat, flat),
        in_specs=[pl.BlockSpec(memory_space=pltpu.SMEM)] + [in_vmem()] * 4,
        out_specs=(in_vmem(),) * 3,
        scratch_shapes=[pltpu.VMEM((rows, 2 * rows), F32)],
        compiler_params=params(),
        cost_estimate=cost(
            8 * rows * rows * channels, 14 * rows * channels, 4 * rows * rows * channels // HD
        ),
        name="score",
    )(there, queries, keys, before, values)


def value_kernel(probs_ref, before_ref, own_ref, inverse_ref, out_ref, square_ref):
    rows, channels = own_ref.shape
    square = jnp.zeros((rows, LANES), F32)
    for k in range(channels // LANES):
        lanes = slice(k * LANES, (k + 1) * LANES)
        total = own_ref[:, lanes] + inverse_ref[:, lanes] * jnp.dot(
            probs_ref[k], before_ref[:, lanes], preferred_element_type=F32
        )
        out_ref[:, lanes] = total
        square = square + total * total
    square_ref[0] = square


def value_mix(probs, before, own, inverse):
    rows, channels = own.shape
    return pl.pallas_call(
        value_kernel,
        out_shape=(
            jax.ShapeDtypeStruct((rows, channels), F32),
            jax.ShapeDtypeStruct((1, rows, LANES), F32),
        ),
        in_specs=[in_vmem()] * 4,
        out_specs=(in_vmem(),) * 2,
        compiler_params=params(),
        cost_estimate=cost(2 * rows * rows * channels, 12 * rows * channels),
        name="value_mix",
    )(probs, before, own, inverse)


def normalize_kernel(count, panels, pieces, with_head, *refs):
    square_refs, refs = refs[:panels], refs[panels:]
    mixed_refs, refs = refs[:count], refs[count:]
    if with_head:
        head_ref, refs = refs[0], refs[1:]
    out_refs, (held_ref, sems) = refs[:count], refs[count:]
    rows = mixed_refs[0].shape[0]
    piece = rows // pieces
    copies = []
    for n in range(count):
        square = square_refs[0][n]
        for ref in square_refs[1:]:
            square = square + ref[n]
        scale = lax.rsqrt(jnp.sum(square, axis=-1, keepdims=True) * (1.0 / CHANNELS) + 1e-06)
        for m in range(pieces):
            at = slice(m * piece, (m + 1) * piece)
            value = mixed_refs[n][at, :]
            if with_head and n == 0 and m == 0:
                value = jnp.concatenate([head_ref[...], value[8:]], axis=0)
            held_ref[n, at, :] = (value * scale[at]).astype(BF16)
            copy = pltpu.make_async_copy(
                held_ref.at[n, pl.ds(m * piece, piece)],
                out_refs[n].at[pl.ds(m * piece, piece)],
                sems.at[n, m],
            )
            copy.start()
            copies.append(copy)
    for copy in copies:
        copy.wait()


def normalize(squares, mixed, head=None, pieces=3):
    rows, channels = mixed[0].shape
    count = len(mixed)
    operands = (*squares, *mixed) + (() if head is None else (head,))
    return pl.pallas_call(
        functools.partial(normalize_kernel, count, len(squares), pieces, head is not None),
        out_shape=(jax.ShapeDtypeStruct((rows, channels), BF16),) * count,
        in_specs=[in_vmem()] * len(operands),
        out_specs=(pl.BlockSpec(memory_space=pl.ANY),) * count,
        scratch_shapes=[
            pltpu.VMEM((count, rows, channels), BF16),
            pltpu.SemaphoreType.DMA((count, pieces)),
        ],
        compiler_params=params(),
        cost_estimate=cost(4 * count * rows * channels, 6 * count * rows * channels),
        name="normalize",
    )(*operands)


def from_behind(value):
    count = lax.axis_size("ctx")
    return lax.ppermute(value, "ctx", [(source, source + 1) for source in range(count - 1)])


def of_panels(square):
    count = lax.axis_size("panel")
    return [square] + [
        lax.ppermute(square, "panel", [(n, (n + shift) % count) for n in range(count)])
        for shift in range(1, count)
    ]


def body(se, se_short, se_filter, mr, mr_short, raw, decay, queries, keys, values):
    rows = queries.shape[0]
    decay = decay[None, :]
    key_before = from_behind(keys)
    packet = from_behind(pack(se, mr, se_short, mr_short, 4))
    value_before = from_behind(values)
    own, se_mix, se_square = own_part(mr, se, mr_short, se_short, raw, decay, se_filter)
    there = jnp.where(lax.axis_index("ctx") == 0, rows, 0).astype(jnp.int32)[None]
    probs, attended, inverse = score(there, queries, keys, key_before, values, 4)
    head, mr_mix, square = mix(
        packet, own, se_square, mr, se, mr_short, se_short, raw, decay, se_filter
    )
    se_out, mr_out = normalize(of_panels(square), (se_mix, mr_mix), head)
    value_before, se_out, mr_out = lax.optimization_barrier((value_before, se_out, mr_out))
    attended, square = value_mix(probs, value_before, attended, inverse)
    (attn_out,) = normalize(of_panels(square), (attended,))
    return se_out, mr_out, attn_out


def solution(mesh):
    placed = (
        P(None, "ctx", "panel"),
        P(None, None, "panel"),
        P(None, "panel"),
        P(None, "ctx", "panel"),
        P(None, None, "panel"),
        P(None, "panel"),
        P("panel"),
        P("ctx", "panel"),
        P("ctx", "panel"),
        P("ctx", "panel"),
    )
    return jax.shard_map(
        body,
        mesh=mesh,
        in_specs=placed,
        out_specs=(P("ctx", "panel"), P("ctx", "panel"), P("ctx", "panel")),
        check_vma=False,
    )
```

```python
import functools
import math

import jax
import jax.numpy as jnp
from jax import lax
from jax.experimental import pallas as pl
from jax.experimental.pallas import tpu as pltpu
from jax.sharding import PartitionSpec as P

CHANNELS = 4096
HD = 128
LSE = 7
MEDIUM_TAPS = 128
LANES = 128
F32 = jnp.float32
BF16 = jnp.bfloat16


def params(mebibytes=6):
    return pltpu.CompilerParams(vmem_limit_bytes=mebibytes * 1024 * 1024)


def in_vmem():
    return pl.BlockSpec(memory_space=pltpu.VMEM)


def cost(flops, nbytes, trans=0):
    return pl.CostEstimate(flops=int(flops), bytes_accessed=int(nbytes), transcendentals=int(trans))


def roll(value, shift):
    shift = shift % value.shape[0]
    return pltpu.roll(value, shift, 0) if shift else value


def row_is(rows, at):
    return lax.broadcasted_iota(jnp.int32, (rows, LANES), 0) == at


def features(u, front, taps):
    ext = jnp.concatenate([front, u], axis=0)
    total = taps[0] * ext
    for j in range(1, len(taps)):
        total = total + taps[j] * roll(ext, j)
    return total[8:]


def tap_rows(ref, stream, lanes):
    return [ref[stream, j : j + 1, lanes] for j in range(ref.shape[1])]


def lane_block(k):
    return pl.ds(pl.multiple_of(k * LANES, LANES), LANES)


def tap_tile(taps_ref, j, lanes):
    return jnp.broadcast_to(taps_ref[j : j + 1, lanes], (8, LANES))


def pack_kernel(
    per, mr_ref, se_ref, mr_short_ref, se_short_ref, out_ref, m_ref, tail_ref, mw_ref, sw_ref, last_ref, sems
):
    _, rows, channels = mr_ref.shape
    width = per * LANES
    chunk = MEDIUM_TAPS + 16
    nothing = jnp.zeros((8, LANES), F32)
    end = pl.ds(rows - 16, 16)
    copies = [
        pltpu.make_async_copy(mr_short_ref, mw_ref, sems.at[0]),
        pltpu.make_async_copy(se_short_ref, sw_ref, sems.at[1]),
        pltpu.make_async_copy(mr_ref.at[pl.ds(0, 1), end], tail_ref.at[pl.ds(0, 1)], sems.at[2]),
        pltpu.make_async_copy(se_ref.at[:, end], tail_ref.at[pl.ds(1, 3)], sems.at[3]),
    ]
    first = len(copies)
    for n in range(channels // width):
        at = pl.ds(n * width, width)
        copies.append(
            pltpu.make_async_copy(
                mr_ref.at[pl.ds(1, 2), :, at], m_ref.at[:, :, at], sems.at[first + n]
            )
        )
    for copy in copies:
        copy.start()
    for copy in copies[:first]:
        copy.wait()
    last_ref[...] = jnp.zeros_like(last_ref)

    def one(block):
        lanes = lane_block(block)
        m1 = m_ref[0, :, lanes].astype(F32)
        m2 = m_ref[1, :, lanes].astype(F32)
        z1 = features(m1, nothing, tap_rows(mw_ref, 1, lanes))
        z2 = features(m2, nothing, tap_rows(mw_ref, 2, lanes))
        product = (z1 * z2)[rows - MEDIUM_TAPS :]
        tail_m0 = tail_ref[0, :, lanes].astype(F32)[8:]
        tail_m1, tail_m2 = m1[rows - 8 :], m2[rows - 8 :]
        head = jnp.where(row_is(8, 0), roll(tail_m2, 2), product[:8])
        product = jnp.concatenate([head, product[8:]], axis=0)
        s0 = tail_ref[1, :, lanes].astype(F32)[8:]
        s1 = tail_ref[2, :, lanes].astype(F32)
        s2 = tail_ref[3, :, lanes].astype(F32)
        y1 = features(s1, nothing, tap_rows(sw_ref, 1, lanes))[8:]
        y2 = features(s2, nothing, tap_rows(sw_ref, 2, lanes))[8:]
        at = lax.broadcasted_iota(jnp.int32, (8, LANES), 0)
        x1 = jnp.where(at < 2, roll(s0, 2), y1 * y2)
        x2 = jnp.where(
            at < 2,
            roll(s1[8:], 2),
            jnp.where(at < 4, roll(s2[8:], 4), jnp.where(at < 6, roll(tail_m0, 6), tail_m1)),
        )
        start = pl.multiple_of(block * chunk, 16)
        out_ref[pl.ds(start, MEDIUM_TAPS), :] = product.astype(BF16)
        out_ref[pl.ds(start + MEDIUM_TAPS, 16), :] = jnp.concatenate([x1, x2], axis=0).astype(BF16)
        last_ref[pl.ds(block, 1), :] = tail_m2[7:8]

    for n in range(channels // width):
        copies[first + n].wait()
        pl.loop(n * per, (n + 1) * per)(one)

    out_ref[out_ref.shape[0] - 16 :, :] = last_ref[...].astype(BF16)


def pack(se, mr, se_short, mr_short, per):
    _, rows, channels = se.shape
    blocks = channels // LANES
    total = blocks * (MEDIUM_TAPS + 16) + 16
    return pl.pallas_call(
        functools.partial(pack_kernel, per),
        out_shape=jax.ShapeDtypeStruct((total, LANES), BF16),
        in_specs=[pl.BlockSpec(memory_space=pltpu.HBM)] * 4,
        out_specs=in_vmem(),
        scratch_shapes=[
            pltpu.VMEM((2, rows, channels), BF16),
            pltpu.VMEM((4, 16, channels), BF16),
            pltpu.VMEM(mr_short.shape, F32),
            pltpu.VMEM(se_short.shape, F32),
            pltpu.VMEM((16, LANES), F32),
            pltpu.SemaphoreType.DMA((4 + blocks // per,)),
        ],
        compiler_params=params(),
        cost_estimate=cost(20 * rows * channels, 6 * rows * channels),
        name="pack",
    )(*(pltpu.with_memory_space_constraint(x, pltpu.HBM) for x in (mr, se, mr_short, se_short)))


def own_kernel(
    per,
    m_ref,
    s_ref,
    mw_ref,
    sw_ref,
    raw_hbm_ref,
    decay_ref,
    filter_ref,
    own_ref,
    z0_ref,
    se_ref,
    square_ref,
    taps_ref,
    heads_ref,
    raw_ref,
    sems,
):
    rows, channels = own_ref.shape
    tiles = rows // 8
    width = per * LANES
    nothing = jnp.zeros((8, LANES), F32)

    def fetch(n):
        at = pl.ds(pl.multiple_of(n * width, width), width)
        return pltpu.make_async_copy(raw_hbm_ref.at[:, at], raw_ref.at[:, at], sems.at[n])

    for n in range(channels // width):
        fetch(n).start()
    square_ref[...] = jnp.zeros_like(square_ref)

    @pl.loop(0, channels // LANES)
    def _(k):
        @pl.when(k % per == 0)
        def _():
            fetch(k // per).wait()

        lanes = lane_block(k)
        u = [s_ref[n, :, lanes].astype(F32) for n in range(3)]
        for n in range(3):
            heads_ref[n, :, lanes] = u[n][:8]
        s = [features(u[n], nothing, tap_rows(sw_ref, n, lanes)) for n in range(3)]
        ext = jnp.concatenate([nothing, (s[1] * s[2]).astype(BF16).astype(F32)], axis=0)
        total = filter_ref[0:1, lanes] * ext
        for j in range(1, LSE):
            total = total + filter_ref[j : j + 1, lanes] * roll(ext, j)
        mixed = s[0] * total[8:]
        se_ref[:, lanes] = mixed
        square_ref[8:, :] += mixed[8:] * mixed[8:]

        steps = lax.broadcasted_iota(jnp.int32, (MEDIUM_TAPS, LANES), 0).astype(F32)
        taps_ref[:, lanes] = raw_ref[:, lanes] * jnp.exp(-decay_ref[0:1, lanes] * steps)
        u = [m_ref[n, :, lanes].astype(F32) for n in range(3)]
        for n in range(3):
            heads_ref[3 + n, :, lanes] = u[n][:8]
        z = [features(u[n], nothing, tap_rows(mw_ref, n, lanes)) for n in range(3)]
        z0_ref[:, lanes] = z[0]
        product = (z[1] * z[2]).astype(BF16).astype(F32)
        at = lax.broadcasted_iota(jnp.int32, (8, LANES), 0)
        head = jnp.where(at < 2, 0.0, product[:8])
        ext = jnp.concatenate([nothing, head, product[8:]], axis=0)
        total = [None] * tiles
        for r in range(8):
            shifted = roll(ext, r)
            tap = [tap_tile(taps_ref, 8 * a + r, lanes) for a in range(MEDIUM_TAPS // 8)]
            for i in range(tiles):
                for a in range(min(i + 1, MEDIUM_TAPS // 8)):
                    at_tile = 8 * (i - a + 1)
                    term = tap[a] * shifted[at_tile : at_tile + 8]
                    total[i] = term if total[i] is None else total[i] + term
        own_ref[:, lanes] = jnp.concatenate(total, axis=0)


def own_part(mr, se, mr_short, se_short, raw, decay, se_filter, per):
    _, rows, channels = mr.shape
    mixed = jax.ShapeDtypeStruct((rows, channels), F32)
    raw = pltpu.with_memory_space_constraint(raw, pltpu.HBM)
    return pl.pallas_call(
        functools.partial(own_kernel, per),
        out_shape=(
            mixed,
            mixed,
            mixed,
            jax.ShapeDtypeStruct((rows, LANES), F32),
            jax.ShapeDtypeStruct((MEDIUM_TAPS, channels), F32),
            jax.ShapeDtypeStruct((6, 8, channels), F32),
        ),
        in_specs=[in_vmem()] * 4 + [pl.BlockSpec(memory_space=pltpu.HBM)] + [in_vmem()] * 2,
        out_specs=(in_vmem(),) * 6,
        scratch_shapes=[
            pltpu.VMEM((MEDIUM_TAPS, channels), F32),
            pltpu.SemaphoreType.DMA((channels // (per * LANES),)),
        ],
        compiler_params=params(),
        cost_estimate=cost(180 * rows * channels, 24 * rows * channels),
        name="own_part",
    )(mr, se, mr_short, se_short, raw, decay, se_filter)


def mix_kernel(
    packet_ref,
    own_ref,
    z0_ref,
    se_square_ref,
    taps_ref,
    heads_ref,
    mw_ref,
    sw_ref,
    filter_ref,
    head_ref,
    mr_ref,
    square_ref,
    last_ref,
):
    rows, channels = own_ref.shape
    tiles = rows // 8
    chunk = MEDIUM_TAPS + 16
    nothing = jnp.zeros((8, LANES), F32)
    last_ref[...] = packet_ref[packet_ref.shape[0] - 16 :, :].astype(F32)
    square_ref[0] = se_square_ref[...]
    square_ref[1] = jnp.zeros((rows, LANES), F32)

    @pl.loop(0, channels // LANES)
    def _(k):
        lanes = lane_block(k)
        start = pl.multiple_of(k * chunk, 16)
        before = packet_ref[pl.ds(start, MEDIUM_TAPS), :].astype(F32)
        x = packet_ref[pl.ds(start + MEDIUM_TAPS, 16), :].astype(F32)
        x1, x2 = x[:8], x[8:]
        last = last_ref[pl.ds(k, 1), :]

        fronts = (roll(x1, 6), roll(x2, 6), roll(x2, 4))
        s = [
            features(heads_ref[n, :, lanes], fronts[n], tap_rows(sw_ref, n, lanes))
            for n in range(3)
        ]
        ext = jnp.concatenate([x1, (s[1] * s[2]).astype(BF16).astype(F32)], axis=0)
        total = filter_ref[0:1, lanes] * ext
        for j in range(1, LSE):
            total = total + filter_ref[j : j + 1, lanes] * roll(ext, j)
        mixed = s[0] * total[8:]
        head_ref[:, lanes] = mixed
        square_ref[0, :8, :] += mixed * mixed

        taps = taps_ref[:, lanes]
        front2 = jnp.where(row_is(8, 7), last, roll(before[:8], 6))
        fronts = (roll(x2, 2), x2, front2)
        z = [
            features(heads_ref[3 + n, :, lanes], fronts[n], tap_rows(mw_ref, n, lanes))
            for n in range(3)
        ]
        first = (z[1] * z[2]).astype(BF16).astype(F32)
        padded = jnp.concatenate([taps, jnp.zeros((rows - MEDIUM_TAPS, LANES), F32)], axis=0)
        base = own_ref[:, lanes] + padded * first[0:1] + roll(padded, 1) * first[1:2]
        total = [base[8 * i : 8 * i + 8] for i in range(tiles)]
        ext = jnp.concatenate([before, nothing], axis=0)
        count = MEDIUM_TAPS // 8
        for r in range(8):
            shifted = roll(ext, r)
            tap = [tap_tile(taps_ref, 8 * a + r, lanes) for a in range(count)]
            for i in range(count):
                for a in range(i if r else i + 1, count):
                    at_tile = 8 * (i - a + count)
                    total[i] = total[i] + tap[a] * shifted[at_tile : at_tile + 8]
        z0 = jnp.concatenate([z[0], z0_ref[8:, lanes]], axis=0)
        mixed = z0 * jnp.concatenate(total, axis=0)
        mr_ref[:, lanes] = mixed
        square_ref[1] += mixed * mixed


def mix(packet, own, z0, se_square, taps, heads, mr_short, se_short, se_filter):
    rows, channels = own.shape
    return pl.pallas_call(
        mix_kernel,
        out_shape=(
            jax.ShapeDtypeStruct((8, channels), F32),
            jax.ShapeDtypeStruct((rows, channels), F32),
            jax.ShapeDtypeStruct((2, rows, LANES), F32),
        ),
        in_specs=[in_vmem()] * 9,
        out_specs=(in_vmem(),) * 3,
        scratch_shapes=[pltpu.VMEM((16, LANES), F32)],
        compiler_params=params(),
        cost_estimate=cost(140 * rows * channels, 16 * rows * channels),
        name="mix",
    )(packet, own, z0, se_square, taps, heads, mr_short, se_short, se_filter)


def score_kernel(per, there_ref, q_ref, k_ref, before_ref, v_ref, probs_ref, out_ref, inverse_ref, bias_ref):
    rows, channels = q_ref.shape
    at = lax.broadcasted_iota(jnp.int32, (rows, 2 * rows), 0)
    key = lax.broadcasted_iota(jnp.int32, (rows, 2 * rows), 1)
    valid = (key <= at + rows) & (key >= there_ref[0])
    bias_ref[...] = jnp.where(valid, 0.0, -1e30)
    factor = math.log2(math.e) / math.sqrt(HD)
    zeros, ones = jnp.zeros((rows, LANES), BF16), jnp.ones((rows, LANES), BF16)

    @pl.loop(0, channels // (LANES * per))
    def _(group):
        for n in range(per):
            head = group * per + n
            lanes = lane_block(head)
            both = jnp.concatenate([before_ref[:, lanes], k_ref[:, lanes]], axis=0)
            scores = lax.dot_general(
                q_ref[:, lanes], both, (((1,), (1,)), ((), ())), preferred_element_type=F32
            )
            scores = scores + bias_ref[...]
            top = jnp.max(scores, axis=-1, keepdims=True)
            probs = jnp.exp2((scores - top) * factor).astype(BF16)
            probs_ref[head] = probs[:, :rows]
            own = jnp.concatenate(
                [
                    jnp.concatenate([zeros, v_ref[:, lanes]], axis=0),
                    jnp.concatenate([ones, ones], axis=0),
                ],
                axis=1,
            )
            total = jnp.dot(probs, own, preferred_element_type=F32)
            inverse = 1.0 / total[:, LANES:]
            inverse_ref[:, lanes] = inverse
            out_ref[:, lanes] = total[:, :LANES] * inverse


def score(there, queries, keys, before, values, per):
    rows, channels = queries.shape
    flat = jax.ShapeDtypeStruct((rows, channels), F32)
    return pl.pallas_call(
        functools.partial(score_kernel, per),
        out_shape=(jax.ShapeDtypeStruct((channels // HD, rows, rows), BF16), flat, flat),
        in_specs=[pl.BlockSpec(memory_space=pltpu.SMEM)] + [in_vmem()] * 4,
        out_specs=(in_vmem(),) * 3,
        scratch_shapes=[pltpu.VMEM((rows, 2 * rows), F32)],
        compiler_params=params(),
        cost_estimate=cost(
            8 * rows * rows * channels, 14 * rows * channels, 4 * rows * rows * channels // HD
        ),
        name="score",
    )(there, queries, keys, before, values)


def value_kernel(probs_ref, before_ref, own_ref, inverse_ref, out_ref, square_ref):
    rows, channels = own_ref.shape
    square = jnp.zeros((rows, LANES), F32)
    for k in range(channels // LANES):
        lanes = slice(k * LANES, (k + 1) * LANES)
        total = own_ref[:, lanes] + inverse_ref[:, lanes] * jnp.dot(
            probs_ref[k], before_ref[:, lanes], preferred_element_type=F32
        )
        out_ref[:, lanes] = total
        square = square + total * total
    square_ref[0] = square


def value_mix(probs, before, own, inverse):
    rows, channels = own.shape
    return pl.pallas_call(
        value_kernel,
        out_shape=(
            jax.ShapeDtypeStruct((rows, channels), F32),
            jax.ShapeDtypeStruct((1, rows, LANES), F32),
        ),
        in_specs=[in_vmem()] * 4,
        out_specs=(in_vmem(),) * 2,
        compiler_params=params(),
        cost_estimate=cost(2 * rows * rows * channels, 12 * rows * channels),
        name="value_mix",
    )(probs, before, own, inverse)


def normalize_kernel(count, panels, pieces, with_head, *refs):
    square_refs, refs = refs[:panels], refs[panels:]
    mixed_refs, refs = refs[:count], refs[count:]
    if with_head:
        head_ref, refs = refs[0], refs[1:]
    out_refs, (held_ref, sems) = refs[:count], refs[count:]
    rows = mixed_refs[0].shape[0]
    piece = rows // pieces
    copies = []
    for n in range(count):
        square = square_refs[0][n]
        for ref in square_refs[1:]:
            square = square + ref[n]
        scale = lax.rsqrt(jnp.sum(square, axis=-1, keepdims=True) * (1.0 / CHANNELS) + 1e-06)
        for m in range(pieces):
            at = slice(m * piece, (m + 1) * piece)
            value = mixed_refs[n][at, :]
            if with_head and n == 0 and m == 0:
                value = jnp.concatenate([head_ref[...], value[8:]], axis=0)
            held_ref[n, at, :] = (value * scale[at]).astype(BF16)
            copy = pltpu.make_async_copy(
                held_ref.at[n, pl.ds(m * piece, piece)],
                out_refs[n].at[pl.ds(m * piece, piece)],
                sems.at[n, m],
            )
            copy.start()
            copies.append(copy)
    for copy in copies:
        copy.wait()


def normalize(squares, mixed, head=None, pieces=3):
    rows, channels = mixed[0].shape
    count = len(mixed)
    operands = (*squares, *mixed) + (() if head is None else (head,))
    return pl.pallas_call(
        functools.partial(normalize_kernel, count, len(squares), pieces, head is not None),
        out_shape=(jax.ShapeDtypeStruct((rows, channels), BF16),) * count,
        in_specs=[in_vmem()] * len(operands),
        out_specs=(pl.BlockSpec(memory_space=pl.ANY),) * count,
        scratch_shapes=[
            pltpu.VMEM((count, rows, channels), BF16),
            pltpu.SemaphoreType.DMA((count, pieces)),
        ],
        compiler_params=params(),
        cost_estimate=cost(4 * count * rows * channels, 6 * count * rows * channels),
        name="normalize",
    )(*operands)


def from_behind(value):
    count = lax.axis_size("ctx")
    return lax.ppermute(value, "ctx", [(source, source + 1) for source in range(count - 1)])


def of_panels(square):
    count = lax.axis_size("panel")
    return [square] + [
        lax.ppermute(square, "panel", [(n, (n + shift) % count) for n in range(count)])
        for shift in range(1, count)
    ]


def body(se, se_short, se_filter, mr, mr_short, raw, decay, queries, keys, values):
    rows = queries.shape[0]
    decay = decay[None, :]
    key_before = from_behind(keys)
    packet = from_behind(pack(se, mr, se_short, mr_short, 4))
    own, z0, se_mix, se_square, taps, heads = own_part(
        mr, se, mr_short, se_short, raw, decay, se_filter, 4
    )
    values_later, own = lax.optimization_barrier((values, own))
    value_before = from_behind(values_later)
    there = jnp.where(lax.axis_index("ctx") == 0, rows, 0).astype(jnp.int32)[None]
    probs, attended, inverse = score(there, queries, keys, key_before, values, 4)
    packet, attended = lax.optimization_barrier((packet, attended))
    head, mr_mix, square = mix(
        packet, own, z0, se_square, taps, heads, mr_short, se_short, se_filter
    )
    se_out, mr_out = normalize(of_panels(square), (se_mix, mr_mix), head)
    value_before, se_out, mr_out = lax.optimization_barrier((value_before, se_out, mr_out))
    attended, square = value_mix(probs, value_before, attended, inverse)
    (attn_out,) = normalize(of_panels(square), (attended,))
    return se_out, mr_out, attn_out


def solution(mesh):
    placed = (
        P(None, "ctx", "panel"),
        P(None, None, "panel"),
        P(None, "panel"),
        P(None, "ctx", "panel"),
        P(None, None, "panel"),
        P(None, "panel"),
        P("panel"),
        P("ctx", "panel"),
        P("ctx", "panel"),
        P("ctx", "panel"),
    )
    return jax.shard_map(
        body,
        mesh=mesh,
        in_specs=placed,
        out_specs=(P("ctx", "panel"), P("ctx", "panel"), P("ctx", "panel")),
        check_vma=False,
    )
```

```python
import functools
import math

import jax
import jax.numpy as jnp
from jax import lax
from jax.experimental import pallas as pl
from jax.experimental.pallas import tpu as pltpu
from jax.sharding import PartitionSpec as P

CHANNELS = 4096
HD = 128
LSE = 7
MEDIUM_TAPS = 128
LANES = 128
F32 = jnp.float32
BF16 = jnp.bfloat16


def params(mebibytes=6):
    return pltpu.CompilerParams(vmem_limit_bytes=mebibytes * 1024 * 1024)


def in_vmem():
    return pl.BlockSpec(memory_space=pltpu.VMEM)


def cost(flops, nbytes, trans=0):
    return pl.CostEstimate(flops=int(flops), bytes_accessed=int(nbytes), transcendentals=int(trans))


def roll(value, shift):
    shift = shift % value.shape[0]
    return pltpu.roll(value, shift, 0) if shift else value


def row_is(rows, at):
    return lax.broadcasted_iota(jnp.int32, (rows, LANES), 0) == at


def features(u, front, taps):
    ext = jnp.concatenate([front, u], axis=0)
    total = taps[0] * ext
    for j in range(1, len(taps)):
        total = total + taps[j] * roll(ext, j)
    return total[8:]


def tap_rows(ref, stream, lanes):
    return [ref[stream, j : j + 1, lanes] for j in range(ref.shape[1])]


def lane_block(k):
    return pl.ds(pl.multiple_of(k * LANES, LANES), LANES)


def tap_tile(held_ref, j):
    return jnp.broadcast_to(held_ref[j : j + 1, :], (8, LANES))


def pack_kernel(
    per, mr_ref, se_ref, mr_short_ref, se_short_ref, out_ref, m_ref, tail_ref, mw_ref, sw_ref, last_ref, sems
):
    _, rows, channels = mr_ref.shape
    width = per * LANES
    chunk = MEDIUM_TAPS + 16
    nothing = jnp.zeros((8, LANES), F32)
    end = pl.ds(rows - 16, 16)
    copies = [
        pltpu.make_async_copy(mr_short_ref, mw_ref, sems.at[0]),
        pltpu.make_async_copy(se_short_ref, sw_ref, sems.at[1]),
        pltpu.make_async_copy(mr_ref.at[pl.ds(0, 1), end], tail_ref.at[pl.ds(0, 1)], sems.at[2]),
        pltpu.make_async_copy(se_ref.at[:, end], tail_ref.at[pl.ds(1, 3)], sems.at[3]),
    ]
    first = len(copies)
    for n in range(channels // width):
        at = pl.ds(n * width, width)
        copies.append(
            pltpu.make_async_copy(
                mr_ref.at[pl.ds(1, 2), :, at], m_ref.at[:, :, at], sems.at[first + n]
            )
        )
    for copy in copies:
        copy.start()
    for copy in copies[:first]:
        copy.wait()
    last_ref[...] = jnp.zeros_like(last_ref)

    def one(block):
        lanes = lane_block(block)
        m1 = m_ref[0, :, lanes].astype(F32)
        m2 = m_ref[1, :, lanes].astype(F32)
        z1 = features(m1, nothing, tap_rows(mw_ref, 1, lanes))
        z2 = features(m2, nothing, tap_rows(mw_ref, 2, lanes))
        product = (z1 * z2)[rows - MEDIUM_TAPS :]
        tail_m0 = tail_ref[0, :, lanes].astype(F32)[8:]
        tail_m1, tail_m2 = m1[rows - 8 :], m2[rows - 8 :]
        head = jnp.where(row_is(8, 0), roll(tail_m2, 2), product[:8])
        product = jnp.concatenate([head, product[8:]], axis=0)
        s0 = tail_ref[1, :, lanes].astype(F32)[8:]
        s1 = tail_ref[2, :, lanes].astype(F32)
        s2 = tail_ref[3, :, lanes].astype(F32)
        y1 = features(s1, nothing, tap_rows(sw_ref, 1, lanes))[8:]
        y2 = features(s2, nothing, tap_rows(sw_ref, 2, lanes))[8:]
        at = lax.broadcasted_iota(jnp.int32, (8, LANES), 0)
        x1 = jnp.where(at < 2, roll(s0, 2), y1 * y2)
        x2 = jnp.where(
            at < 2,
            roll(s1[8:], 2),
            jnp.where(at < 4, roll(s2[8:], 4), jnp.where(at < 6, roll(tail_m0, 6), tail_m1)),
        )
        start = pl.multiple_of(block * chunk, 16)
        out_ref[pl.ds(start, MEDIUM_TAPS), :] = product.astype(BF16)
        out_ref[pl.ds(start + MEDIUM_TAPS, 16), :] = jnp.concatenate([x1, x2], axis=0).astype(BF16)
        last_ref[pl.ds(block, 1), :] = tail_m2[7:8]

    for n in range(channels // width):
        copies[first + n].wait()
        pl.loop(n * per, (n + 1) * per)(one)

    out_ref[out_ref.shape[0] - 16 :, :] = last_ref[...].astype(BF16)


def pack(se, mr, se_short, mr_short, per):
    _, rows, channels = se.shape
    blocks = channels // LANES
    total = blocks * (MEDIUM_TAPS + 16) + 16
    return pl.pallas_call(
        functools.partial(pack_kernel, per),
        out_shape=jax.ShapeDtypeStruct((total, LANES), BF16),
        in_specs=[pl.BlockSpec(memory_space=pltpu.HBM)] * 4,
        out_specs=in_vmem(),
        scratch_shapes=[
            pltpu.VMEM((2, rows, channels), BF16),
            pltpu.VMEM((4, 16, channels), BF16),
            pltpu.VMEM(mr_short.shape, F32),
            pltpu.VMEM(se_short.shape, F32),
            pltpu.VMEM((16, LANES), F32),
            pltpu.SemaphoreType.DMA((4 + blocks // per,)),
        ],
        compiler_params=params(),
        cost_estimate=cost(20 * rows * channels, 6 * rows * channels),
        name="pack",
    )(*(pltpu.with_memory_space_constraint(x, pltpu.HBM) for x in (mr, se, mr_short, se_short)))


def own_kernel(
    per,
    m_ref,
    s_ref,
    mw_ref,
    sw_ref,
    raw_hbm_ref,
    decay_ref,
    filter_ref,
    own_ref,
    z0_ref,
    se_ref,
    square_ref,
    taps_ref,
    heads_ref,
    raw_ref,
    held_ref,
    sems,
):
    rows, channels = own_ref.shape
    tiles = rows // 8
    width = per * LANES
    nothing = jnp.zeros((8, LANES), F32)

    def fetch(n):
        at = pl.ds(pl.multiple_of(n * width, width), width)
        return pltpu.make_async_copy(raw_hbm_ref.at[:, at], raw_ref.at[:, at], sems.at[n])

    for n in range(channels // width):
        fetch(n).start()
    square_ref[...] = jnp.zeros_like(square_ref)

    @pl.loop(0, channels // LANES)
    def _(k):
        @pl.when(k % per == 0)
        def _():
            fetch(k // per).wait()

        lanes = lane_block(k)
        u = [s_ref[n, :, lanes].astype(F32) for n in range(3)]
        for n in range(3):
            heads_ref[n, :, lanes] = u[n][:8]
        s = [features(u[n], nothing, tap_rows(sw_ref, n, lanes)) for n in range(3)]
        ext = jnp.concatenate([nothing, (s[1] * s[2]).astype(BF16).astype(F32)], axis=0)
        total = filter_ref[0:1, lanes] * ext
        for j in range(1, LSE):
            total = total + filter_ref[j : j + 1, lanes] * roll(ext, j)
        mixed = s[0] * total[8:]
        se_ref[:, lanes] = mixed
        square_ref[8:, :] += mixed[8:] * mixed[8:]

        steps = lax.broadcasted_iota(jnp.int32, (MEDIUM_TAPS, LANES), 0).astype(F32)
        taps = raw_ref[:, lanes] * jnp.exp(-decay_ref[0:1, lanes] * steps)
        held_ref[...] = taps
        taps_ref[:, lanes] = taps
        u = [m_ref[n, :, lanes].astype(F32) for n in range(3)]
        for n in range(3):
            heads_ref[3 + n, :, lanes] = u[n][:8]
        z = [features(u[n], nothing, tap_rows(mw_ref, n, lanes)) for n in range(3)]
        z0_ref[:, lanes] = z[0]
        product = (z[1] * z[2]).astype(BF16).astype(F32)
        at = lax.broadcasted_iota(jnp.int32, (8, LANES), 0)
        head = jnp.where(at < 2, 0.0, product[:8])
        ext = jnp.concatenate([nothing, head, product[8:]], axis=0)
        total = [None] * tiles
        for r in range(8):
            shifted = roll(ext, r)
            tap = [tap_tile(held_ref, 8 * a + r) for a in range(MEDIUM_TAPS // 8)]
            for i in range(tiles):
                for a in range(min(i + 1, MEDIUM_TAPS // 8)):
                    at_tile = 8 * (i - a + 1)
                    term = tap[a] * shifted[at_tile : at_tile + 8]
                    total[i] = term if total[i] is None else total[i] + term
        own_ref[:, lanes] = jnp.concatenate(total, axis=0)


def own_part(mr, se, mr_short, se_short, raw, decay, se_filter, per):
    _, rows, channels = mr.shape
    mixed = jax.ShapeDtypeStruct((rows, channels), F32)
    raw = pltpu.with_memory_space_constraint(raw, pltpu.HBM)
    return pl.pallas_call(
        functools.partial(own_kernel, per),
        out_shape=(
            mixed,
            mixed,
            mixed,
            jax.ShapeDtypeStruct((rows, LANES), F32),
            jax.ShapeDtypeStruct((MEDIUM_TAPS, channels), F32),
            jax.ShapeDtypeStruct((6, 8, channels), F32),
        ),
        in_specs=[in_vmem()] * 4 + [pl.BlockSpec(memory_space=pltpu.HBM)] + [in_vmem()] * 2,
        out_specs=(in_vmem(),) * 6,
        scratch_shapes=[
            pltpu.VMEM((MEDIUM_TAPS, channels), F32),
            pltpu.VMEM((MEDIUM_TAPS, LANES), F32),
            pltpu.SemaphoreType.DMA((channels // (per * LANES),)),
        ],
        compiler_params=params(),
        cost_estimate=cost(180 * rows * channels, 24 * rows * channels),
        name="own_part",
    )(mr, se, mr_short, se_short, raw, decay, se_filter)


def mix_kernel(
    packet_ref,
    own_ref,
    z0_ref,
    se_square_ref,
    taps_ref,
    heads_ref,
    mw_ref,
    sw_ref,
    filter_ref,
    head_ref,
    mr_ref,
    square_ref,
    last_ref,
    held_ref,
):
    rows, channels = own_ref.shape
    tiles = rows // 8
    chunk = MEDIUM_TAPS + 16
    nothing = jnp.zeros((8, LANES), F32)
    last_ref[...] = packet_ref[packet_ref.shape[0] - 16 :, :].astype(F32)
    square_ref[0] = se_square_ref[...]
    square_ref[1] = jnp.zeros((rows, LANES), F32)

    @pl.loop(0, channels // LANES)
    def _(k):
        lanes = lane_block(k)
        start = pl.multiple_of(k * chunk, 16)
        before = packet_ref[pl.ds(start, MEDIUM_TAPS), :].astype(F32)
        x = packet_ref[pl.ds(start + MEDIUM_TAPS, 16), :].astype(F32)
        x1, x2 = x[:8], x[8:]
        last = last_ref[pl.ds(k, 1), :]

        fronts = (roll(x1, 6), roll(x2, 6), roll(x2, 4))
        s = [
            features(heads_ref[n, :, lanes], fronts[n], tap_rows(sw_ref, n, lanes))
            for n in range(3)
        ]
        ext = jnp.concatenate([x1, (s[1] * s[2]).astype(BF16).astype(F32)], axis=0)
        total = filter_ref[0:1, lanes] * ext
        for j in range(1, LSE):
            total = total + filter_ref[j : j + 1, lanes] * roll(ext, j)
        mixed = s[0] * total[8:]
        head_ref[:, lanes] = mixed
        square_ref[0, :8, :] += mixed * mixed

        taps = taps_ref[:, lanes]
        held_ref[...] = taps
        front2 = jnp.where(row_is(8, 7), last, roll(before[:8], 6))
        fronts = (roll(x2, 2), x2, front2)
        z = [
            features(heads_ref[3 + n, :, lanes], fronts[n], tap_rows(mw_ref, n, lanes))
            for n in range(3)
        ]
        first = (z[1] * z[2]).astype(BF16).astype(F32)
        padded = jnp.concatenate([taps, jnp.zeros((rows - MEDIUM_TAPS, LANES), F32)], axis=0)
        base = own_ref[:, lanes] + padded * first[0:1] + roll(padded, 1) * first[1:2]
        total = [base[8 * i : 8 * i + 8] for i in range(tiles)]
        ext = jnp.concatenate([before, nothing], axis=0)
        count = MEDIUM_TAPS // 8
        for r in range(8):
            shifted = roll(ext, r)
            tap = [tap_tile(held_ref, 8 * a + r) for a in range(count)]
            for i in range(count):
                for a in range(i if r else i + 1, count):
                    at_tile = 8 * (i - a + count)
                    total[i] = total[i] + tap[a] * shifted[at_tile : at_tile + 8]
        z0 = jnp.concatenate([z[0], z0_ref[8:, lanes]], axis=0)
        mixed = z0 * jnp.concatenate(total, axis=0)
        mr_ref[:, lanes] = mixed
        square_ref[1] += mixed * mixed


def mix(packet, own, z0, se_square, taps, heads, mr_short, se_short, se_filter):
    rows, channels = own.shape
    return pl.pallas_call(
        mix_kernel,
        out_shape=(
            jax.ShapeDtypeStruct((8, channels), F32),
            jax.ShapeDtypeStruct((rows, channels), F32),
            jax.ShapeDtypeStruct((2, rows, LANES), F32),
        ),
        in_specs=[in_vmem()] * 9,
        out_specs=(in_vmem(),) * 3,
        scratch_shapes=[pltpu.VMEM((16, LANES), F32), pltpu.VMEM((MEDIUM_TAPS, LANES), F32)],
        compiler_params=params(),
        cost_estimate=cost(140 * rows * channels, 16 * rows * channels),
        name="mix",
    )(packet, own, z0, se_square, taps, heads, mr_short, se_short, se_filter)


def score_kernel(per, q_ref, k_ref, before_ref, v_ref, probs_ref, out_ref, inverse_ref, bias_ref):
    rows, channels = q_ref.shape
    at = lax.broadcasted_iota(jnp.int32, (rows, 2 * rows), 0)
    key = lax.broadcasted_iota(jnp.int32, (rows, 2 * rows), 1)
    valid = (key <= at + rows) & ((key >= rows) | (lax.axis_index("ctx") > 0))
    bias_ref[...] = jnp.where(valid, 0.0, -1e30)
    factor = math.log2(math.e) / math.sqrt(HD)
    zeros, ones = jnp.zeros((rows, LANES), BF16), jnp.ones((rows, LANES), BF16)

    @pl.loop(0, channels // (LANES * per))
    def _(group):
        for n in range(per):
            head = group * per + n
            lanes = lane_block(head)
            both = jnp.concatenate([before_ref[:, lanes], k_ref[:, lanes]], axis=0)
            scores = lax.dot_general(
                q_ref[:, lanes], both, (((1,), (1,)), ((), ())), preferred_element_type=F32
            )
            scores = scores + bias_ref[...]
            top = jnp.max(scores, axis=-1, keepdims=True)
            probs = jnp.exp2((scores - top) * factor).astype(BF16)
            probs_ref[head] = probs[:, :rows]
            own = jnp.concatenate(
                [
                    jnp.concatenate([zeros, v_ref[:, lanes]], axis=0),
                    jnp.concatenate([ones, ones], axis=0),
                ],
                axis=1,
            )
            total = jnp.dot(probs, own, preferred_element_type=F32)
            inverse = 1.0 / total[:, LANES:]
            inverse_ref[:, lanes] = inverse
            out_ref[:, lanes] = total[:, :LANES] * inverse


def score(queries, keys, before, values, per):
    rows, channels = queries.shape
    flat = jax.ShapeDtypeStruct((rows, channels), F32)
    return pl.pallas_call(
        functools.partial(score_kernel, per),
        out_shape=(jax.ShapeDtypeStruct((channels // HD, rows, rows), BF16), flat, flat),
        in_specs=[in_vmem()] * 4,
        out_specs=(in_vmem(),) * 3,
        scratch_shapes=[pltpu.VMEM((rows, 2 * rows), F32)],
        compiler_params=params(),
        cost_estimate=cost(
            8 * rows * rows * channels, 14 * rows * channels, 4 * rows * rows * channels // HD
        ),
        name="score",
    )(queries, keys, before, values)


def value_kernel(probs_ref, before_ref, own_ref, inverse_ref, out_ref, square_ref):
    rows, channels = own_ref.shape
    square = jnp.zeros((rows, LANES), F32)
    for k in range(channels // LANES):
        lanes = slice(k * LANES, (k + 1) * LANES)
        total = own_ref[:, lanes] + inverse_ref[:, lanes] * jnp.dot(
            probs_ref[k], before_ref[:, lanes], preferred_element_type=F32
        )
        out_ref[:, lanes] = total
        square = square + total * total
    square_ref[0] = square


def value_mix(probs, before, own, inverse):
    rows, channels = own.shape
    return pl.pallas_call(
        value_kernel,
        out_shape=(
            jax.ShapeDtypeStruct((rows, channels), F32),
            jax.ShapeDtypeStruct((1, rows, LANES), F32),
        ),
        in_specs=[in_vmem()] * 4,
        out_specs=(in_vmem(),) * 2,
        compiler_params=params(),
        cost_estimate=cost(2 * rows * rows * channels, 12 * rows * channels),
        name="value_mix",
    )(probs, before, own, inverse)


def normalize_kernel(count, panels, pieces, with_head, *refs):
    square_refs, refs = refs[:panels], refs[panels:]
    mixed_refs, refs = refs[:count], refs[count:]
    if with_head:
        head_ref, refs = refs[0], refs[1:]
    out_refs, (held_ref, sems) = refs[:count], refs[count:]
    rows = mixed_refs[0].shape[0]
    piece = rows // pieces
    copies = []
    for n in range(count):
        square = square_refs[0][n]
        for ref in square_refs[1:]:
            square = square + ref[n]
        scale = lax.rsqrt(jnp.sum(square, axis=-1, keepdims=True) * (1.0 / CHANNELS) + 1e-06)
        for m in range(pieces):
            at = slice(m * piece, (m + 1) * piece)
            value = mixed_refs[n][at, :]
            if with_head and n == 0 and m == 0:
                value = jnp.concatenate([head_ref[...], value[8:]], axis=0)
            held_ref[n, at, :] = (value * scale[at]).astype(BF16)
            copy = pltpu.make_async_copy(
                held_ref.at[n, pl.ds(m * piece, piece)],
                out_refs[n].at[pl.ds(m * piece, piece)],
                sems.at[n, m],
            )
            copy.start()
            copies.append(copy)
    for copy in copies:
        copy.wait()


def normalize(squares, mixed, head=None, pieces=3):
    rows, channels = mixed[0].shape
    count = len(mixed)
    operands = (*squares, *mixed) + (() if head is None else (head,))
    return pl.pallas_call(
        functools.partial(normalize_kernel, count, len(squares), pieces, head is not None),
        out_shape=(jax.ShapeDtypeStruct((rows, channels), BF16),) * count,
        in_specs=[in_vmem()] * len(operands),
        out_specs=(pl.BlockSpec(memory_space=pl.ANY),) * count,
        scratch_shapes=[
            pltpu.VMEM((count, rows, channels), BF16),
            pltpu.SemaphoreType.DMA((count, pieces)),
        ],
        compiler_params=params(),
        cost_estimate=cost(4 * count * rows * channels, 6 * count * rows * channels),
        name="normalize",
    )(*operands)


def from_behind(value):
    count = lax.axis_size("ctx")
    return lax.ppermute(value, "ctx", [(source, source + 1) for source in range(count - 1)])


def of_panels(square):
    count = lax.axis_size("panel")
    return [square] + [
        lax.ppermute(square, "panel", [(n, (n + shift) % count) for n in range(count)])
        for shift in range(1, count)
    ]


def body(se, se_short, se_filter, mr, mr_short, raw, decay, queries, keys, values):
    decay = decay[None, :]
    key_before = from_behind(keys)
    packet = from_behind(pack(se, mr, se_short, mr_short, 4))
    own, z0, se_mix, se_square, taps, heads = own_part(
        mr, se, mr_short, se_short, raw, decay, se_filter, 4
    )
    values_later, own = lax.optimization_barrier((values, own))
    value_before = from_behind(values_later)
    probs, attended, inverse = score(queries, keys, key_before, values, 4)
    packet, attended = lax.optimization_barrier((packet, attended))
    head, mr_mix, square = mix(
        packet, own, z0, se_square, taps, heads, mr_short, se_short, se_filter
    )
    se_out, mr_out = normalize(of_panels(square), (se_mix, mr_mix), head)
    value_before, se_out, mr_out = lax.optimization_barrier((value_before, se_out, mr_out))
    attended, square = value_mix(probs, value_before, attended, inverse)
    (attn_out,) = normalize(of_panels(square), (attended,))
    return se_out, mr_out, attn_out


def solution(mesh):
    placed = (
        P(None, "ctx", "panel"),
        P(None, None, "panel"),
        P(None, "panel"),
        P(None, "ctx", "panel"),
        P(None, None, "panel"),
        P(None, "panel"),
        P("panel"),
        P("ctx", "panel"),
        P("ctx", "panel"),
        P("ctx", "panel"),
    )
    return jax.shard_map(
        body,
        mesh=mesh,
        in_specs=placed,
        out_specs=(P("ctx", "panel"), P("ctx", "panel"), P("ctx", "panel")),
        check_vma=False,
    )
```

```python
import functools
import math

import jax
import jax.numpy as jnp
from jax import lax
from jax.experimental import pallas as pl
from jax.experimental.pallas import tpu as pltpu
from jax.sharding import PartitionSpec as P

CHANNELS = 4096
HD = 128
LSE = 7
MEDIUM_TAPS = 128
LANES = 128
F32 = jnp.float32
BF16 = jnp.bfloat16


def params(mebibytes=6):
    return pltpu.CompilerParams(vmem_limit_bytes=mebibytes * 1024 * 1024)


def in_vmem():
    return pl.BlockSpec(memory_space=pltpu.VMEM)


def cost(flops, nbytes, trans=0):
    return pl.CostEstimate(flops=int(flops), bytes_accessed=int(nbytes), transcendentals=int(trans))


def roll(value, shift):
    shift = shift % value.shape[0]
    return pltpu.roll(value, shift, 0) if shift else value


def row_is(rows, at):
    return lax.broadcasted_iota(jnp.int32, (rows, LANES), 0) == at


def features(u, front, taps):
    ext = jnp.concatenate([front, u], axis=0)
    total = taps[0] * ext
    for j in range(1, len(taps)):
        total = total + taps[j] * roll(ext, j)
    return total[8:]


def tap_rows(ref, stream, lanes):
    return [ref[stream, j : j + 1, lanes] for j in range(ref.shape[1])]


def lane_block(k):
    return pl.ds(pl.multiple_of(k * LANES, LANES), LANES)


def tap_tile(held_ref, j):
    return jnp.broadcast_to(held_ref[j : j + 1, :], (8, LANES))


def pack_kernel(
    per, mr_ref, se_ref, mr_short_ref, se_short_ref, out_ref, m_ref, tail_ref, mw_ref, sw_ref, last_ref, sems
):
    _, rows, channels = mr_ref.shape
    width = per * LANES
    chunk = MEDIUM_TAPS + 16
    nothing = jnp.zeros((8, LANES), F32)
    end = pl.ds(rows - 16, 16)
    copies = [
        pltpu.make_async_copy(mr_short_ref, mw_ref, sems.at[0]),
        pltpu.make_async_copy(se_short_ref, sw_ref, sems.at[1]),
        pltpu.make_async_copy(mr_ref.at[pl.ds(0, 1), end], tail_ref.at[pl.ds(0, 1)], sems.at[2]),
        pltpu.make_async_copy(se_ref.at[:, end], tail_ref.at[pl.ds(1, 3)], sems.at[3]),
    ]
    first = len(copies)
    for n in range(channels // width):
        at = pl.ds(n * width, width)
        copies.append(
            pltpu.make_async_copy(
                mr_ref.at[pl.ds(1, 2), :, at], m_ref.at[:, :, at], sems.at[first + n]
            )
        )
    for copy in copies:
        copy.start()
    for copy in copies[:first]:
        copy.wait()
    last_ref[...] = jnp.zeros_like(last_ref)

    def one(block):
        lanes = lane_block(block)
        m1 = m_ref[0, :, lanes].astype(F32)
        m2 = m_ref[1, :, lanes].astype(F32)
        z1 = features(m1, nothing, tap_rows(mw_ref, 1, lanes))
        z2 = features(m2, nothing, tap_rows(mw_ref, 2, lanes))
        product = (z1 * z2)[rows - MEDIUM_TAPS :]
        tail_m0 = tail_ref[0, :, lanes].astype(F32)[8:]
        tail_m1, tail_m2 = m1[rows - 8 :], m2[rows - 8 :]
        head = jnp.where(row_is(8, 0), roll(tail_m2, 2), product[:8])
        product = jnp.concatenate([head, product[8:]], axis=0)
        s0 = tail_ref[1, :, lanes].astype(F32)[8:]
        s1 = tail_ref[2, :, lanes].astype(F32)
        s2 = tail_ref[3, :, lanes].astype(F32)
        y1 = features(s1, nothing, tap_rows(sw_ref, 1, lanes))[8:]
        y2 = features(s2, nothing, tap_rows(sw_ref, 2, lanes))[8:]
        at = lax.broadcasted_iota(jnp.int32, (8, LANES), 0)
        x1 = jnp.where(at < 2, roll(s0, 2), y1 * y2)
        x2 = jnp.where(
            at < 2,
            roll(s1[8:], 2),
            jnp.where(at < 4, roll(s2[8:], 4), jnp.where(at < 6, roll(tail_m0, 6), tail_m1)),
        )
        start = pl.multiple_of(block * chunk, 16)
        out_ref[pl.ds(start, MEDIUM_TAPS), :] = product.astype(BF16)
        out_ref[pl.ds(start + MEDIUM_TAPS, 16), :] = jnp.concatenate([x1, x2], axis=0).astype(BF16)
        last_ref[pl.ds(block, 1), :] = tail_m2[7:8]

    for n in range(channels // width):
        copies[first + n].wait()
        pl.loop(n * per, (n + 1) * per)(one)

    out_ref[out_ref.shape[0] - 16 :, :] = last_ref[...].astype(BF16)


def pack(se, mr, se_short, mr_short, per):
    _, rows, channels = se.shape
    blocks = channels // LANES
    total = blocks * (MEDIUM_TAPS + 16) + 16
    return pl.pallas_call(
        functools.partial(pack_kernel, per),
        out_shape=jax.ShapeDtypeStruct((total, LANES), BF16),
        in_specs=[pl.BlockSpec(memory_space=pltpu.HBM)] * 4,
        out_specs=in_vmem(),
        scratch_shapes=[
            pltpu.VMEM((2, rows, channels), BF16),
            pltpu.VMEM((4, 16, channels), BF16),
            pltpu.VMEM(mr_short.shape, F32),
            pltpu.VMEM(se_short.shape, F32),
            pltpu.VMEM((16, LANES), F32),
            pltpu.SemaphoreType.DMA((4 + blocks // per,)),
        ],
        compiler_params=params(),
        cost_estimate=cost(20 * rows * channels, 6 * rows * channels),
        name="pack",
    )(*(pltpu.with_memory_space_constraint(x, pltpu.HBM) for x in (mr, se, mr_short, se_short)))


def own_kernel(
    per,
    m_ref,
    s_ref,
    mw_ref,
    sw_ref,
    raw_hbm_ref,
    decay_ref,
    filter_ref,
    own_ref,
    z0_ref,
    se_ref,
    square_ref,
    taps_ref,
    heads_ref,
    raw_ref,
    held_ref,
    sems,
):
    rows, channels = own_ref.shape
    tiles = rows // 8
    width = per * LANES
    nothing = jnp.zeros((8, LANES), F32)

    def fetch(n):
        at = pl.ds(pl.multiple_of(n * width, width), width)
        return pltpu.make_async_copy(raw_hbm_ref.at[:, at], raw_ref.at[:, at], sems.at[n])

    for n in range(channels // width):
        fetch(n).start()
    square_ref[...] = jnp.zeros_like(square_ref)

    @pl.loop(0, channels // LANES)
    def _(k):
        @pl.when(k % per == 0)
        def _():
            fetch(k // per).wait()

        lanes = lane_block(k)
        u = [s_ref[n, :, lanes].astype(F32) for n in range(3)]
        for n in range(3):
            heads_ref[n, :, lanes] = u[n][:8]
        s = [features(u[n], nothing, tap_rows(sw_ref, n, lanes)) for n in range(3)]
        ext = jnp.concatenate([nothing, (s[1] * s[2]).astype(BF16).astype(F32)], axis=0)
        total = filter_ref[0:1, lanes] * ext
        for j in range(1, LSE):
            total = total + filter_ref[j : j + 1, lanes] * roll(ext, j)
        mixed = s[0] * total[8:]
        se_ref[:, lanes] = mixed
        square_ref[8:, :] += mixed[8:] * mixed[8:]

        steps = lax.broadcasted_iota(jnp.int32, (MEDIUM_TAPS, LANES), 0).astype(F32)
        taps = raw_ref[:, lanes] * jnp.exp(-decay_ref[0:1, lanes] * steps)
        held_ref[...] = taps
        taps_ref[:, lanes] = taps
        u = [m_ref[n, :, lanes].astype(F32) for n in range(3)]
        for n in range(3):
            heads_ref[3 + n, :, lanes] = u[n][:8]
        z = [features(u[n], nothing, tap_rows(mw_ref, n, lanes)) for n in range(3)]
        z0_ref[:, lanes] = z[0]
        product = (z[1] * z[2]).astype(BF16).astype(F32)
        at = lax.broadcasted_iota(jnp.int32, (8, LANES), 0)
        head = jnp.where(at < 2, 0.0, product[:8])
        ext = jnp.concatenate([nothing, head, product[8:]], axis=0)
        total = [None] * tiles
        for r in range(8):
            shifted = roll(ext, r)
            tap = [tap_tile(held_ref, 8 * a + r) for a in range(MEDIUM_TAPS // 8)]
            for i in range(tiles):
                for a in range(min(i + 1, MEDIUM_TAPS // 8)):
                    at_tile = 8 * (i - a + 1)
                    term = tap[a] * shifted[at_tile : at_tile + 8]
                    total[i] = term if total[i] is None else total[i] + term
        own_ref[:, lanes] = jnp.concatenate(total, axis=0)


def own_part(mr, se, mr_short, se_short, raw, decay, se_filter, per):
    _, rows, channels = mr.shape
    mixed = jax.ShapeDtypeStruct((rows, channels), F32)
    raw = pltpu.with_memory_space_constraint(raw, pltpu.HBM)
    return pl.pallas_call(
        functools.partial(own_kernel, per),
        out_shape=(
            mixed,
            mixed,
            mixed,
            jax.ShapeDtypeStruct((rows, LANES), F32),
            jax.ShapeDtypeStruct((MEDIUM_TAPS, channels), F32),
            jax.ShapeDtypeStruct((6, 8, channels), F32),
        ),
        in_specs=[in_vmem()] * 4 + [pl.BlockSpec(memory_space=pltpu.HBM)] + [in_vmem()] * 2,
        out_specs=(in_vmem(),) * 6,
        scratch_shapes=[
            pltpu.VMEM((MEDIUM_TAPS, channels), F32),
            pltpu.VMEM((MEDIUM_TAPS, LANES), F32),
            pltpu.SemaphoreType.DMA((channels // (per * LANES),)),
        ],
        compiler_params=params(),
        cost_estimate=cost(180 * rows * channels, 24 * rows * channels),
        name="own_part",
    )(mr, se, mr_short, se_short, raw, decay, se_filter)


def mix_kernel(
    packet_ref,
    own_ref,
    z0_ref,
    se_square_ref,
    taps_ref,
    heads_ref,
    mw_ref,
    sw_ref,
    filter_ref,
    head_ref,
    mr_ref,
    square_ref,
    last_ref,
    held_ref,
):
    rows, channels = own_ref.shape
    tiles = rows // 8
    chunk = MEDIUM_TAPS + 16
    nothing = jnp.zeros((8, LANES), F32)
    last_ref[...] = packet_ref[packet_ref.shape[0] - 16 :, :].astype(F32)
    square_ref[0] = se_square_ref[...]
    square_ref[1] = jnp.zeros((rows, LANES), F32)

    @pl.loop(0, channels // LANES)
    def _(k):
        lanes = lane_block(k)
        start = pl.multiple_of(k * chunk, 16)
        before = packet_ref[pl.ds(start, MEDIUM_TAPS), :].astype(F32)
        x = packet_ref[pl.ds(start + MEDIUM_TAPS, 16), :].astype(F32)
        x1, x2 = x[:8], x[8:]
        last = last_ref[pl.ds(k, 1), :]

        fronts = (roll(x1, 6), roll(x2, 6), roll(x2, 4))
        s = [
            features(heads_ref[n, :, lanes], fronts[n], tap_rows(sw_ref, n, lanes))
            for n in range(3)
        ]
        ext = jnp.concatenate([x1, (s[1] * s[2]).astype(BF16).astype(F32)], axis=0)
        total = filter_ref[0:1, lanes] * ext
        for j in range(1, LSE):
            total = total + filter_ref[j : j + 1, lanes] * roll(ext, j)
        mixed = s[0] * total[8:]
        head_ref[:, lanes] = mixed
        square_ref[0, :8, :] += mixed * mixed

        taps = taps_ref[:, lanes]
        held_ref[...] = taps
        front2 = jnp.where(row_is(8, 7), last, roll(before[:8], 6))
        fronts = (roll(x2, 2), x2, front2)
        z = [
            features(heads_ref[3 + n, :, lanes], fronts[n], tap_rows(mw_ref, n, lanes))
            for n in range(3)
        ]
        first = (z[1] * z[2]).astype(BF16).astype(F32)
        padded = jnp.concatenate([taps, jnp.zeros((rows - MEDIUM_TAPS, LANES), F32)], axis=0)
        base = own_ref[:, lanes] + padded * first[0:1] + roll(padded, 1) * first[1:2]
        total = [base[8 * i : 8 * i + 8] for i in range(tiles)]
        ext = jnp.concatenate([before, nothing], axis=0)
        count = MEDIUM_TAPS // 8
        for r in range(8):
            shifted = roll(ext, r)
            tap = [tap_tile(held_ref, 8 * a + r) for a in range(count)]
            for i in range(count):
                for a in range(i if r else i + 1, count):
                    at_tile = 8 * (i - a + count)
                    total[i] = total[i] + tap[a] * shifted[at_tile : at_tile + 8]
        z0 = jnp.concatenate([z[0], z0_ref[8:, lanes]], axis=0)
        mixed = z0 * jnp.concatenate(total, axis=0)
        mr_ref[:, lanes] = mixed
        square_ref[1] += mixed * mixed


def mix(packet, own, z0, se_square, taps, heads, mr_short, se_short, se_filter):
    rows, channels = own.shape
    return pl.pallas_call(
        mix_kernel,
        out_shape=(
            jax.ShapeDtypeStruct((8, channels), F32),
            jax.ShapeDtypeStruct((rows, channels), F32),
            jax.ShapeDtypeStruct((2, rows, LANES), F32),
        ),
        in_specs=[in_vmem()] * 9,
        out_specs=(in_vmem(),) * 3,
        scratch_shapes=[pltpu.VMEM((16, LANES), F32), pltpu.VMEM((MEDIUM_TAPS, LANES), F32)],
        compiler_params=params(),
        cost_estimate=cost(140 * rows * channels, 16 * rows * channels),
        name="mix",
    )(packet, own, z0, se_square, taps, heads, mr_short, se_short, se_filter)


def score_kernel(per, q_ref, k_ref, before_ref, v_ref, probs_ref, out_ref, inverse_ref, bias_ref):
    rows, channels = q_ref.shape
    at = lax.broadcasted_iota(jnp.int32, (rows, 2 * rows), 0)
    key = lax.broadcasted_iota(jnp.int32, (rows, 2 * rows), 1)
    valid = (key <= at + rows) & ((key >= rows) | (lax.axis_index("ctx") > 0))
    bias_ref[...] = jnp.where(valid, 0.0, -1e30)
    factor = math.log2(math.e) / math.sqrt(HD)
    zeros, ones = jnp.zeros((rows, LANES), BF16), jnp.ones((rows, LANES), BF16)

    @pl.loop(0, channels // (LANES * per))
    def _(group):
        for n in range(per):
            head = group * per + n
            lanes = lane_block(head)
            both = jnp.concatenate([before_ref[:, lanes], k_ref[:, lanes]], axis=0)
            scores = lax.dot_general(
                q_ref[:, lanes], both, (((1,), (1,)), ((), ())), preferred_element_type=F32
            )
            scores = scores + bias_ref[...]
            top = jnp.max(scores, axis=-1, keepdims=True)
            probs = jnp.exp2((scores - top) * factor).astype(BF16)
            probs_ref[head] = probs[:, :rows]
            own = jnp.concatenate(
                [
                    jnp.concatenate([zeros, v_ref[:, lanes]], axis=0),
                    jnp.concatenate([ones, ones], axis=0),
                ],
                axis=1,
            )
            total = jnp.dot(probs, own, preferred_element_type=F32)
            inverse = 1.0 / total[:, LANES:]
            inverse_ref[:, lanes] = inverse
            out_ref[:, lanes] = total[:, :LANES] * inverse


def score(queries, keys, before, values, per):
    rows, channels = queries.shape
    flat = jax.ShapeDtypeStruct((rows, channels), F32)
    return pl.pallas_call(
        functools.partial(score_kernel, per),
        out_shape=(jax.ShapeDtypeStruct((channels // HD, rows, rows), BF16), flat, flat),
        in_specs=[in_vmem()] * 4,
        out_specs=(in_vmem(),) * 3,
        scratch_shapes=[pltpu.VMEM((rows, 2 * rows), F32)],
        compiler_params=params(),
        cost_estimate=cost(
            8 * rows * rows * channels, 14 * rows * channels, 4 * rows * rows * channels // HD
        ),
        name="score",
    )(queries, keys, before, values)


def value_kernel(probs_ref, before_ref, own_ref, inverse_ref, out_ref, square_ref):
    rows, channels = own_ref.shape
    square = jnp.zeros((rows, LANES), F32)
    for k in range(channels // LANES):
        lanes = slice(k * LANES, (k + 1) * LANES)
        total = own_ref[:, lanes] + inverse_ref[:, lanes] * jnp.dot(
            probs_ref[k], before_ref[:, lanes], preferred_element_type=F32
        )
        out_ref[:, lanes] = total
        square = square + total * total
    square_ref[0] = square


def value_mix(probs, before, own, inverse):
    rows, channels = own.shape
    return pl.pallas_call(
        value_kernel,
        out_shape=(
            jax.ShapeDtypeStruct((rows, channels), F32),
            jax.ShapeDtypeStruct((1, rows, LANES), F32),
        ),
        in_specs=[in_vmem()] * 4,
        out_specs=(in_vmem(),) * 2,
        compiler_params=params(),
        cost_estimate=cost(2 * rows * rows * channels, 12 * rows * channels),
        name="value_mix",
    )(probs, before, own, inverse)


def normalize_kernel(count, panels, pieces, with_head, *refs):
    square_refs, refs = refs[:panels], refs[panels:]
    mixed_refs, refs = refs[:count], refs[count:]
    if with_head:
        head_ref, refs = refs[0], refs[1:]
    out_refs, (held_ref, sems) = refs[:count], refs[count:]
    rows = mixed_refs[0].shape[0]
    piece = rows // pieces
    copies = []
    for n in range(count):
        for m in range(pieces):
            at = slice(m * piece, (m + 1) * piece)
            square = square_refs[0][n, at, :]
            for ref in square_refs[1:]:
                square = square + ref[n, at, :]
            scale = lax.rsqrt(jnp.sum(square, axis=-1, keepdims=True) * (1.0 / CHANNELS) + 1e-06)
            value = mixed_refs[n][at, :]
            if with_head and n == 0 and m == 0:
                value = jnp.concatenate([head_ref[...], value[8:]], axis=0)
            held_ref[n, at, :] = (value * scale).astype(BF16)
            copy = pltpu.make_async_copy(
                held_ref.at[n, pl.ds(m * piece, piece)],
                out_refs[n].at[pl.ds(m * piece, piece)],
                sems.at[n, m],
            )
            copy.start()
            copies.append(copy)
    for copy in copies:
        copy.wait()


def normalize(squares, mixed, head=None, pieces=9):
    rows, channels = mixed[0].shape
    count = len(mixed)
    operands = (*squares, *mixed) + (() if head is None else (head,))
    return pl.pallas_call(
        functools.partial(normalize_kernel, count, len(squares), pieces, head is not None),
        out_shape=(jax.ShapeDtypeStruct((rows, channels), BF16),) * count,
        in_specs=[in_vmem()] * len(operands),
        out_specs=(pl.BlockSpec(memory_space=pl.ANY),) * count,
        scratch_shapes=[
            pltpu.VMEM((count, rows, channels), BF16),
            pltpu.SemaphoreType.DMA((count, pieces)),
        ],
        compiler_params=params(),
        cost_estimate=cost(4 * count * rows * channels, 6 * count * rows * channels),
        name="normalize",
    )(*operands)


def from_behind(value):
    count = lax.axis_size("ctx")
    return lax.ppermute(value, "ctx", [(source, source + 1) for source in range(count - 1)])


def of_panels(square):
    count = lax.axis_size("panel")
    return [square] + [
        lax.ppermute(square, "panel", [(n, (n + shift) % count) for n in range(count)])
        for shift in range(1, count)
    ]


def body(se, se_short, se_filter, mr, mr_short, raw, decay, queries, keys, values):
    decay = decay[None, :]
    key_before = from_behind(keys)
    packet = from_behind(pack(se, mr, se_short, mr_short, 4))
    own, z0, se_mix, se_square, taps, heads = own_part(
        mr, se, mr_short, se_short, raw, decay, se_filter, 4
    )
    value_before = from_behind(values)
    probs, attended, inverse = score(queries, keys, key_before, values, 4)
    packet, attended = lax.optimization_barrier((packet, attended))
    head, mr_mix, square = mix(
        packet, own, z0, se_square, taps, heads, mr_short, se_short, se_filter
    )
    se_out, mr_out = normalize(of_panels(square), (se_mix, mr_mix), head)
    value_before, se_out, mr_out = lax.optimization_barrier((value_before, se_out, mr_out))
    attended, square = value_mix(probs, value_before, attended, inverse)
    (attn_out,) = normalize(of_panels(square), (attended,))
    return se_out, mr_out, attn_out


def solution(mesh):
    placed = (
        P(None, "ctx", "panel"),
        P(None, None, "panel"),
        P(None, "panel"),
        P(None, "ctx", "panel"),
        P(None, None, "panel"),
        P(None, "panel"),
        P("panel"),
        P("ctx", "panel"),
        P("ctx", "panel"),
        P("ctx", "panel"),
    )
    return jax.shard_map(
        body,
        mesh=mesh,
        in_specs=placed,
        out_specs=(P("ctx", "panel"), P("ctx", "panel"), P("ctx", "panel")),
        check_vma=False,
    )
```

```python
import functools
import math

import jax
import jax.numpy as jnp
from jax import lax
from jax.experimental import pallas as pl
from jax.experimental.pallas import tpu as pltpu
from jax.sharding import PartitionSpec as P

CHANNELS = 4096
HD = 128
LSE = 7
MEDIUM_TAPS = 128
LANES = 128
F32 = jnp.float32
BF16 = jnp.bfloat16


def params(mebibytes=6):
    return pltpu.CompilerParams(vmem_limit_bytes=mebibytes * 1024 * 1024)


def in_vmem():
    return pl.BlockSpec(memory_space=pltpu.VMEM)


def cost(flops, nbytes, trans=0):
    return pl.CostEstimate(flops=int(flops), bytes_accessed=int(nbytes), transcendentals=int(trans))


def roll(value, shift):
    shift = shift % value.shape[0]
    return pltpu.roll(value, shift, 0) if shift else value


def row_is(rows, at):
    return lax.broadcasted_iota(jnp.int32, (rows, LANES), 0) == at


def features(u, front, taps):
    ext = jnp.concatenate([front, u], axis=0)
    total = taps[0] * ext
    for j in range(1, len(taps)):
        total = total + taps[j] * roll(ext, j)
    return total[8:]


def tap_rows(ref, stream, lanes):
    return [ref[stream, j : j + 1, lanes] for j in range(ref.shape[1])]


def lane_block(k):
    return pl.ds(pl.multiple_of(k * LANES, LANES), LANES)


def tap_tile(held_ref, j):
    return jnp.broadcast_to(held_ref[j : j + 1, :], (8, LANES))


def pack_kernel(
    per, mr_ref, se_ref, mr_short_ref, se_short_ref, out_ref, m_ref, tail_ref, mw_ref, sw_ref, last_ref, sems
):
    _, rows, channels = mr_ref.shape
    width = per * LANES
    chunk = MEDIUM_TAPS + 16
    nothing = jnp.zeros((8, LANES), F32)
    end = pl.ds(rows - 16, 16)
    copies = [
        pltpu.make_async_copy(mr_short_ref, mw_ref, sems.at[0]),
        pltpu.make_async_copy(se_short_ref, sw_ref, sems.at[1]),
        pltpu.make_async_copy(mr_ref.at[pl.ds(0, 1), end], tail_ref.at[pl.ds(0, 1)], sems.at[2]),
        pltpu.make_async_copy(se_ref.at[:, end], tail_ref.at[pl.ds(1, 3)], sems.at[3]),
    ]
    first = len(copies)
    for n in range(channels // width):
        at = pl.ds(n * width, width)
        copies.append(
            pltpu.make_async_copy(
                mr_ref.at[pl.ds(1, 2), :, at], m_ref.at[:, :, at], sems.at[first + n]
            )
        )
    for copy in copies:
        copy.start()
    for copy in copies[:first]:
        copy.wait()
    last_ref[...] = jnp.zeros_like(last_ref)

    def one(block):
        lanes = lane_block(block)
        m1 = m_ref[0, :, lanes].astype(F32)
        m2 = m_ref[1, :, lanes].astype(F32)
        z1 = features(m1, nothing, tap_rows(mw_ref, 1, lanes))
        z2 = features(m2, nothing, tap_rows(mw_ref, 2, lanes))
        product = (z1 * z2)[rows - MEDIUM_TAPS :]
        tail_m0 = tail_ref[0, :, lanes].astype(F32)[8:]
        tail_m1, tail_m2 = m1[rows - 8 :], m2[rows - 8 :]
        head = jnp.where(row_is(8, 0), roll(tail_m2, 2), product[:8])
        product = jnp.concatenate([head, product[8:]], axis=0)
        s0 = tail_ref[1, :, lanes].astype(F32)[8:]
        s1 = tail_ref[2, :, lanes].astype(F32)
        s2 = tail_ref[3, :, lanes].astype(F32)
        y1 = features(s1, nothing, tap_rows(sw_ref, 1, lanes))[8:]
        y2 = features(s2, nothing, tap_rows(sw_ref, 2, lanes))[8:]
        at = lax.broadcasted_iota(jnp.int32, (8, LANES), 0)
        x1 = jnp.where(at < 2, roll(s0, 2), y1 * y2)
        x2 = jnp.where(
            at < 2,
            roll(s1[8:], 2),
            jnp.where(at < 4, roll(s2[8:], 4), jnp.where(at < 6, roll(tail_m0, 6), tail_m1)),
        )
        start = pl.multiple_of(block * chunk, 16)
        out_ref[pl.ds(start, MEDIUM_TAPS), :] = product.astype(BF16)
        out_ref[pl.ds(start + MEDIUM_TAPS, 16), :] = jnp.concatenate([x1, x2], axis=0).astype(BF16)
        last_ref[pl.ds(block, 1), :] = tail_m2[7:8]

    for n in range(channels // width):
        copies[first + n].wait()
        pl.loop(n * per, (n + 1) * per)(one)

    out_ref[out_ref.shape[0] - 16 :, :] = last_ref[...].astype(BF16)


def pack(se, mr, se_short, mr_short, per):
    _, rows, channels = se.shape
    blocks = channels // LANES
    total = blocks * (MEDIUM_TAPS + 16) + 16
    return pl.pallas_call(
        functools.partial(pack_kernel, per),
        out_shape=jax.ShapeDtypeStruct((total, LANES), BF16),
        in_specs=[pl.BlockSpec(memory_space=pltpu.HBM)] * 4,
        out_specs=in_vmem(),
        scratch_shapes=[
            pltpu.VMEM((2, rows, channels), BF16),
            pltpu.VMEM((4, 16, channels), BF16),
            pltpu.VMEM(mr_short.shape, F32),
            pltpu.VMEM(se_short.shape, F32),
            pltpu.VMEM((16, LANES), F32),
            pltpu.SemaphoreType.DMA((4 + blocks // per,)),
        ],
        compiler_params=params(),
        cost_estimate=cost(20 * rows * channels, 6 * rows * channels),
        name="pack",
    )(*(pltpu.with_memory_space_constraint(x, pltpu.HBM) for x in (mr, se, mr_short, se_short)))


def own_kernel(
    per,
    m_ref,
    s_ref,
    mw_ref,
    sw_ref,
    raw_hbm_ref,
    decay_ref,
    filter_ref,
    own_ref,
    z0_ref,
    se_ref,
    square_ref,
    taps_ref,
    heads_ref,
    raw_ref,
    held_ref,
    sems,
):
    rows, channels = own_ref.shape
    tiles = rows // 8
    width = per * LANES
    nothing = jnp.zeros((8, LANES), F32)

    def fetch(n):
        at = pl.ds(pl.multiple_of(n * width, width), width)
        return pltpu.make_async_copy(raw_hbm_ref.at[:, at], raw_ref.at[:, at], sems.at[n])

    for n in range(channels // width):
        fetch(n).start()
    square_ref[...] = jnp.zeros_like(square_ref)

    @pl.loop(0, channels // LANES)
    def _(k):
        @pl.when(k % per == 0)
        def _():
            fetch(k // per).wait()

        lanes = lane_block(k)
        u = [s_ref[n, :, lanes].astype(F32) for n in range(3)]
        for n in range(3):
            heads_ref[n, :, lanes] = u[n][:8]
        s = [features(u[n], nothing, tap_rows(sw_ref, n, lanes)) for n in range(3)]
        ext = jnp.concatenate([nothing, (s[1] * s[2]).astype(BF16).astype(F32)], axis=0)
        total = filter_ref[0:1, lanes] * ext
        for j in range(1, LSE):
            total = total + filter_ref[j : j + 1, lanes] * roll(ext, j)
        mixed = s[0] * total[8:]
        se_ref[:, lanes] = mixed
        square_ref[8:, :] += mixed[8:] * mixed[8:]

        steps = lax.broadcasted_iota(jnp.int32, (MEDIUM_TAPS, LANES), 0).astype(F32)
        taps = raw_ref[:, lanes] * jnp.exp(-decay_ref[0:1, lanes] * steps)
        held_ref[...] = taps
        taps_ref[:, lanes] = taps
        u = [m_ref[n, :, lanes].astype(F32) for n in range(3)]
        for n in range(3):
            heads_ref[3 + n, :, lanes] = u[n][:8]
        z = [features(u[n], nothing, tap_rows(mw_ref, n, lanes)) for n in range(3)]
        z0_ref[:, lanes] = z[0]
        product = (z[1] * z[2]).astype(BF16).astype(F32)
        at = lax.broadcasted_iota(jnp.int32, (8, LANES), 0)
        head = jnp.where(at < 2, 0.0, product[:8])
        ext = jnp.concatenate([nothing, head, product[8:]], axis=0)
        total = [None] * tiles
        for r in range(8):
            shifted = roll(ext, r)
            tap = [tap_tile(held_ref, 8 * a + r) for a in range(MEDIUM_TAPS // 8)]
            for i in range(tiles):
                for a in range(min(i + 1, MEDIUM_TAPS // 8)):
                    at_tile = 8 * (i - a + 1)
                    term = tap[a] * shifted[at_tile : at_tile + 8]
                    total[i] = term if total[i] is None else total[i] + term
        own_ref[:, lanes] = jnp.concatenate(total, axis=0)


def own_part(mr, se, mr_short, se_short, raw, decay, se_filter, per):
    _, rows, channels = mr.shape
    mixed = jax.ShapeDtypeStruct((rows, channels), F32)
    raw = pltpu.with_memory_space_constraint(raw, pltpu.HBM)
    return pl.pallas_call(
        functools.partial(own_kernel, per),
        out_shape=(
            mixed,
            mixed,
            mixed,
            jax.ShapeDtypeStruct((rows, LANES), F32),
            jax.ShapeDtypeStruct((MEDIUM_TAPS, channels), F32),
            jax.ShapeDtypeStruct((6, 8, channels), F32),
        ),
        in_specs=[in_vmem()] * 4 + [pl.BlockSpec(memory_space=pltpu.HBM)] + [in_vmem()] * 2,
        out_specs=(in_vmem(),) * 6,
        scratch_shapes=[
            pltpu.VMEM((MEDIUM_TAPS, channels), F32),
            pltpu.VMEM((MEDIUM_TAPS, LANES), F32),
            pltpu.SemaphoreType.DMA((channels // (per * LANES),)),
        ],
        compiler_params=params(),
        cost_estimate=cost(180 * rows * channels, 24 * rows * channels),
        name="own_part",
    )(mr, se, mr_short, se_short, raw, decay, se_filter)


def mix_kernel(
    packet_ref,
    own_ref,
    z0_ref,
    se_square_ref,
    taps_ref,
    heads_ref,
    mw_ref,
    sw_ref,
    filter_ref,
    head_ref,
    mr_ref,
    square_ref,
    last_ref,
    held_ref,
):
    rows, channels = own_ref.shape
    tiles = rows // 8
    chunk = MEDIUM_TAPS + 16
    nothing = jnp.zeros((8, LANES), F32)
    last_ref[...] = packet_ref[packet_ref.shape[0] - 16 :, :].astype(F32)
    square_ref[0] = se_square_ref[...]
    square_ref[1] = jnp.zeros((rows, LANES), F32)

    @pl.loop(0, channels // LANES)
    def _(k):
        lanes = lane_block(k)
        start = pl.multiple_of(k * chunk, 16)
        before = packet_ref[pl.ds(start, MEDIUM_TAPS), :].astype(F32)
        x = packet_ref[pl.ds(start + MEDIUM_TAPS, 16), :].astype(F32)
        x1, x2 = x[:8], x[8:]
        last = last_ref[pl.ds(k, 1), :]

        fronts = (roll(x1, 6), roll(x2, 6), roll(x2, 4))
        s = [
            features(heads_ref[n, :, lanes], fronts[n], tap_rows(sw_ref, n, lanes))
            for n in range(3)
        ]
        ext = jnp.concatenate([x1, (s[1] * s[2]).astype(BF16).astype(F32)], axis=0)
        total = filter_ref[0:1, lanes] * ext
        for j in range(1, LSE):
            total = total + filter_ref[j : j + 1, lanes] * roll(ext, j)
        mixed = s[0] * total[8:]
        head_ref[:, lanes] = mixed
        square_ref[0, :8, :] += mixed * mixed

        taps = taps_ref[:, lanes]
        held_ref[...] = taps
        front2 = jnp.where(row_is(8, 7), last, roll(before[:8], 6))
        fronts = (roll(x2, 2), x2, front2)
        z = [
            features(heads_ref[3 + n, :, lanes], fronts[n], tap_rows(mw_ref, n, lanes))
            for n in range(3)
        ]
        first = (z[1] * z[2]).astype(BF16).astype(F32)
        padded = jnp.concatenate([taps, jnp.zeros((rows - MEDIUM_TAPS, LANES), F32)], axis=0)
        base = own_ref[:, lanes] + padded * first[0:1] + roll(padded, 1) * first[1:2]
        total = [base[8 * i : 8 * i + 8] for i in range(tiles)]
        ext = jnp.concatenate([before, nothing], axis=0)
        count = MEDIUM_TAPS // 8
        for r in range(8):
            shifted = roll(ext, r)
            tap = [tap_tile(held_ref, 8 * a + r) for a in range(count)]
            for i in range(count):
                for a in range(i if r else i + 1, count):
                    at_tile = 8 * (i - a + count)
                    total[i] = total[i] + tap[a] * shifted[at_tile : at_tile + 8]
        z0 = jnp.concatenate([z[0], z0_ref[8:, lanes]], axis=0)
        mixed = z0 * jnp.concatenate(total, axis=0)
        mr_ref[:, lanes] = mixed
        square_ref[1] += mixed * mixed


def mix(packet, own, z0, se_square, taps, heads, mr_short, se_short, se_filter):
    rows, channels = own.shape
    return pl.pallas_call(
        mix_kernel,
        out_shape=(
            jax.ShapeDtypeStruct((8, channels), F32),
            jax.ShapeDtypeStruct((rows, channels), F32),
            jax.ShapeDtypeStruct((2, rows, LANES), F32),
        ),
        in_specs=[in_vmem()] * 9,
        out_specs=(in_vmem(),) * 3,
        scratch_shapes=[pltpu.VMEM((16, LANES), F32), pltpu.VMEM((MEDIUM_TAPS, LANES), F32)],
        compiler_params=params(),
        cost_estimate=cost(140 * rows * channels, 16 * rows * channels),
        name="mix",
    )(packet, own, z0, se_square, taps, heads, mr_short, se_short, se_filter)


def score_kernel(per, q_ref, k_ref, before_ref, v_ref, probs_ref, out_ref, inverse_ref, bias_ref):
    rows, channels = q_ref.shape
    at = lax.broadcasted_iota(jnp.int32, (rows, 2 * rows), 0)
    key = lax.broadcasted_iota(jnp.int32, (rows, 2 * rows), 1)
    valid = (key <= at + rows) & ((key >= rows) | (lax.axis_index("ctx") > 0))
    bias_ref[...] = jnp.where(valid, 0.0, -1e30)
    factor = math.log2(math.e) / math.sqrt(HD)
    zeros, ones = jnp.zeros((rows, LANES), BF16), jnp.ones((rows, LANES), BF16)

    @pl.loop(0, channels // (LANES * per))
    def _(group):
        for n in range(per):
            head = group * per + n
            lanes = lane_block(head)
            both = jnp.concatenate([before_ref[:, lanes], k_ref[:, lanes]], axis=0)
            scores = lax.dot_general(
                q_ref[:, lanes], both, (((1,), (1,)), ((), ())), preferred_element_type=F32
            )
            scores = scores + bias_ref[...]
            top = jnp.max(scores, axis=-1, keepdims=True)
            probs = jnp.exp2((scores - top) * factor).astype(BF16)
            probs_ref[head] = probs[:, :rows]
            own = jnp.concatenate(
                [
                    jnp.concatenate([zeros, v_ref[:, lanes]], axis=0),
                    jnp.concatenate([ones, ones], axis=0),
                ],
                axis=1,
            )
            total = jnp.dot(probs, own, preferred_element_type=F32)
            inverse = 1.0 / total[:, LANES:]
            inverse_ref[:, lanes] = inverse
            out_ref[:, lanes] = total[:, :LANES] * inverse


def score(queries, keys, before, values, per):
    rows, channels = queries.shape
    flat = jax.ShapeDtypeStruct((rows, channels), F32)
    return pl.pallas_call(
        functools.partial(score_kernel, per),
        out_shape=(jax.ShapeDtypeStruct((channels // HD, rows, rows), BF16), flat, flat),
        in_specs=[in_vmem()] * 4,
        out_specs=(in_vmem(),) * 3,
        scratch_shapes=[pltpu.VMEM((rows, 2 * rows), F32)],
        compiler_params=params(),
        cost_estimate=cost(
            8 * rows * rows * channels, 14 * rows * channels, 4 * rows * rows * channels // HD
        ),
        name="score",
    )(queries, keys, before, values)


def value_kernel(probs_ref, before_ref, own_ref, inverse_ref, others_ref, out_ref, square_ref):
    rows, channels = own_ref.shape
    square = jnp.zeros((rows, LANES), F32)
    for k in range(channels // LANES):
        lanes = slice(k * LANES, (k + 1) * LANES)
        total = own_ref[:, lanes] + inverse_ref[:, lanes] * jnp.dot(
            probs_ref[k], before_ref[:, lanes], preferred_element_type=F32
        )
        out_ref[:, lanes] = total
        square = square + total * total
    square_ref[:2] = others_ref[...]
    square_ref[2] = square


def value_mix(probs, before, own, inverse, square):
    rows, channels = own.shape
    return pl.pallas_call(
        value_kernel,
        out_shape=(
            jax.ShapeDtypeStruct((rows, channels), F32),
            jax.ShapeDtypeStruct((3, rows, LANES), F32),
        ),
        in_specs=[in_vmem()] * 5,
        out_specs=(in_vmem(),) * 2,
        compiler_params=params(),
        cost_estimate=cost(2 * rows * rows * channels, 12 * rows * channels),
        name="value_mix",
    )(probs, before, own, inverse, square)


def normalize_kernel(count, panels, pieces, with_head, *refs):
    square_refs, refs = refs[:panels], refs[panels:]
    mixed_refs, refs = refs[:count], refs[count:]
    if with_head:
        head_ref, refs = refs[0], refs[1:]
    out_refs, (held_ref, sems) = refs[:count], refs[count:]
    rows = mixed_refs[0].shape[0]
    piece = rows // pieces
    copies = []
    for n in range(count):
        for m in range(pieces):
            at = slice(m * piece, (m + 1) * piece)
            square = square_refs[0][n, at, :]
            for ref in square_refs[1:]:
                square = square + ref[n, at, :]
            scale = lax.rsqrt(jnp.sum(square, axis=-1, keepdims=True) * (1.0 / CHANNELS) + 1e-06)
            value = mixed_refs[n][at, :]
            if with_head and n == 0 and m == 0:
                value = jnp.concatenate([head_ref[...], value[8:]], axis=0)
            held_ref[n, at, :] = (value * scale).astype(BF16)
            copy = pltpu.make_async_copy(
                held_ref.at[n, pl.ds(m * piece, piece)],
                out_refs[n].at[pl.ds(m * piece, piece)],
                sems.at[n, m],
            )
            copy.start()
            copies.append(copy)
    for copy in copies:
        copy.wait()


def normalize(squares, mixed, head=None, pieces=3):
    rows, channels = mixed[0].shape
    count = len(mixed)
    operands = (*squares, *mixed) + (() if head is None else (head,))
    return pl.pallas_call(
        functools.partial(normalize_kernel, count, len(squares), pieces, head is not None),
        out_shape=(jax.ShapeDtypeStruct((rows, channels), BF16),) * count,
        in_specs=[in_vmem()] * len(operands),
        out_specs=(pl.BlockSpec(memory_space=pl.ANY),) * count,
        scratch_shapes=[
            pltpu.VMEM((count, rows, channels), BF16),
            pltpu.SemaphoreType.DMA((count, pieces)),
        ],
        compiler_params=params(),
        cost_estimate=cost(4 * count * rows * channels, 6 * count * rows * channels),
        name="normalize",
    )(*operands)


def from_behind(value):
    count = lax.axis_size("ctx")
    return lax.ppermute(value, "ctx", [(source, source + 1) for source in range(count - 1)])


def of_panels(square):
    count = lax.axis_size("panel")
    return [square] + [
        lax.ppermute(square, "panel", [(n, (n + shift) % count) for n in range(count)])
        for shift in range(1, count)
    ]


def body(se, se_short, se_filter, mr, mr_short, raw, decay, queries, keys, values):
    decay = decay[None, :]
    key_before = from_behind(keys)
    packet = from_behind(pack(se, mr, se_short, mr_short, 4))
    own, z0, se_mix, se_square, taps, heads = own_part(
        mr, se, mr_short, se_short, raw, decay, se_filter, 4
    )
    value_before = from_behind(values)
    probs, attended, inverse = score(queries, keys, key_before, values, 4)
    packet, attended = lax.optimization_barrier((packet, attended))
    head, mr_mix, square = mix(
        packet, own, z0, se_square, taps, heads, mr_short, se_short, se_filter
    )
    attended, square = value_mix(probs, value_before, attended, inverse, square)
    return normalize(of_panels(square), (se_mix, mr_mix, attended), head)


def solution(mesh):
    placed = (
        P(None, "ctx", "panel"),
        P(None, None, "panel"),
        P(None, "panel"),
        P(None, "ctx", "panel"),
        P(None, None, "panel"),
        P(None, "panel"),
        P("panel"),
        P("ctx", "panel"),
        P("ctx", "panel"),
        P("ctx", "panel"),
    )
    return jax.shard_map(
        body,
        mesh=mesh,
        in_specs=placed,
        out_specs=(P("ctx", "panel"), P("ctx", "panel"), P("ctx", "panel")),
        check_vma=False,
    )
```

```python
import functools
import math

import jax
import jax.numpy as jnp
from jax import lax
from jax.experimental import pallas as pl
from jax.experimental.pallas import tpu as pltpu
from jax.sharding import PartitionSpec as P

CHANNELS = 4096
HD = 128
LSE = 7
MEDIUM_TAPS = 128
LANES = 128
F32 = jnp.float32
BF16 = jnp.bfloat16


def params(mebibytes=6):
    return pltpu.CompilerParams(vmem_limit_bytes=mebibytes * 1024 * 1024)


def in_vmem():
    return pl.BlockSpec(memory_space=pltpu.VMEM)


def cost(flops, nbytes, trans=0):
    return pl.CostEstimate(flops=int(flops), bytes_accessed=int(nbytes), transcendentals=int(trans))


def roll(value, shift):
    shift = shift % value.shape[0]
    return pltpu.roll(value, shift, 0) if shift else value


def row_is(rows, at):
    return lax.broadcasted_iota(jnp.int32, (rows, LANES), 0) == at


def features(u, front, taps):
    ext = jnp.concatenate([front, u], axis=0)
    total = taps[0] * ext
    for j in range(1, len(taps)):
        total = total + taps[j] * roll(ext, j)
    return total[8:]


def tap_rows(ref, stream, lanes):
    return [ref[stream, j : j + 1, lanes] for j in range(ref.shape[1])]


def lane_block(k):
    return pl.ds(pl.multiple_of(k * LANES, LANES), LANES)


def tap_tile(held_ref, j):
    return jnp.broadcast_to(held_ref[j : j + 1, :], (8, LANES))


def pack_kernel(
    per, mr_ref, se_ref, mr_short_ref, se_short_ref, out_ref, m_ref, tail_ref, mw_ref, sw_ref, last_ref, sems
):
    _, rows, channels = mr_ref.shape
    width = per * LANES
    chunk = MEDIUM_TAPS + 16
    nothing = jnp.zeros((8, LANES), F32)
    end = pl.ds(rows - 16, 16)
    copies = [
        pltpu.make_async_copy(mr_short_ref, mw_ref, sems.at[0]),
        pltpu.make_async_copy(se_short_ref, sw_ref, sems.at[1]),
        pltpu.make_async_copy(mr_ref.at[pl.ds(0, 1), end], tail_ref.at[pl.ds(0, 1)], sems.at[2]),
        pltpu.make_async_copy(se_ref.at[:, end], tail_ref.at[pl.ds(1, 3)], sems.at[3]),
    ]
    first = len(copies)
    for n in range(channels // width):
        at = pl.ds(n * width, width)
        copies.append(
            pltpu.make_async_copy(
                mr_ref.at[pl.ds(1, 2), :, at], m_ref.at[:, :, at], sems.at[first + n]
            )
        )
    for copy in copies:
        copy.start()
    for copy in copies[:first]:
        copy.wait()
    last_ref[...] = jnp.zeros_like(last_ref)

    def one(block):
        lanes = lane_block(block)
        m1 = m_ref[0, :, lanes].astype(F32)
        m2 = m_ref[1, :, lanes].astype(F32)
        z1 = features(m1, nothing, tap_rows(mw_ref, 1, lanes))
        z2 = features(m2, nothing, tap_rows(mw_ref, 2, lanes))
        product = (z1 * z2)[rows - MEDIUM_TAPS :]
        tail_m0 = tail_ref[0, :, lanes].astype(F32)[8:]
        tail_m1, tail_m2 = m1[rows - 8 :], m2[rows - 8 :]
        head = jnp.where(row_is(8, 0), roll(tail_m2, 2), product[:8])
        product = jnp.concatenate([head, product[8:]], axis=0)
        s0 = tail_ref[1, :, lanes].astype(F32)[8:]
        s1 = tail_ref[2, :, lanes].astype(F32)
        s2 = tail_ref[3, :, lanes].astype(F32)
        y1 = features(s1, nothing, tap_rows(sw_ref, 1, lanes))[8:]
        y2 = features(s2, nothing, tap_rows(sw_ref, 2, lanes))[8:]
        at = lax.broadcasted_iota(jnp.int32, (8, LANES), 0)
        x1 = jnp.where(at < 2, roll(s0, 2), y1 * y2)
        x2 = jnp.where(
            at < 2,
            roll(s1[8:], 2),
            jnp.where(at < 4, roll(s2[8:], 4), jnp.where(at < 6, roll(tail_m0, 6), tail_m1)),
        )
        start = pl.multiple_of(block * chunk, 16)
        out_ref[pl.ds(start, MEDIUM_TAPS), :] = product.astype(BF16)
        out_ref[pl.ds(start + MEDIUM_TAPS, 16), :] = jnp.concatenate([x1, x2], axis=0).astype(BF16)
        last_ref[pl.ds(block, 1), :] = tail_m2[7:8]

    for n in range(channels // width):
        copies[first + n].wait()
        pl.loop(n * per, (n + 1) * per)(one)

    out_ref[out_ref.shape[0] - 16 :, :] = last_ref[...].astype(BF16)


def pack(se, mr, se_short, mr_short, per):
    _, rows, channels = se.shape
    blocks = channels // LANES
    total = blocks * (MEDIUM_TAPS + 16) + 16
    return pl.pallas_call(
        functools.partial(pack_kernel, per),
        out_shape=jax.ShapeDtypeStruct((total, LANES), BF16),
        in_specs=[pl.BlockSpec(memory_space=pltpu.HBM)] * 4,
        out_specs=in_vmem(),
        scratch_shapes=[
            pltpu.VMEM((2, rows, channels), BF16),
            pltpu.VMEM((4, 16, channels), BF16),
            pltpu.VMEM(mr_short.shape, F32),
            pltpu.VMEM(se_short.shape, F32),
            pltpu.VMEM((16, LANES), F32),
            pltpu.SemaphoreType.DMA((4 + blocks // per,)),
        ],
        compiler_params=params(),
        cost_estimate=cost(20 * rows * channels, 6 * rows * channels),
        name="pack",
    )(*(pltpu.with_memory_space_constraint(x, pltpu.HBM) for x in (mr, se, mr_short, se_short)))


def own_kernel(
    per,
    m_hbm_ref,
    s_hbm_ref,
    mw_ref,
    sw_ref,
    raw_hbm_ref,
    decay_ref,
    filter_ref,
    own_ref,
    z0_ref,
    se_ref,
    square_ref,
    taps_ref,
    heads_ref,
    m_ref,
    s_ref,
    raw_ref,
    held_ref,
    sems,
):
    rows, channels = own_ref.shape
    tiles = rows // 8
    width = per * LANES
    nothing = jnp.zeros((8, LANES), F32)

    def fetch(n):
        at = pl.ds(pl.multiple_of(n * width, width), width)
        return (
            pltpu.make_async_copy(s_hbm_ref.at[:, :, at], s_ref.at[:, :, at], sems.at[0, n]),
            pltpu.make_async_copy(m_hbm_ref.at[:, :, at], m_ref.at[:, :, at], sems.at[1, n]),
            pltpu.make_async_copy(raw_hbm_ref.at[:, at], raw_ref.at[:, at], sems.at[2, n]),
        )

    for n in range(channels // width):
        for copy in fetch(n):
            copy.start()
    square_ref[...] = jnp.zeros_like(square_ref)

    @pl.loop(0, channels // LANES)
    def _(k):
        @pl.when(k % per == 0)
        def _():
            for copy in fetch(k // per):
                copy.wait()

        lanes = lane_block(k)
        u = [s_ref[n, :, lanes].astype(F32) for n in range(3)]
        for n in range(3):
            heads_ref[n, :, lanes] = u[n][:8]
        s = [features(u[n], nothing, tap_rows(sw_ref, n, lanes)) for n in range(3)]
        ext = jnp.concatenate([nothing, (s[1] * s[2]).astype(BF16).astype(F32)], axis=0)
        total = filter_ref[0:1, lanes] * ext
        for j in range(1, LSE):
            total = total + filter_ref[j : j + 1, lanes] * roll(ext, j)
        mixed = s[0] * total[8:]
        se_ref[:, lanes] = mixed
        square_ref[8:, :] += mixed[8:] * mixed[8:]

        steps = lax.broadcasted_iota(jnp.int32, (MEDIUM_TAPS, LANES), 0).astype(F32)
        taps = raw_ref[:, lanes] * jnp.exp(-decay_ref[0:1, lanes] * steps)
        held_ref[...] = taps
        taps_ref[:, lanes] = taps
        u = [m_ref[n, :, lanes].astype(F32) for n in range(3)]
        for n in range(3):
            heads_ref[3 + n, :, lanes] = u[n][:8]
        z = [features(u[n], nothing, tap_rows(mw_ref, n, lanes)) for n in range(3)]
        z0_ref[:, lanes] = z[0]
        product = (z[1] * z[2]).astype(BF16).astype(F32)
        at = lax.broadcasted_iota(jnp.int32, (8, LANES), 0)
        head = jnp.where(at < 2, 0.0, product[:8])
        ext = jnp.concatenate([nothing, head, product[8:]], axis=0)
        total = [None] * tiles
        for r in range(8):
            shifted = roll(ext, r)
            tap = [tap_tile(held_ref, 8 * a + r) for a in range(MEDIUM_TAPS // 8)]
            for i in range(tiles):
                for a in range(min(i + 1, MEDIUM_TAPS // 8)):
                    at_tile = 8 * (i - a + 1)
                    term = tap[a] * shifted[at_tile : at_tile + 8]
                    total[i] = term if total[i] is None else total[i] + term
        own_ref[:, lanes] = jnp.concatenate(total, axis=0)


def own_part(mr, se, mr_short, se_short, raw, decay, se_filter, per):
    _, rows, channels = mr.shape
    mixed = jax.ShapeDtypeStruct((rows, channels), F32)
    mr, se, raw = (pltpu.with_memory_space_constraint(x, pltpu.HBM) for x in (mr, se, raw))
    in_hbm = pl.BlockSpec(memory_space=pltpu.HBM)
    return pl.pallas_call(
        functools.partial(own_kernel, per),
        out_shape=(
            mixed,
            mixed,
            mixed,
            jax.ShapeDtypeStruct((rows, LANES), F32),
            jax.ShapeDtypeStruct((MEDIUM_TAPS, channels), F32),
            jax.ShapeDtypeStruct((6, 8, channels), F32),
        ),
        in_specs=[in_hbm] * 2 + [in_vmem()] * 2 + [in_hbm] + [in_vmem()] * 2,
        out_specs=(in_vmem(),) * 6,
        scratch_shapes=[
            pltpu.VMEM(mr.shape, BF16),
            pltpu.VMEM(se.shape, BF16),
            pltpu.VMEM((MEDIUM_TAPS, channels), F32),
            pltpu.VMEM((MEDIUM_TAPS, LANES), F32),
            pltpu.SemaphoreType.DMA((3, channels // (per * LANES))),
        ],
        compiler_params=params(10),
        cost_estimate=cost(180 * rows * channels, 24 * rows * channels),
        name="own_part",
    )(mr, se, mr_short, se_short, raw, decay, se_filter)


def mix_kernel(
    packet_ref,
    own_ref,
    z0_ref,
    se_square_ref,
    taps_ref,
    heads_ref,
    mw_ref,
    sw_ref,
    filter_ref,
    head_ref,
    mr_ref,
    square_ref,
    last_ref,
    held_ref,
):
    rows, channels = own_ref.shape
    tiles = rows // 8
    chunk = MEDIUM_TAPS + 16
    nothing = jnp.zeros((8, LANES), F32)
    last_ref[...] = packet_ref[packet_ref.shape[0] - 16 :, :].astype(F32)
    square_ref[0] = se_square_ref[...]
    square_ref[1] = jnp.zeros((rows, LANES), F32)

    @pl.loop(0, channels // LANES)
    def _(k):
        lanes = lane_block(k)
        start = pl.multiple_of(k * chunk, 16)
        before = packet_ref[pl.ds(start, MEDIUM_TAPS), :].astype(F32)
        x = packet_ref[pl.ds(start + MEDIUM_TAPS, 16), :].astype(F32)
        x1, x2 = x[:8], x[8:]
        last = last_ref[pl.ds(k, 1), :]

        fronts = (roll(x1, 6), roll(x2, 6), roll(x2, 4))
        s = [
            features(heads_ref[n, :, lanes], fronts[n], tap_rows(sw_ref, n, lanes))
            for n in range(3)
        ]
        ext = jnp.concatenate([x1, (s[1] * s[2]).astype(BF16).astype(F32)], axis=0)
        total = filter_ref[0:1, lanes] * ext
        for j in range(1, LSE):
            total = total + filter_ref[j : j + 1, lanes] * roll(ext, j)
        mixed = s[0] * total[8:]
        head_ref[:, lanes] = mixed
        square_ref[0, :8, :] += mixed * mixed

        taps = taps_ref[:, lanes]
        held_ref[...] = taps
        front2 = jnp.where(row_is(8, 7), last, roll(before[:8], 6))
        fronts = (roll(x2, 2), x2, front2)
        z = [
            features(heads_ref[3 + n, :, lanes], fronts[n], tap_rows(mw_ref, n, lanes))
            for n in range(3)
        ]
        first = (z[1] * z[2]).astype(BF16).astype(F32)
        padded = jnp.concatenate([taps, jnp.zeros((rows - MEDIUM_TAPS, LANES), F32)], axis=0)
        base = own_ref[:, lanes] + padded * first[0:1] + roll(padded, 1) * first[1:2]
        total = [base[8 * i : 8 * i + 8] for i in range(tiles)]
        ext = jnp.concatenate([before, nothing], axis=0)
        count = MEDIUM_TAPS // 8
        for r in range(8):
            shifted = roll(ext, r)
            tap = [tap_tile(held_ref, 8 * a + r) for a in range(count)]
            for i in range(count):
                for a in range(i if r else i + 1, count):
                    at_tile = 8 * (i - a + count)
                    total[i] = total[i] + tap[a] * shifted[at_tile : at_tile + 8]
        z0 = jnp.concatenate([z[0], z0_ref[8:, lanes]], axis=0)
        mixed = z0 * jnp.concatenate(total, axis=0)
        mr_ref[:, lanes] = mixed
        square_ref[1] += mixed * mixed


def mix(packet, own, z0, se_square, taps, heads, mr_short, se_short, se_filter):
    rows, channels = own.shape
    return pl.pallas_call(
        mix_kernel,
        out_shape=(
            jax.ShapeDtypeStruct((8, channels), F32),
            jax.ShapeDtypeStruct((rows, channels), F32),
            jax.ShapeDtypeStruct((2, rows, LANES), F32),
        ),
        in_specs=[in_vmem()] * 9,
        out_specs=(in_vmem(),) * 3,
        scratch_shapes=[pltpu.VMEM((16, LANES), F32), pltpu.VMEM((MEDIUM_TAPS, LANES), F32)],
        compiler_params=params(),
        cost_estimate=cost(140 * rows * channels, 16 * rows * channels),
        name="mix",
    )(packet, own, z0, se_square, taps, heads, mr_short, se_short, se_filter)


def score_kernel(per, q_ref, k_ref, before_ref, v_ref, probs_ref, out_ref, inverse_ref, bias_ref):
    rows, channels = q_ref.shape
    at = lax.broadcasted_iota(jnp.int32, (rows, 2 * rows), 0)
    key = lax.broadcasted_iota(jnp.int32, (rows, 2 * rows), 1)
    valid = (key <= at + rows) & ((key >= rows) | (lax.axis_index("ctx") > 0))
    bias_ref[...] = jnp.where(valid, 0.0, -1e30)
    factor = math.log2(math.e) / math.sqrt(HD)
    zeros, ones = jnp.zeros((rows, LANES), BF16), jnp.ones((rows, LANES), BF16)

    @pl.loop(0, channels // (LANES * per))
    def _(group):
        for n in range(per):
            head = group * per + n
            lanes = lane_block(head)
            both = jnp.concatenate([before_ref[:, lanes], k_ref[:, lanes]], axis=0)
            scores = lax.dot_general(
                q_ref[:, lanes], both, (((1,), (1,)), ((), ())), preferred_element_type=F32
            )
            scores = scores + bias_ref[...]
            top = jnp.max(scores, axis=-1, keepdims=True)
            probs = jnp.exp2((scores - top) * factor).astype(BF16)
            probs_ref[head] = probs[:, :rows]
            own = jnp.concatenate(
                [
                    jnp.concatenate([zeros, v_ref[:, lanes]], axis=0),
                    jnp.concatenate([ones, ones], axis=0),
                ],
                axis=1,
            )
            total = jnp.dot(probs, own, preferred_element_type=F32)
            inverse = 1.0 / total[:, LANES:]
            inverse_ref[:, lanes] = inverse
            out_ref[:, lanes] = total[:, :LANES] * inverse


def score(queries, keys, before, values, per):
    rows, channels = queries.shape
    flat = jax.ShapeDtypeStruct((rows, channels), F32)
    return pl.pallas_call(
        functools.partial(score_kernel, per),
        out_shape=(jax.ShapeDtypeStruct((channels // HD, rows, rows), BF16), flat, flat),
        in_specs=[in_vmem()] * 4,
        out_specs=(in_vmem(),) * 3,
        scratch_shapes=[pltpu.VMEM((rows, 2 * rows), F32)],
        compiler_params=params(),
        cost_estimate=cost(
            8 * rows * rows * channels, 14 * rows * channels, 4 * rows * rows * channels // HD
        ),
        name="score",
    )(queries, keys, before, values)


def value_kernel(probs_ref, before_ref, own_ref, inverse_ref, out_ref, square_ref):
    rows, channels = own_ref.shape
    square = jnp.zeros((rows, LANES), F32)
    for k in range(channels // LANES):
        lanes = slice(k * LANES, (k + 1) * LANES)
        total = own_ref[:, lanes] + inverse_ref[:, lanes] * jnp.dot(
            probs_ref[k], before_ref[:, lanes], preferred_element_type=F32
        )
        out_ref[:, lanes] = total
        square = square + total * total
    square_ref[0] = square


def value_mix(probs, before, own, inverse):
    rows, channels = own.shape
    return pl.pallas_call(
        value_kernel,
        out_shape=(
            jax.ShapeDtypeStruct((rows, channels), F32),
            jax.ShapeDtypeStruct((1, rows, LANES), F32),
        ),
        in_specs=[in_vmem()] * 4,
        out_specs=(in_vmem(),) * 2,
        compiler_params=params(),
        cost_estimate=cost(2 * rows * rows * channels, 12 * rows * channels),
        name="value_mix",
    )(probs, before, own, inverse)


def normalize_kernel(count, panels, pieces, with_head, *refs):
    square_refs, refs = refs[:panels], refs[panels:]
    mixed_refs, refs = refs[:count], refs[count:]
    if with_head:
        head_ref, refs = refs[0], refs[1:]
    out_refs, (held_ref, sems) = refs[:count], refs[count:]
    rows = mixed_refs[0].shape[0]
    piece = rows // pieces
    copies = []
    for n in range(count):
        square = square_refs[0][n]
        for ref in square_refs[1:]:
            square = square + ref[n]
        scale = lax.rsqrt(jnp.sum(square, axis=-1, keepdims=True) * (1.0 / CHANNELS) + 1e-06)
        for m in range(pieces):
            at = slice(m * piece, (m + 1) * piece)
            value = mixed_refs[n][at, :]
            if with_head and n == 0 and m == 0:
                value = jnp.concatenate([head_ref[...], value[8:]], axis=0)
            held_ref[n, at, :] = (value * scale[at]).astype(BF16)
            copy = pltpu.make_async_copy(
                held_ref.at[n, pl.ds(m * piece, piece)],
                out_refs[n].at[pl.ds(m * piece, piece)],
                sems.at[n, m],
            )
            copy.start()
            copies.append(copy)
    for copy in copies:
        copy.wait()


def normalize(squares, mixed, head=None, pieces=3):
    rows, channels = mixed[0].shape
    count = len(mixed)
    operands = (*squares, *mixed) + (() if head is None else (head,))
    return pl.pallas_call(
        functools.partial(normalize_kernel, count, len(squares), pieces, head is not None),
        out_shape=(jax.ShapeDtypeStruct((rows, channels), BF16),) * count,
        in_specs=[in_vmem()] * len(operands),
        out_specs=(pl.BlockSpec(memory_space=pl.ANY),) * count,
        scratch_shapes=[
            pltpu.VMEM((count, rows, channels), BF16),
            pltpu.SemaphoreType.DMA((count, pieces)),
        ],
        compiler_params=params(),
        cost_estimate=cost(4 * count * rows * channels, 6 * count * rows * channels),
        name="normalize",
    )(*operands)


def from_behind(value):
    count = lax.axis_size("ctx")
    return lax.ppermute(value, "ctx", [(source, source + 1) for source in range(count - 1)])


def of_panels(square):
    count = lax.axis_size("panel")
    return [square] + [
        lax.ppermute(square, "panel", [(n, (n + shift) % count) for n in range(count)])
        for shift in range(1, count)
    ]


def body(se, se_short, se_filter, mr, mr_short, raw, decay, queries, keys, values):
    decay = decay[None, :]
    key_before = from_behind(keys)
    packet = from_behind(pack(se, mr, se_short, mr_short, 4))
    own, z0, se_mix, se_square, taps, heads = own_part(
        mr, se, mr_short, se_short, raw, decay, se_filter, 4
    )
    values_later, own = lax.optimization_barrier((values, own))
    value_before = from_behind(values_later)
    probs, attended, inverse = score(queries, keys, key_before, values, 4)
    packet, attended = lax.optimization_barrier((packet, attended))
    head, mr_mix, square = mix(
        packet, own, z0, se_square, taps, heads, mr_short, se_short, se_filter
    )
    se_out, mr_out = normalize(of_panels(square), (se_mix, mr_mix), head)
    value_before, se_out, mr_out = lax.optimization_barrier((value_before, se_out, mr_out))
    attended, square = value_mix(probs, value_before, attended, inverse)
    (attn_out,) = normalize(of_panels(square), (attended,))
    return se_out, mr_out, attn_out


def solution(mesh):
    placed = (
        P(None, "ctx", "panel"),
        P(None, None, "panel"),
        P(None, "panel"),
        P(None, "ctx", "panel"),
        P(None, None, "panel"),
        P(None, "panel"),
        P("panel"),
        P("ctx", "panel"),
        P("ctx", "panel"),
        P("ctx", "panel"),
    )
    return jax.shard_map(
        body,
        mesh=mesh,
        in_specs=placed,
        out_specs=(P("ctx", "panel"), P("ctx", "panel"), P("ctx", "panel")),
        check_vma=False,
    )
```

```python
import functools
import math

import jax
import jax.numpy as jnp
from jax import lax
from jax.experimental import pallas as pl
from jax.experimental.pallas import tpu as pltpu
from jax.sharding import PartitionSpec as P

CHANNELS = 4096
HD = 128
LSE = 7
MEDIUM_TAPS = 128
LANES = 128
F32 = jnp.float32
BF16 = jnp.bfloat16


def params(mebibytes=6):
    return pltpu.CompilerParams(vmem_limit_bytes=mebibytes * 1024 * 1024)


def in_vmem():
    return pl.BlockSpec(memory_space=pltpu.VMEM)


def cost(flops, nbytes, trans=0):
    return pl.CostEstimate(flops=int(flops), bytes_accessed=int(nbytes), transcendentals=int(trans))


def roll(value, shift):
    shift = shift % value.shape[0]
    return pltpu.roll(value, shift, 0) if shift else value


def row_is(rows, at):
    return lax.broadcasted_iota(jnp.int32, (rows, LANES), 0) == at


def features(u, front, taps):
    ext = jnp.concatenate([front, u], axis=0)
    total = taps[0] * ext
    for j in range(1, len(taps)):
        total = total + taps[j] * roll(ext, j)
    return total[8:]


def tap_rows(ref, stream, lanes):
    return [ref[stream, j : j + 1, lanes] for j in range(ref.shape[1])]


def lane_block(k):
    return pl.ds(pl.multiple_of(k * LANES, LANES), LANES)


def tap_tile(held_ref, j):
    return jnp.broadcast_to(held_ref[j : j + 1, :], (8, LANES))


def pack_kernel(
    per, mr_ref, se_ref, mr_short_ref, se_short_ref, out_ref, m_ref, tail_ref, mw_ref, sw_ref, last_ref, sems
):
    _, rows, channels = mr_ref.shape
    width = per * LANES
    chunk = MEDIUM_TAPS + 16
    nothing = jnp.zeros((8, LANES), F32)
    end = pl.ds(rows - 16, 16)
    copies = [
        pltpu.make_async_copy(mr_short_ref, mw_ref, sems.at[0]),
        pltpu.make_async_copy(se_short_ref, sw_ref, sems.at[1]),
        pltpu.make_async_copy(mr_ref.at[pl.ds(0, 1), end], tail_ref.at[pl.ds(0, 1)], sems.at[2]),
        pltpu.make_async_copy(se_ref.at[:, end], tail_ref.at[pl.ds(1, 3)], sems.at[3]),
    ]
    first = len(copies)
    for n in range(channels // width):
        at = pl.ds(n * width, width)
        copies.append(
            pltpu.make_async_copy(
                mr_ref.at[pl.ds(1, 2), :, at], m_ref.at[:, :, at], sems.at[first + n]
            )
        )
    for copy in copies:
        copy.start()
    for copy in copies[:first]:
        copy.wait()
    last_ref[...] = jnp.zeros_like(last_ref)

    def one(block):
        lanes = lane_block(block)
        m1 = m_ref[0, :, lanes].astype(F32)
        m2 = m_ref[1, :, lanes].astype(F32)
        z1 = features(m1, nothing, tap_rows(mw_ref, 1, lanes))
        z2 = features(m2, nothing, tap_rows(mw_ref, 2, lanes))
        product = (z1 * z2)[rows - MEDIUM_TAPS :]
        tail_m0 = tail_ref[0, :, lanes].astype(F32)[8:]
        tail_m1, tail_m2 = m1[rows - 8 :], m2[rows - 8 :]
        head = jnp.where(row_is(8, 0), roll(tail_m2, 2), product[:8])
        product = jnp.concatenate([head, product[8:]], axis=0)
        s0 = tail_ref[1, :, lanes].astype(F32)[8:]
        s1 = tail_ref[2, :, lanes].astype(F32)
        s2 = tail_ref[3, :, lanes].astype(F32)
        y1 = features(s1, nothing, tap_rows(sw_ref, 1, lanes))[8:]
        y2 = features(s2, nothing, tap_rows(sw_ref, 2, lanes))[8:]
        at = lax.broadcasted_iota(jnp.int32, (8, LANES), 0)
        x1 = jnp.where(at < 2, roll(s0, 2), y1 * y2)
        x2 = jnp.where(
            at < 2,
            roll(s1[8:], 2),
            jnp.where(at < 4, roll(s2[8:], 4), jnp.where(at < 6, roll(tail_m0, 6), tail_m1)),
        )
        start = pl.multiple_of(block * chunk, 16)
        out_ref[pl.ds(start, MEDIUM_TAPS), :] = product.astype(BF16)
        out_ref[pl.ds(start + MEDIUM_TAPS, 16), :] = jnp.concatenate([x1, x2], axis=0).astype(BF16)
        last_ref[pl.ds(block, 1), :] = tail_m2[7:8]

    for n in range(channels // width):
        copies[first + n].wait()
        pl.loop(n * per, (n + 1) * per)(one)

    out_ref[out_ref.shape[0] - 16 :, :] = last_ref[...].astype(BF16)


def pack(se, mr, se_short, mr_short, per):
    _, rows, channels = se.shape
    blocks = channels // LANES
    total = blocks * (MEDIUM_TAPS + 16) + 16
    return pl.pallas_call(
        functools.partial(pack_kernel, per),
        out_shape=jax.ShapeDtypeStruct((total, LANES), BF16),
        in_specs=[pl.BlockSpec(memory_space=pltpu.HBM)] * 4,
        out_specs=in_vmem(),
        scratch_shapes=[
            pltpu.VMEM((2, rows, channels), BF16),
            pltpu.VMEM((4, 16, channels), BF16),
            pltpu.VMEM(mr_short.shape, F32),
            pltpu.VMEM(se_short.shape, F32),
            pltpu.VMEM((16, LANES), F32),
            pltpu.SemaphoreType.DMA((4 + blocks // per,)),
        ],
        compiler_params=params(),
        cost_estimate=cost(20 * rows * channels, 6 * rows * channels),
        name="pack",
    )(*(pltpu.with_memory_space_constraint(x, pltpu.HBM) for x in (mr, se, mr_short, se_short)))


def own_kernel(
    per,
    m_hbm_ref,
    s_hbm_ref,
    raw_hbm_ref,
    mw_hbm_ref,
    sw_hbm_ref,
    decay_hbm_ref,
    filter_hbm_ref,
    own_ref,
    z0_ref,
    se_ref,
    square_ref,
    taps_ref,
    heads_ref,
    mw_ref,
    sw_ref,
    filter_ref,
    m_ref,
    s_ref,
    raw_ref,
    decay_ref,
    held_ref,
    sems,
    small_sems,
):
    rows, channels = own_ref.shape
    tiles = rows // 8
    width = per * LANES
    nothing = jnp.zeros((8, LANES), F32)

    def fetch(n):
        at = pl.ds(pl.multiple_of(n * width, width), width)
        return (
            pltpu.make_async_copy(s_hbm_ref.at[:, :, at], s_ref.at[:, :, at], sems.at[0, n]),
            pltpu.make_async_copy(m_hbm_ref.at[:, :, at], m_ref.at[:, :, at], sems.at[1, n]),
            pltpu.make_async_copy(raw_hbm_ref.at[:, at], raw_ref.at[:, at], sems.at[2, n]),
        )

    small = [
        pltpu.make_async_copy(mw_hbm_ref, mw_ref, small_sems.at[0]),
        pltpu.make_async_copy(sw_hbm_ref, sw_ref, small_sems.at[1]),
        pltpu.make_async_copy(decay_hbm_ref, decay_ref, small_sems.at[2]),
        pltpu.make_async_copy(filter_hbm_ref, filter_ref, small_sems.at[3]),
    ]
    for copy in small:
        copy.start()
    for n in range(channels // width):
        for copy in fetch(n):
            copy.start()
    for copy in small:
        copy.wait()
    square_ref[...] = jnp.zeros_like(square_ref)

    @pl.loop(0, channels // LANES)
    def _(k):
        @pl.when(k % per == 0)
        def _():
            for copy in fetch(k // per):
                copy.wait()

        lanes = lane_block(k)
        u = [s_ref[n, :, lanes].astype(F32) for n in range(3)]
        for n in range(3):
            heads_ref[n, :, lanes] = u[n][:8]
        s = [features(u[n], nothing, tap_rows(sw_ref, n, lanes)) for n in range(3)]
        ext = jnp.concatenate([nothing, (s[1] * s[2]).astype(BF16).astype(F32)], axis=0)
        total = filter_ref[0:1, lanes] * ext
        for j in range(1, LSE):
            total = total + filter_ref[j : j + 1, lanes] * roll(ext, j)
        mixed = s[0] * total[8:]
        se_ref[:, lanes] = mixed
        square_ref[8:, :] += mixed[8:] * mixed[8:]

        steps = lax.broadcasted_iota(jnp.int32, (MEDIUM_TAPS, LANES), 0).astype(F32)
        taps = raw_ref[:, lanes] * jnp.exp(-decay_ref[0:1, lanes] * steps)
        held_ref[...] = taps
        taps_ref[:, lanes] = taps
        u = [m_ref[n, :, lanes].astype(F32) for n in range(3)]
        for n in range(3):
            heads_ref[3 + n, :, lanes] = u[n][:8]
        z = [features(u[n], nothing, tap_rows(mw_ref, n, lanes)) for n in range(3)]
        z0_ref[:, lanes] = z[0]
        product = (z[1] * z[2]).astype(BF16).astype(F32)
        at = lax.broadcasted_iota(jnp.int32, (8, LANES), 0)
        head = jnp.where(at < 2, 0.0, product[:8])
        ext = jnp.concatenate([nothing, head, product[8:]], axis=0)
        total = [None] * tiles
        for r in range(8):
            shifted = roll(ext, r)
            tap = [tap_tile(held_ref, 8 * a + r) for a in range(MEDIUM_TAPS // 8)]
            for i in range(tiles):
                for a in range(min(i + 1, MEDIUM_TAPS // 8)):
                    at_tile = 8 * (i - a + 1)
                    term = tap[a] * shifted[at_tile : at_tile + 8]
                    total[i] = term if total[i] is None else total[i] + term
        own_ref[:, lanes] = jnp.concatenate(total, axis=0)


def own_part(mr, se, mr_short, se_short, raw, decay, se_filter, per):
    _, rows, channels = mr.shape
    mixed = jax.ShapeDtypeStruct((rows, channels), F32)
    operands = (mr, se, raw, mr_short, se_short, decay, se_filter)
    return pl.pallas_call(
        functools.partial(own_kernel, per),
        out_shape=(
            mixed,
            mixed,
            mixed,
            jax.ShapeDtypeStruct((rows, LANES), F32),
            jax.ShapeDtypeStruct((MEDIUM_TAPS, channels), F32),
            jax.ShapeDtypeStruct((6, 8, channels), F32),
            jax.ShapeDtypeStruct(mr_short.shape, F32),
            jax.ShapeDtypeStruct(se_short.shape, F32),
            jax.ShapeDtypeStruct(se_filter.shape, F32),
        ),
        in_specs=[pl.BlockSpec(memory_space=pltpu.HBM)] * 7,
        out_specs=(in_vmem(),) * 9,
        scratch_shapes=[
            pltpu.VMEM(mr.shape, BF16),
            pltpu.VMEM(se.shape, BF16),
            pltpu.VMEM((MEDIUM_TAPS, channels), F32),
            pltpu.VMEM(decay.shape, F32),
            pltpu.VMEM((MEDIUM_TAPS, LANES), F32),
            pltpu.SemaphoreType.DMA((3, channels // (per * LANES))),
            pltpu.SemaphoreType.DMA((4,)),
        ],
        compiler_params=params(10),
        cost_estimate=cost(180 * rows * channels, 24 * rows * channels),
        name="own_part",
    )(*(pltpu.with_memory_space_constraint(x, pltpu.HBM) for x in operands))


def mix_kernel(
    packet_ref,
    own_ref,
    z0_ref,
    se_square_ref,
    taps_ref,
    heads_ref,
    mw_ref,
    sw_ref,
    filter_ref,
    head_ref,
    mr_ref,
    square_ref,
    last_ref,
    held_ref,
):
    rows, channels = own_ref.shape
    tiles = rows // 8
    chunk = MEDIUM_TAPS + 16
    nothing = jnp.zeros((8, LANES), F32)
    last_ref[...] = packet_ref[packet_ref.shape[0] - 16 :, :].astype(F32)
    square_ref[0] = se_square_ref[...]
    square_ref[1] = jnp.zeros((rows, LANES), F32)

    @pl.loop(0, channels // LANES)
    def _(k):
        lanes = lane_block(k)
        start = pl.multiple_of(k * chunk, 16)
        before = packet_ref[pl.ds(start, MEDIUM_TAPS), :].astype(F32)
        x = packet_ref[pl.ds(start + MEDIUM_TAPS, 16), :].astype(F32)
        x1, x2 = x[:8], x[8:]
        last = last_ref[pl.ds(k, 1), :]

        fronts = (roll(x1, 6), roll(x2, 6), roll(x2, 4))
        s = [
            features(heads_ref[n, :, lanes], fronts[n], tap_rows(sw_ref, n, lanes))
            for n in range(3)
        ]
        ext = jnp.concatenate([x1, (s[1] * s[2]).astype(BF16).astype(F32)], axis=0)
        total = filter_ref[0:1, lanes] * ext
        for j in range(1, LSE):
            total = total + filter_ref[j : j + 1, lanes] * roll(ext, j)
        mixed = s[0] * total[8:]
        head_ref[:, lanes] = mixed
        square_ref[0, :8, :] += mixed * mixed

        taps = taps_ref[:, lanes]
        held_ref[...] = taps
        front2 = jnp.where(row_is(8, 7), last, roll(before[:8], 6))
        fronts = (roll(x2, 2), x2, front2)
        z = [
            features(heads_ref[3 + n, :, lanes], fronts[n], tap_rows(mw_ref, n, lanes))
            for n in range(3)
        ]
        first = (z[1] * z[2]).astype(BF16).astype(F32)
        padded = jnp.concatenate([taps, jnp.zeros((rows - MEDIUM_TAPS, LANES), F32)], axis=0)
        base = own_ref[:, lanes] + padded * first[0:1] + roll(padded, 1) * first[1:2]
        total = [base[8 * i : 8 * i + 8] for i in range(tiles)]
        ext = jnp.concatenate([before, nothing], axis=0)
        count = MEDIUM_TAPS // 8
        for r in range(8):
            shifted = roll(ext, r)
            tap = [tap_tile(held_ref, 8 * a + r) for a in range(count)]
            for i in range(count):
                for a in range(i if r else i + 1, count):
                    at_tile = 8 * (i - a + count)
                    total[i] = total[i] + tap[a] * shifted[at_tile : at_tile + 8]
        z0 = jnp.concatenate([z[0], z0_ref[8:, lanes]], axis=0)
        mixed = z0 * jnp.concatenate(total, axis=0)
        mr_ref[:, lanes] = mixed
        square_ref[1] += mixed * mixed


def mix(packet, own, z0, se_square, taps, heads, mr_short, se_short, se_filter):
    rows, channels = own.shape
    return pl.pallas_call(
        mix_kernel,
        out_shape=(
            jax.ShapeDtypeStruct((8, channels), F32),
            jax.ShapeDtypeStruct((rows, channels), F32),
            jax.ShapeDtypeStruct((2, rows, LANES), F32),
        ),
        in_specs=[in_vmem()] * 9,
        out_specs=(in_vmem(),) * 3,
        scratch_shapes=[pltpu.VMEM((16, LANES), F32), pltpu.VMEM((MEDIUM_TAPS, LANES), F32)],
        compiler_params=params(),
        cost_estimate=cost(140 * rows * channels, 16 * rows * channels),
        name="mix",
    )(packet, own, z0, se_square, taps, heads, mr_short, se_short, se_filter)


def score_kernel(per, q_ref, k_ref, before_ref, v_ref, probs_ref, out_ref, inverse_ref, bias_ref):
    rows, channels = q_ref.shape
    at = lax.broadcasted_iota(jnp.int32, (rows, 2 * rows), 0)
    key = lax.broadcasted_iota(jnp.int32, (rows, 2 * rows), 1)
    valid = (key <= at + rows) & ((key >= rows) | (lax.axis_index("ctx") > 0))
    bias_ref[...] = jnp.where(valid, 0.0, -1e30)
    factor = math.log2(math.e) / math.sqrt(HD)
    zeros, ones = jnp.zeros((rows, LANES), BF16), jnp.ones((rows, LANES), BF16)

    @pl.loop(0, channels // (LANES * per))
    def _(group):
        for n in range(per):
            head = group * per + n
            lanes = lane_block(head)
            both = jnp.concatenate([before_ref[:, lanes], k_ref[:, lanes]], axis=0)
            scores = lax.dot_general(
                q_ref[:, lanes], both, (((1,), (1,)), ((), ())), preferred_element_type=F32
            )
            scores = scores + bias_ref[...]
            top = jnp.max(scores, axis=-1, keepdims=True)
            probs = jnp.exp2((scores - top) * factor).astype(BF16)
            probs_ref[head] = probs[:, :rows]
            own = jnp.concatenate(
                [
                    jnp.concatenate([zeros, v_ref[:, lanes]], axis=0),
                    jnp.concatenate([ones, ones], axis=0),
                ],
                axis=1,
            )
            total = jnp.dot(probs, own, preferred_element_type=F32)
            inverse = 1.0 / total[:, LANES:]
            inverse_ref[:, lanes] = inverse
            out_ref[:, lanes] = total[:, :LANES] * inverse


def score(queries, keys, before, values, per):
    rows, channels = queries.shape
    flat = jax.ShapeDtypeStruct((rows, channels), F32)
    return pl.pallas_call(
        functools.partial(score_kernel, per),
        out_shape=(jax.ShapeDtypeStruct((channels // HD, rows, rows), BF16), flat, flat),
        in_specs=[in_vmem()] * 4,
        out_specs=(in_vmem(),) * 3,
        scratch_shapes=[pltpu.VMEM((rows, 2 * rows), F32)],
        compiler_params=params(),
        cost_estimate=cost(
            8 * rows * rows * channels, 14 * rows * channels, 4 * rows * rows * channels // HD
        ),
        name="score",
    )(queries, keys, before, values)


def value_kernel(probs_ref, before_ref, own_ref, inverse_ref, out_ref, square_ref):
    rows, channels = own_ref.shape
    square = jnp.zeros((rows, LANES), F32)
    for k in range(channels // LANES):
        lanes = slice(k * LANES, (k + 1) * LANES)
        total = own_ref[:, lanes] + inverse_ref[:, lanes] * jnp.dot(
            probs_ref[k], before_ref[:, lanes], preferred_element_type=F32
        )
        out_ref[:, lanes] = total
        square = square + total * total
    square_ref[0] = square


def value_mix(probs, before, own, inverse):
    rows, channels = own.shape
    return pl.pallas_call(
        value_kernel,
        out_shape=(
            jax.ShapeDtypeStruct((rows, channels), F32),
            jax.ShapeDtypeStruct((1, rows, LANES), F32),
        ),
        in_specs=[in_vmem()] * 4,
        out_specs=(in_vmem(),) * 2,
        compiler_params=params(),
        cost_estimate=cost(2 * rows * rows * channels, 12 * rows * channels),
        name="value_mix",
    )(probs, before, own, inverse)


def normalize_kernel(count, panels, pieces, with_head, *refs):
    square_refs, refs = refs[:panels], refs[panels:]
    mixed_refs, refs = refs[:count], refs[count:]
    if with_head:
        head_ref, refs = refs[0], refs[1:]
    out_refs, (held_ref, sems) = refs[:count], refs[count:]
    rows = mixed_refs[0].shape[0]
    piece = rows // pieces
    copies = []
    for n in range(count):
        square = square_refs[0][n]
        for ref in square_refs[1:]:
            square = square + ref[n]
        scale = lax.rsqrt(jnp.sum(square, axis=-1, keepdims=True) * (1.0 / CHANNELS) + 1e-06)
        for m in range(pieces):
            at = slice(m * piece, (m + 1) * piece)
            value = mixed_refs[n][at, :]
            if with_head and n == 0 and m == 0:
                value = jnp.concatenate([head_ref[...], value[8:]], axis=0)
            held_ref[n, at, :] = (value * scale[at]).astype(BF16)
            copy = pltpu.make_async_copy(
                held_ref.at[n, pl.ds(m * piece, piece)],
                out_refs[n].at[pl.ds(m * piece, piece)],
                sems.at[n, m],
            )
            copy.start()
            copies.append(copy)
    for copy in copies:
        copy.wait()


def normalize(squares, mixed, head=None, pieces=3):
    rows, channels = mixed[0].shape
    count = len(mixed)
    operands = (*squares, *mixed) + (() if head is None else (head,))
    return pl.pallas_call(
        functools.partial(normalize_kernel, count, len(squares), pieces, head is not None),
        out_shape=(jax.ShapeDtypeStruct((rows, channels), BF16),) * count,
        in_specs=[in_vmem()] * len(operands),
        out_specs=(pl.BlockSpec(memory_space=pl.ANY),) * count,
        scratch_shapes=[
            pltpu.VMEM((count, rows, channels), BF16),
            pltpu.SemaphoreType.DMA((count, pieces)),
        ],
        compiler_params=params(),
        cost_estimate=cost(4 * count * rows * channels, 6 * count * rows * channels),
        name="normalize",
    )(*operands)


def from_behind(value):
    count = lax.axis_size("ctx")
    return lax.ppermute(value, "ctx", [(source, source + 1) for source in range(count - 1)])


def of_panels(square):
    count = lax.axis_size("panel")
    return [square] + [
        lax.ppermute(square, "panel", [(n, (n + shift) % count) for n in range(count)])
        for shift in range(1, count)
    ]


def body(se, se_short, se_filter, mr, mr_short, raw, decay, queries, keys, values):
    decay = decay[None, :]
    key_before = from_behind(keys)
    packet = from_behind(pack(se, mr, se_short, mr_short, 4))
    own, z0, se_mix, se_square, taps, heads, mr_taps, se_taps, filter_taps = own_part(
        mr, se, mr_short, se_short, raw, decay, se_filter, 4
    )
    values_later, own = lax.optimization_barrier((values, own))
    value_before = from_behind(values_later)
    probs, attended, inverse = score(queries, keys, key_before, values, 4)
    packet, attended = lax.optimization_barrier((packet, attended))
    head, mr_mix, square = mix(
        packet, own, z0, se_square, taps, heads, mr_taps, se_taps, filter_taps
    )
    se_out, mr_out = normalize(of_panels(square), (se_mix, mr_mix), head)
    value_before, se_out, mr_out = lax.optimization_barrier((value_before, se_out, mr_out))
    attended, square = value_mix(probs, value_before, attended, inverse)
    (attn_out,) = normalize(of_panels(square), (attended,))
    return se_out, mr_out, attn_out


def solution(mesh):
    placed = (
        P(None, "ctx", "panel"),
        P(None, None, "panel"),
        P(None, "panel"),
        P(None, "ctx", "panel"),
        P(None, None, "panel"),
        P(None, "panel"),
        P("panel"),
        P("ctx", "panel"),
        P("ctx", "panel"),
        P("ctx", "panel"),
    )
    return jax.shard_map(
        body,
        mesh=mesh,
        in_specs=placed,
        out_specs=(P("ctx", "panel"), P("ctx", "panel"), P("ctx", "panel")),
        check_vma=False,
    )
```

```python
import functools
import math

import jax
import jax.numpy as jnp
from jax import lax
from jax.experimental import pallas as pl
from jax.experimental.pallas import tpu as pltpu
from jax.sharding import PartitionSpec as P

CHANNELS = 4096
HD = 128
LSE = 7
MEDIUM_TAPS = 128
LANES = 128
F32 = jnp.float32
BF16 = jnp.bfloat16


def params(mebibytes=6):
    return pltpu.CompilerParams(vmem_limit_bytes=mebibytes * 1024 * 1024)


def in_vmem():
    return pl.BlockSpec(memory_space=pltpu.VMEM)


def cost(flops, nbytes, trans=0):
    return pl.CostEstimate(flops=int(flops), bytes_accessed=int(nbytes), transcendentals=int(trans))


def roll(value, shift):
    shift = shift % value.shape[0]
    return pltpu.roll(value, shift, 0) if shift else value


def row_is(rows, at):
    return lax.broadcasted_iota(jnp.int32, (rows, LANES), 0) == at


def features(u, front, taps):
    ext = jnp.concatenate([front, u], axis=0)
    total = taps[0] * ext
    for j in range(1, len(taps)):
        total = total + taps[j] * roll(ext, j)
    return total[8:]


def tap_rows(ref, stream, lanes):
    return [ref[stream, j : j + 1, lanes] for j in range(ref.shape[1])]


def lane_block(k):
    return pl.ds(pl.multiple_of(k * LANES, LANES), LANES)


def tap_tile(held_ref, j):
    return jnp.broadcast_to(held_ref[j : j + 1, :], (8, LANES))


def pack_kernel(
    per, mr_ref, se_ref, mr_short_ref, se_short_ref, out_ref, m_ref, tail_ref, mw_ref, sw_ref, last_ref, sems
):
    _, rows, channels = mr_ref.shape
    width = per * LANES
    chunk = MEDIUM_TAPS + 16
    nothing = jnp.zeros((8, LANES), F32)
    end = pl.ds(rows - 16, 16)
    copies = [
        pltpu.make_async_copy(mr_short_ref, mw_ref, sems.at[0]),
        pltpu.make_async_copy(se_short_ref, sw_ref, sems.at[1]),
        pltpu.make_async_copy(mr_ref.at[pl.ds(0, 1), end], tail_ref.at[pl.ds(0, 1)], sems.at[2]),
        pltpu.make_async_copy(se_ref.at[:, end], tail_ref.at[pl.ds(1, 3)], sems.at[3]),
    ]
    first = len(copies)
    for n in range(channels // width):
        at = pl.ds(n * width, width)
        copies.append(
            pltpu.make_async_copy(
                mr_ref.at[pl.ds(1, 2), :, at], m_ref.at[:, :, at], sems.at[first + n]
            )
        )
    for copy in copies:
        copy.start()
    for copy in copies[:first]:
        copy.wait()
    last_ref[...] = jnp.zeros_like(last_ref)

    def one(block):
        lanes = lane_block(block)
        m1 = m_ref[0, :, lanes].astype(F32)
        m2 = m_ref[1, :, lanes].astype(F32)
        z1 = features(m1, nothing, tap_rows(mw_ref, 1, lanes))
        z2 = features(m2, nothing, tap_rows(mw_ref, 2, lanes))
        product = (z1 * z2)[rows - MEDIUM_TAPS :]
        tail_m0 = tail_ref[0, :, lanes].astype(F32)[8:]
        tail_m1, tail_m2 = m1[rows - 8 :], m2[rows - 8 :]
        head = jnp.where(row_is(8, 0), roll(tail_m2, 2), product[:8])
        product = jnp.concatenate([head, product[8:]], axis=0)
        s0 = tail_ref[1, :, lanes].astype(F32)[8:]
        s1 = tail_ref[2, :, lanes].astype(F32)
        s2 = tail_ref[3, :, lanes].astype(F32)
        y1 = features(s1, nothing, tap_rows(sw_ref, 1, lanes))[8:]
        y2 = features(s2, nothing, tap_rows(sw_ref, 2, lanes))[8:]
        at = lax.broadcasted_iota(jnp.int32, (8, LANES), 0)
        x1 = jnp.where(at < 2, roll(s0, 2), y1 * y2)
        x2 = jnp.where(
            at < 2,
            roll(s1[8:], 2),
            jnp.where(at < 4, roll(s2[8:], 4), jnp.where(at < 6, roll(tail_m0, 6), tail_m1)),
        )
        start = pl.multiple_of(block * chunk, 16)
        out_ref[pl.ds(start, MEDIUM_TAPS), :] = product.astype(BF16)
        out_ref[pl.ds(start + MEDIUM_TAPS, 16), :] = jnp.concatenate([x1, x2], axis=0).astype(BF16)
        last_ref[pl.ds(block, 1), :] = tail_m2[7:8]

    for n in range(channels // width):
        copies[first + n].wait()
        pl.loop(n * per, (n + 1) * per)(one)

    out_ref[out_ref.shape[0] - 16 :, :] = last_ref[...].astype(BF16)


def pack(se, mr, se_short, mr_short, per):
    _, rows, channels = se.shape
    blocks = channels // LANES
    total = blocks * (MEDIUM_TAPS + 16) + 16
    return pl.pallas_call(
        functools.partial(pack_kernel, per),
        out_shape=jax.ShapeDtypeStruct((total, LANES), BF16),
        in_specs=[pl.BlockSpec(memory_space=pltpu.HBM)] * 4,
        out_specs=in_vmem(),
        scratch_shapes=[
            pltpu.VMEM((2, rows, channels), BF16),
            pltpu.VMEM((4, 16, channels), BF16),
            pltpu.VMEM(mr_short.shape, F32),
            pltpu.VMEM(se_short.shape, F32),
            pltpu.VMEM((16, LANES), F32),
            pltpu.SemaphoreType.DMA((4 + blocks // per,)),
        ],
        compiler_params=params(),
        cost_estimate=cost(20 * rows * channels, 6 * rows * channels),
        name="pack",
    )(*(pltpu.with_memory_space_constraint(x, pltpu.HBM) for x in (mr, se, mr_short, se_short)))


def own_kernel(
    per,
    m_hbm_ref,
    s_hbm_ref,
    raw_hbm_ref,
    mw_hbm_ref,
    sw_hbm_ref,
    decay_hbm_ref,
    filter_hbm_ref,
    own_ref,
    z0_ref,
    se_ref,
    square_ref,
    taps_ref,
    heads_ref,
    mw_ref,
    sw_ref,
    filter_ref,
    m_ref,
    s_ref,
    raw_ref,
    decay_ref,
    held_ref,
    sems,
    small_sems,
):
    rows, channels = own_ref.shape
    tiles = rows // 8
    width = per * LANES
    nothing = jnp.zeros((8, LANES), F32)

    def fetch(n):
        at = pl.ds(pl.multiple_of(n * width, width), width)
        return (
            pltpu.make_async_copy(s_hbm_ref.at[:, :, at], s_ref.at[:, :, at], sems.at[0, n]),
            pltpu.make_async_copy(m_hbm_ref.at[:, :, at], m_ref.at[:, :, at], sems.at[1, n]),
            pltpu.make_async_copy(raw_hbm_ref.at[:, at], raw_ref.at[:, at], sems.at[2, n]),
        )

    small = [
        pltpu.make_async_copy(mw_hbm_ref, mw_ref, small_sems.at[0]),
        pltpu.make_async_copy(sw_hbm_ref, sw_ref, small_sems.at[1]),
        pltpu.make_async_copy(decay_hbm_ref, decay_ref, small_sems.at[2]),
        pltpu.make_async_copy(filter_hbm_ref, filter_ref, small_sems.at[3]),
    ]
    for copy in small:
        copy.start()
    for n in range(channels // width):
        for copy in fetch(n):
            copy.start()
    for copy in small:
        copy.wait()
    square_ref[...] = jnp.zeros_like(square_ref)

    @pl.loop(0, channels // LANES)
    def _(k):
        @pl.when(k % per == 0)
        def _():
            for copy in fetch(k // per):
                copy.wait()

        lanes = lane_block(k)
        u = [s_ref[n, :, lanes].astype(F32) for n in range(3)]
        for n in range(3):
            heads_ref[n, :, lanes] = u[n][:8]
        s = [features(u[n], nothing, tap_rows(sw_ref, n, lanes)) for n in range(3)]
        ext = jnp.concatenate([nothing, (s[1] * s[2]).astype(BF16).astype(F32)], axis=0)
        total = filter_ref[0:1, lanes] * ext
        for j in range(1, LSE):
            total = total + filter_ref[j : j + 1, lanes] * roll(ext, j)
        mixed = s[0] * total[8:]
        se_ref[:, lanes] = mixed
        square_ref[8:, :] += mixed[8:] * mixed[8:]

        steps = lax.broadcasted_iota(jnp.int32, (MEDIUM_TAPS, LANES), 0).astype(F32)
        taps = raw_ref[:, lanes] * jnp.exp(-decay_ref[0:1, lanes] * steps)
        held_ref[...] = taps
        taps_ref[:, lanes] = taps
        u = [m_ref[n, :, lanes].astype(F32) for n in range(3)]
        for n in range(3):
            heads_ref[3 + n, :, lanes] = u[n][:8]
        z = [features(u[n], nothing, tap_rows(mw_ref, n, lanes)) for n in range(3)]
        z0_ref[:, lanes] = z[0]
        product = (z[1] * z[2]).astype(BF16).astype(F32)
        at = lax.broadcasted_iota(jnp.int32, (8, LANES), 0)
        head = jnp.where(at < 2, 0.0, product[:8])
        ext = jnp.concatenate([nothing, head, product[8:]], axis=0)
        total = [None] * tiles
        for r in range(8):
            shifted = roll(ext, r)
            tap = [tap_tile(held_ref, 8 * a + r) for a in range(MEDIUM_TAPS // 8)]
            for i in range(tiles):
                for a in range(min(i + 1, MEDIUM_TAPS // 8)):
                    at_tile = 8 * (i - a + 1)
                    term = tap[a] * shifted[at_tile : at_tile + 8]
                    total[i] = term if total[i] is None else total[i] + term
        own_ref[:, lanes] = jnp.concatenate(total, axis=0)


def own_part(mr, se, mr_short, se_short, raw, decay, se_filter, per):
    _, rows, channels = mr.shape
    mixed = jax.ShapeDtypeStruct((rows, channels), F32)
    operands = (mr, se, raw, mr_short, se_short, decay, se_filter)
    return pl.pallas_call(
        functools.partial(own_kernel, per),
        out_shape=(
            mixed,
            mixed,
            mixed,
            jax.ShapeDtypeStruct((rows, LANES), F32),
            jax.ShapeDtypeStruct((MEDIUM_TAPS, channels), F32),
            jax.ShapeDtypeStruct((6, 8, channels), F32),
            jax.ShapeDtypeStruct(mr_short.shape, F32),
            jax.ShapeDtypeStruct(se_short.shape, F32),
            jax.ShapeDtypeStruct(se_filter.shape, F32),
        ),
        in_specs=[pl.BlockSpec(memory_space=pltpu.HBM)] * 7,
        out_specs=(in_vmem(),) * 9,
        scratch_shapes=[
            pltpu.VMEM(mr.shape, BF16),
            pltpu.VMEM(se.shape, BF16),
            pltpu.VMEM((MEDIUM_TAPS, channels), F32),
            pltpu.VMEM(decay.shape, F32),
            pltpu.VMEM((MEDIUM_TAPS, LANES), F32),
            pltpu.SemaphoreType.DMA((3, channels // (per * LANES))),
            pltpu.SemaphoreType.DMA((4,)),
        ],
        compiler_params=params(10),
        cost_estimate=cost(180 * rows * channels, 24 * rows * channels),
        name="own_part",
    )(*(pltpu.with_memory_space_constraint(x, pltpu.HBM) for x in operands))


def mix_kernel(
    packet_ref,
    own_ref,
    z0_ref,
    se_square_ref,
    taps_ref,
    heads_ref,
    mw_ref,
    sw_ref,
    filter_ref,
    head_ref,
    mr_ref,
    square_ref,
    last_ref,
    held_ref,
):
    rows, channels = own_ref.shape
    tiles = rows // 8
    chunk = MEDIUM_TAPS + 16
    nothing = jnp.zeros((8, LANES), F32)
    last_ref[...] = packet_ref[packet_ref.shape[0] - 16 :, :].astype(F32)
    square_ref[0] = se_square_ref[...]
    square_ref[1] = jnp.zeros((rows, LANES), F32)

    @pl.loop(0, channels // LANES)
    def _(k):
        lanes = lane_block(k)
        start = pl.multiple_of(k * chunk, 16)
        before = packet_ref[pl.ds(start, MEDIUM_TAPS), :].astype(F32)
        x = packet_ref[pl.ds(start + MEDIUM_TAPS, 16), :].astype(F32)
        x1, x2 = x[:8], x[8:]
        last = last_ref[pl.ds(k, 1), :]

        fronts = (roll(x1, 6), roll(x2, 6), roll(x2, 4))
        s = [
            features(heads_ref[n, :, lanes], fronts[n], tap_rows(sw_ref, n, lanes))
            for n in range(3)
        ]
        ext = jnp.concatenate([x1, (s[1] * s[2]).astype(BF16).astype(F32)], axis=0)
        total = filter_ref[0:1, lanes] * ext
        for j in range(1, LSE):
            total = total + filter_ref[j : j + 1, lanes] * roll(ext, j)
        mixed = s[0] * total[8:]
        head_ref[:, lanes] = mixed
        square_ref[0, :8, :] += mixed * mixed

        taps = taps_ref[:, lanes]
        held_ref[...] = taps
        front2 = jnp.where(row_is(8, 7), last, roll(before[:8], 6))
        fronts = (roll(x2, 2), x2, front2)
        z = [
            features(heads_ref[3 + n, :, lanes], fronts[n], tap_rows(mw_ref, n, lanes))
            for n in range(3)
        ]
        first = (z[1] * z[2]).astype(BF16).astype(F32)
        padded = jnp.concatenate([taps, jnp.zeros((rows - MEDIUM_TAPS, LANES), F32)], axis=0)
        base = own_ref[:, lanes] + padded * first[0:1] + roll(padded, 1) * first[1:2]
        total = [base[8 * i : 8 * i + 8] for i in range(tiles)]
        ext = jnp.concatenate([before, nothing], axis=0)
        count = MEDIUM_TAPS // 8
        for r in range(8):
            shifted = roll(ext, r)
            tap = [tap_tile(held_ref, 8 * a + r) for a in range(count)]
            for i in range(count):
                for a in range(i if r else i + 1, count):
                    at_tile = 8 * (i - a + count)
                    total[i] = total[i] + tap[a] * shifted[at_tile : at_tile + 8]
        z0 = jnp.concatenate([z[0], z0_ref[8:, lanes]], axis=0)
        mixed = z0 * jnp.concatenate(total, axis=0)
        mr_ref[:, lanes] = mixed
        square_ref[1] += mixed * mixed


def mix(packet, own, z0, se_square, taps, heads, mr_short, se_short, se_filter):
    rows, channels = own.shape
    return pl.pallas_call(
        mix_kernel,
        out_shape=(
            jax.ShapeDtypeStruct((8, channels), F32),
            jax.ShapeDtypeStruct((rows, channels), F32),
            jax.ShapeDtypeStruct((2, rows, LANES), F32),
        ),
        in_specs=[in_vmem()] * 9,
        out_specs=(in_vmem(),) * 3,
        scratch_shapes=[pltpu.VMEM((16, LANES), F32), pltpu.VMEM((MEDIUM_TAPS, LANES), F32)],
        compiler_params=params(),
        cost_estimate=cost(140 * rows * channels, 16 * rows * channels),
        name="mix",
    )(packet, own, z0, se_square, taps, heads, mr_short, se_short, se_filter)


def score_kernel(per, q_ref, k_ref, before_ref, v_ref, probs_ref, out_ref, inverse_ref, bias_ref):
    rows, channels = q_ref.shape
    at = lax.broadcasted_iota(jnp.int32, (rows, 2 * rows), 0)
    key = lax.broadcasted_iota(jnp.int32, (rows, 2 * rows), 1)
    valid = (key <= at + rows) & ((key >= rows) | (lax.axis_index("ctx") > 0))
    bias_ref[...] = jnp.where(valid, 0.0, -1e30)
    factor = math.log2(math.e) / math.sqrt(HD)
    zeros, ones = jnp.zeros((rows, LANES), BF16), jnp.ones((rows, LANES), BF16)

    @pl.loop(0, channels // (LANES * per))
    def _(group):
        for n in range(per):
            head = group * per + n
            lanes = lane_block(head)
            both = jnp.concatenate([before_ref[:, lanes], k_ref[:, lanes]], axis=0)
            scores = lax.dot_general(
                q_ref[:, lanes], both, (((1,), (1,)), ((), ())), preferred_element_type=F32
            )
            scores = scores + bias_ref[...]
            top = jnp.max(scores, axis=-1, keepdims=True)
            probs = jnp.exp2((scores - top) * factor).astype(BF16)
            probs_ref[head] = probs[:, :rows]
            own = jnp.concatenate(
                [
                    jnp.concatenate([zeros, v_ref[:, lanes]], axis=0),
                    jnp.concatenate([ones, ones], axis=0),
                ],
                axis=1,
            )
            total = jnp.dot(probs, own, preferred_element_type=F32)
            inverse = 1.0 / total[:, LANES:]
            inverse_ref[:, lanes] = inverse
            out_ref[:, lanes] = total[:, :LANES] * inverse


def score(queries, keys, before, values, per):
    rows, channels = queries.shape
    flat = jax.ShapeDtypeStruct((rows, channels), F32)
    return pl.pallas_call(
        functools.partial(score_kernel, per),
        out_shape=(jax.ShapeDtypeStruct((channels // HD, rows, rows), BF16), flat, flat),
        in_specs=[in_vmem()] * 4,
        out_specs=(in_vmem(),) * 3,
        scratch_shapes=[pltpu.VMEM((rows, 2 * rows), F32)],
        compiler_params=params(),
        cost_estimate=cost(
            8 * rows * rows * channels, 14 * rows * channels, 4 * rows * rows * channels // HD
        ),
        name="score",
    )(queries, keys, before, values)


def value_kernel(probs_ref, before_ref, own_ref, inverse_ref, out_ref, square_ref):
    rows, channels = own_ref.shape
    square = jnp.zeros((rows, LANES), F32)
    for k in range(channels // LANES):
        lanes = slice(k * LANES, (k + 1) * LANES)
        total = own_ref[:, lanes] + inverse_ref[:, lanes] * jnp.dot(
            probs_ref[k], before_ref[:, lanes], preferred_element_type=F32
        )
        out_ref[:, lanes] = total
        square = square + total * total
    for n in range(square_ref.shape[0]):
        square_ref[n] = square


def value_mix(probs, before, own, inverse, panels):
    rows, channels = own.shape
    return pl.pallas_call(
        value_kernel,
        out_shape=(
            jax.ShapeDtypeStruct((rows, channels), F32),
            jax.ShapeDtypeStruct((panels, rows, LANES), F32),
        ),
        in_specs=[in_vmem()] * 4,
        out_specs=(in_vmem(),) * 2,
        compiler_params=params(),
        cost_estimate=cost(2 * rows * rows * channels, 12 * rows * channels),
        name="value_mix",
    )(probs, before, own, inverse)


def normalize_kernel(count, panels, terms, pieces, with_head, *refs):
    square_refs, refs = refs[:panels], refs[panels:]
    mixed_refs, refs = refs[:count], refs[count:]
    if with_head:
        head_ref, refs = refs[0], refs[1:]
    out_refs, (held_ref, sems) = refs[:count], refs[count:]
    rows = mixed_refs[0].shape[0]
    piece = rows // pieces
    copies = []
    for n in range(count):
        square = sum(ref[n + m] for ref in square_refs for m in range(terms))
        scale = lax.rsqrt(jnp.sum(square, axis=-1, keepdims=True) * (1.0 / CHANNELS) + 1e-06)
        for m in range(pieces):
            at = slice(m * piece, (m + 1) * piece)
            value = mixed_refs[n][at, :]
            if with_head and n == 0 and m == 0:
                value = jnp.concatenate([head_ref[...], value[8:]], axis=0)
            held_ref[n, at, :] = (value * scale[at]).astype(BF16)
            copy = pltpu.make_async_copy(
                held_ref.at[n, pl.ds(m * piece, piece)],
                out_refs[n].at[pl.ds(m * piece, piece)],
                sems.at[n, m],
            )
            copy.start()
            copies.append(copy)
    for copy in copies:
        copy.wait()


def normalize(squares, mixed, head=None, pieces=3, terms=1):
    rows, channels = mixed[0].shape
    count = len(mixed)
    operands = (*squares, *mixed) + (() if head is None else (head,))
    return pl.pallas_call(
        functools.partial(
            normalize_kernel, count, len(squares), terms, pieces, head is not None
        ),
        out_shape=(jax.ShapeDtypeStruct((rows, channels), BF16),) * count,
        in_specs=[in_vmem()] * len(operands),
        out_specs=(pl.BlockSpec(memory_space=pl.ANY),) * count,
        scratch_shapes=[
            pltpu.VMEM((count, rows, channels), BF16),
            pltpu.SemaphoreType.DMA((count, pieces)),
        ],
        compiler_params=params(),
        cost_estimate=cost(4 * count * rows * channels, 6 * count * rows * channels),
        name="normalize",
    )(*operands)


def from_behind(value):
    count = lax.axis_size("ctx")
    return lax.ppermute(value, "ctx", [(source, source + 1) for source in range(count - 1)])


def of_panels(square):
    count = lax.axis_size("panel")
    return [square] + [
        lax.ppermute(square, "panel", [(n, (n + shift) % count) for n in range(count)])
        for shift in range(1, count)
    ]


def body(se, se_short, se_filter, mr, mr_short, raw, decay, queries, keys, values):
    decay = decay[None, :]
    key_before = from_behind(keys)
    packet = from_behind(pack(se, mr, se_short, mr_short, 4))
    own, z0, se_mix, se_square, taps, heads, mr_taps, se_taps, filter_taps = own_part(
        mr, se, mr_short, se_short, raw, decay, se_filter, 4
    )
    values_later, own = lax.optimization_barrier((values, own))
    value_before = from_behind(values_later)
    probs, attended, inverse = score(queries, keys, key_before, values, 4)
    packet, attended = lax.optimization_barrier((packet, attended))
    head, mr_mix, square = mix(
        packet, own, z0, se_square, taps, heads, mr_taps, se_taps, filter_taps
    )
    se_out, mr_out = normalize(of_panels(square), (se_mix, mr_mix), head)
    value_before, se_out, mr_out = lax.optimization_barrier((value_before, se_out, mr_out))
    panels = lax.axis_size("panel")
    attended, square = value_mix(probs, value_before, attended, inverse, panels)
    square = lax.all_to_all(square, "panel", 0, 0, tiled=True)
    (attn_out,) = normalize([square], (attended,), terms=panels)
    return se_out, mr_out, attn_out


def solution(mesh):
    placed = (
        P(None, "ctx", "panel"),
        P(None, None, "panel"),
        P(None, "panel"),
        P(None, "ctx", "panel"),
        P(None, None, "panel"),
        P(None, "panel"),
        P("panel"),
        P("ctx", "panel"),
        P("ctx", "panel"),
        P("ctx", "panel"),
    )
    return jax.shard_map(
        body,
        mesh=mesh,
        in_specs=placed,
        out_specs=(P("ctx", "panel"), P("ctx", "panel"), P("ctx", "panel")),
        check_vma=False,
    )
```

```python
import functools
import math

import jax
import jax.numpy as jnp
from jax import lax
from jax.experimental import pallas as pl
from jax.experimental.pallas import tpu as pltpu
from jax.sharding import PartitionSpec as P

CHANNELS = 4096
HD = 128
LSE = 7
MEDIUM_TAPS = 128
LANES = 128
F32 = jnp.float32
BF16 = jnp.bfloat16


def params(mebibytes=6):
    return pltpu.CompilerParams(vmem_limit_bytes=mebibytes * 1024 * 1024)


def in_vmem():
    return pl.BlockSpec(memory_space=pltpu.VMEM)


def cost(flops, nbytes, trans=0):
    return pl.CostEstimate(flops=int(flops), bytes_accessed=int(nbytes), transcendentals=int(trans))


def roll(value, shift):
    shift = shift % value.shape[0]
    return pltpu.roll(value, shift, 0) if shift else value


def row_is(rows, at):
    return lax.broadcasted_iota(jnp.int32, (rows, LANES), 0) == at


def features(u, front, taps):
    ext = jnp.concatenate([front, u], axis=0)
    total = taps[0] * ext
    for j in range(1, len(taps)):
        total = total + taps[j] * roll(ext, j)
    return total[8:]


def tap_rows(ref, stream, lanes):
    return [ref[stream, j : j + 1, lanes] for j in range(ref.shape[1])]


def lane_block(k):
    return pl.ds(pl.multiple_of(k * LANES, LANES), LANES)


def tap_tile(held_ref, j):
    return jnp.broadcast_to(held_ref[j : j + 1, :], (8, LANES))


def pack_kernel(
    per,
    mr_ref,
    se_ref,
    mr_short_ref,
    se_short_ref,
    decay_hbm_ref,
    filter_hbm_ref,
    values_ref,
    out_ref,
    mw_ref,
    sw_ref,
    decay_ref,
    filter_ref,
    most_ref,
    rest_ref,
    m_ref,
    tail_ref,
    last_ref,
    sems,
    late_sems,
):
    _, rows, channels = mr_ref.shape
    width = per * LANES
    chunk = MEDIUM_TAPS + 16
    nothing = jnp.zeros((8, LANES), F32)
    end = pl.ds(rows - 16, 16)
    copies = [
        pltpu.make_async_copy(mr_short_ref, mw_ref, sems.at[0]),
        pltpu.make_async_copy(se_short_ref, sw_ref, sems.at[1]),
        pltpu.make_async_copy(mr_ref.at[pl.ds(0, 1), end], tail_ref.at[pl.ds(0, 1)], sems.at[2]),
        pltpu.make_async_copy(se_ref.at[:, end], tail_ref.at[pl.ds(1, 3)], sems.at[3]),
    ]
    first = len(copies)
    for n in range(channels // width):
        at = pl.ds(n * width, width)
        copies.append(
            pltpu.make_async_copy(
                mr_ref.at[pl.ds(1, 2), :, at], m_ref.at[:, :, at], sems.at[first + n]
            )
        )
    most = most_ref.shape[1]
    late = [
        pltpu.make_async_copy(values_ref.at[:, pl.ds(0, most)], most_ref, late_sems.at[0]),
        pltpu.make_async_copy(
            values_ref.at[:, pl.ds(most, channels - most)], rest_ref, late_sems.at[1]
        ),
        pltpu.make_async_copy(decay_hbm_ref, decay_ref, late_sems.at[2]),
        pltpu.make_async_copy(filter_hbm_ref, filter_ref, late_sems.at[3]),
    ]
    for copy in copies + late:
        copy.start()
    for copy in copies[:first]:
        copy.wait()
    last_ref[...] = jnp.zeros_like(last_ref)

    def one(block):
        lanes = lane_block(block)
        m1 = m_ref[0, :, lanes].astype(F32)
        m2 = m_ref[1, :, lanes].astype(F32)
        z1 = features(m1, nothing, tap_rows(mw_ref, 1, lanes))
        z2 = features(m2, nothing, tap_rows(mw_ref, 2, lanes))
        product = (z1 * z2)[rows - MEDIUM_TAPS :]
        tail_m0 = tail_ref[0, :, lanes].astype(F32)[8:]
        tail_m1, tail_m2 = m1[rows - 8 :], m2[rows - 8 :]
        head = jnp.where(row_is(8, 0), roll(tail_m2, 2), product[:8])
        product = jnp.concatenate([head, product[8:]], axis=0)
        s0 = tail_ref[1, :, lanes].astype(F32)[8:]
        s1 = tail_ref[2, :, lanes].astype(F32)
        s2 = tail_ref[3, :, lanes].astype(F32)
        y1 = features(s1, nothing, tap_rows(sw_ref, 1, lanes))[8:]
        y2 = features(s2, nothing, tap_rows(sw_ref, 2, lanes))[8:]
        at = lax.broadcasted_iota(jnp.int32, (8, LANES), 0)
        x1 = jnp.where(at < 2, roll(s0, 2), y1 * y2)
        x2 = jnp.where(
            at < 2,
            roll(s1[8:], 2),
            jnp.where(at < 4, roll(s2[8:], 4), jnp.where(at < 6, roll(tail_m0, 6), tail_m1)),
        )
        start = pl.multiple_of(block * chunk, 16)
        out_ref[pl.ds(start, MEDIUM_TAPS), :] = product.astype(BF16)
        out_ref[pl.ds(start + MEDIUM_TAPS, 16), :] = jnp.concatenate([x1, x2], axis=0).astype(BF16)
        last_ref[pl.ds(block, 1), :] = tail_m2[7:8]

    for n in range(channels // width):
        copies[first + n].wait()
        pl.loop(n * per, (n + 1) * per)(one)

    out_ref[out_ref.shape[0] - 16 :, :] = last_ref[...].astype(BF16)
    for copy in late:
        copy.wait()


def pack(se, mr, se_short, mr_short, decay, se_filter, values, last_heads, per):
    _, rows, channels = se.shape
    blocks = channels // LANES
    total = blocks * (MEDIUM_TAPS + 16) + 16
    rest = last_heads * HD
    operands = (mr, se, mr_short, se_short, decay, se_filter, values)
    return pl.pallas_call(
        functools.partial(pack_kernel, per),
        out_shape=(
            jax.ShapeDtypeStruct((total, LANES), BF16),
            jax.ShapeDtypeStruct(mr_short.shape, F32),
            jax.ShapeDtypeStruct(se_short.shape, F32),
            jax.ShapeDtypeStruct(decay.shape, F32),
            jax.ShapeDtypeStruct(se_filter.shape, F32),
            jax.ShapeDtypeStruct((rows, channels - rest), BF16),
            jax.ShapeDtypeStruct((rows, rest), BF16),
        ),
        in_specs=[pl.BlockSpec(memory_space=pltpu.HBM)] * 7,
        out_specs=(in_vmem(),) * 7,
        scratch_shapes=[
            pltpu.VMEM((2, rows, channels), BF16),
            pltpu.VMEM((4, 16, channels), BF16),
            pltpu.VMEM((16, LANES), F32),
            pltpu.SemaphoreType.DMA((4 + blocks // per,)),
            pltpu.SemaphoreType.DMA((4,)),
        ],
        compiler_params=params(),
        cost_estimate=cost(20 * rows * channels, 10 * rows * channels),
        name="pack",
    )(*(pltpu.with_memory_space_constraint(x, pltpu.HBM) for x in operands))


def own_kernel(
    per,
    m_hbm_ref,
    s_hbm_ref,
    raw_hbm_ref,
    mw_ref,
    sw_ref,
    decay_ref,
    filter_ref,
    own_ref,
    z0_ref,
    se_ref,
    square_ref,
    taps_ref,
    heads_ref,
    m_ref,
    s_ref,
    raw_ref,
    held_ref,
    sems,
):
    rows, channels = own_ref.shape
    tiles = rows // 8
    width = per * LANES
    nothing = jnp.zeros((8, LANES), F32)

    def fetch(n):
        at = pl.ds(pl.multiple_of(n * width, width), width)
        return (
            pltpu.make_async_copy(s_hbm_ref.at[:, :, at], s_ref.at[:, :, at], sems.at[0, n]),
            pltpu.make_async_copy(m_hbm_ref.at[:, :, at], m_ref.at[:, :, at], sems.at[1, n]),
            pltpu.make_async_copy(raw_hbm_ref.at[:, at], raw_ref.at[:, at], sems.at[2, n]),
        )

    for n in range(channels // width):
        for copy in fetch(n):
            copy.start()
    square_ref[...] = jnp.zeros_like(square_ref)

    @pl.loop(0, channels // LANES)
    def _(k):
        @pl.when(k % per == 0)
        def _():
            for copy in fetch(k // per):
                copy.wait()

        lanes = lane_block(k)
        u = [s_ref[n, :, lanes].astype(F32) for n in range(3)]
        for n in range(3):
            heads_ref[n, :, lanes] = u[n][:8]
        s = [features(u[n], nothing, tap_rows(sw_ref, n, lanes)) for n in range(3)]
        ext = jnp.concatenate([nothing, (s[1] * s[2]).astype(BF16).astype(F32)], axis=0)
        total = filter_ref[0:1, lanes] * ext
        for j in range(1, LSE):
            total = total + filter_ref[j : j + 1, lanes] * roll(ext, j)
        mixed = s[0] * total[8:]
        se_ref[:, lanes] = mixed
        square_ref[8:, :] += mixed[8:] * mixed[8:]

        steps = lax.broadcasted_iota(jnp.int32, (MEDIUM_TAPS, LANES), 0).astype(F32)
        taps = raw_ref[:, lanes] * jnp.exp(-decay_ref[0:1, lanes] * steps)
        held_ref[...] = taps
        taps_ref[:, lanes] = taps
        u = [m_ref[n, :, lanes].astype(F32) for n in range(3)]
        for n in range(3):
            heads_ref[3 + n, :, lanes] = u[n][:8]
        z = [features(u[n], nothing, tap_rows(mw_ref, n, lanes)) for n in range(3)]
        z0_ref[:, lanes] = z[0]
        product = (z[1] * z[2]).astype(BF16).astype(F32)
        at = lax.broadcasted_iota(jnp.int32, (8, LANES), 0)
        head = jnp.where(at < 2, 0.0, product[:8])
        ext = jnp.concatenate([nothing, head, product[8:]], axis=0)
        total = [None] * tiles
        for r in range(8):
            shifted = roll(ext, r)
            tap = [tap_tile(held_ref, 8 * a + r) for a in range(MEDIUM_TAPS // 8)]
            for i in range(tiles):
                for a in range(min(i + 1, MEDIUM_TAPS // 8)):
                    at_tile = 8 * (i - a + 1)
                    term = tap[a] * shifted[at_tile : at_tile + 8]
                    total[i] = term if total[i] is None else total[i] + term
        own_ref[:, lanes] = jnp.concatenate(total, axis=0)


def own_part(mr, se, mr_short, se_short, raw, decay, se_filter, per):
    _, rows, channels = mr.shape
    mixed = jax.ShapeDtypeStruct((rows, channels), F32)
    mr, se, raw = (pltpu.with_memory_space_constraint(x, pltpu.HBM) for x in (mr, se, raw))
    return pl.pallas_call(
        functools.partial(own_kernel, per),
        out_shape=(
            mixed,
            mixed,
            mixed,
            jax.ShapeDtypeStruct((rows, LANES), F32),
            jax.ShapeDtypeStruct((MEDIUM_TAPS, channels), F32),
            jax.ShapeDtypeStruct((6, 8, channels), F32),
        ),
        in_specs=[pl.BlockSpec(memory_space=pltpu.HBM)] * 3 + [in_vmem()] * 4,
        out_specs=(in_vmem(),) * 6,
        scratch_shapes=[
            pltpu.VMEM(mr.shape, BF16),
            pltpu.VMEM(se.shape, BF16),
            pltpu.VMEM((MEDIUM_TAPS, channels), F32),
            pltpu.VMEM((MEDIUM_TAPS, LANES), F32),
            pltpu.SemaphoreType.DMA((3, channels // (per * LANES))),
        ],
        compiler_params=params(10),
        cost_estimate=cost(180 * rows * channels, 24 * rows * channels),
        name="own_part",
    )(mr, se, raw, mr_short, se_short, decay, se_filter)


def mix_kernel(
    packet_ref,
    own_ref,
    z0_ref,
    se_square_ref,
    taps_ref,
    heads_ref,
    mw_ref,
    sw_ref,
    filter_ref,
    head_ref,
    mr_ref,
    square_ref,
    last_ref,
    held_ref,
):
    rows, channels = own_ref.shape
    tiles = rows // 8
    chunk = MEDIUM_TAPS + 16
    nothing = jnp.zeros((8, LANES), F32)
    last_ref[...] = packet_ref[packet_ref.shape[0] - 16 :, :].astype(F32)
    square_ref[0] = se_square_ref[...]
    square_ref[1] = jnp.zeros((rows, LANES), F32)

    @pl.loop(0, channels // LANES)
    def _(k):
        lanes = lane_block(k)
        start = pl.multiple_of(k * chunk, 16)
        before = packet_ref[pl.ds(start, MEDIUM_TAPS), :].astype(F32)
        x = packet_ref[pl.ds(start + MEDIUM_TAPS, 16), :].astype(F32)
        x1, x2 = x[:8], x[8:]
        last = last_ref[pl.ds(k, 1), :]

        fronts = (roll(x1, 6), roll(x2, 6), roll(x2, 4))
        s = [
            features(heads_ref[n, :, lanes], fronts[n], tap_rows(sw_ref, n, lanes))
            for n in range(3)
        ]
        ext = jnp.concatenate([x1, (s[1] * s[2]).astype(BF16).astype(F32)], axis=0)
        total = filter_ref[0:1, lanes] * ext
        for j in range(1, LSE):
            total = total + filter_ref[j : j + 1, lanes] * roll(ext, j)
        mixed = s[0] * total[8:]
        head_ref[:, lanes] = mixed
        square_ref[0, :8, :] += mixed * mixed

        taps = taps_ref[:, lanes]
        held_ref[...] = taps
        front2 = jnp.where(row_is(8, 7), last, roll(before[:8], 6))
        fronts = (roll(x2, 2), x2, front2)
        z = [
            features(heads_ref[3 + n, :, lanes], fronts[n], tap_rows(mw_ref, n, lanes))
            for n in range(3)
        ]
        first = (z[1] * z[2]).astype(BF16).astype(F32)
        padded = jnp.concatenate([taps, jnp.zeros((rows - MEDIUM_TAPS, LANES), F32)], axis=0)
        base = own_ref[:, lanes] + padded * first[0:1] + roll(padded, 1) * first[1:2]
        total = [base[8 * i : 8 * i + 8] for i in range(tiles)]
        ext = jnp.concatenate([before, nothing], axis=0)
        count = MEDIUM_TAPS // 8
        for r in range(8):
            shifted = roll(ext, r)
            tap = [tap_tile(held_ref, 8 * a + r) for a in range(count)]
            for i in range(count):
                for a in range(i if r else i + 1, count):
                    at_tile = 8 * (i - a + count)
                    total[i] = total[i] + tap[a] * shifted[at_tile : at_tile + 8]
        z0 = jnp.concatenate([z[0], z0_ref[8:, lanes]], axis=0)
        mixed = z0 * jnp.concatenate(total, axis=0)
        mr_ref[:, lanes] = mixed
        square_ref[1] += mixed * mixed


def mix(packet, own, z0, se_square, taps, heads, mr_short, se_short, se_filter):
    rows, channels = own.shape
    return pl.pallas_call(
        mix_kernel,
        out_shape=(
            jax.ShapeDtypeStruct((8, channels), F32),
            jax.ShapeDtypeStruct((rows, channels), F32),
            jax.ShapeDtypeStruct((2, rows, LANES), F32),
        ),
        in_specs=[in_vmem()] * 9,
        out_specs=(in_vmem(),) * 3,
        scratch_shapes=[pltpu.VMEM((16, LANES), F32), pltpu.VMEM((MEDIUM_TAPS, LANES), F32)],
        compiler_params=params(),
        cost_estimate=cost(1, 1),
        name="mix",
    )(packet, own, z0, se_square, taps, heads, mr_short, se_short, se_filter)


def score_kernel(
    per, q_ref, k_ref, before_ref, v_ref, probs_ref, out_ref, inverse_ref, square_ref, bias_ref
):
    rows, channels = q_ref.shape
    at = lax.broadcasted_iota(jnp.int32, (rows, 2 * rows), 0)
    key = lax.broadcasted_iota(jnp.int32, (rows, 2 * rows), 1)
    valid = (key <= at + rows) & ((key >= rows) | (lax.axis_index("ctx") > 0))
    bias_ref[...] = jnp.where(valid, 0.0, -1e30)
    square_ref[...] = jnp.zeros_like(square_ref)
    factor = math.log2(math.e) / math.sqrt(HD)
    zeros, ones = jnp.zeros((rows, LANES), BF16), jnp.ones((rows, LANES), BF16)

    @pl.loop(0, channels // (LANES * per))
    def _(group):
        for n in range(per):
            head = group * per + n
            lanes = lane_block(head)
            both = jnp.concatenate([before_ref[:, lanes], k_ref[:, lanes]], axis=0)
            scores = lax.dot_general(
                q_ref[:, lanes], both, (((1,), (1,)), ((), ())), preferred_element_type=F32
            )
            scores = scores + bias_ref[...]
            top = jnp.max(scores, axis=-1, keepdims=True)
            probs = jnp.exp2((scores - top) * factor).astype(BF16)
            probs_ref[head] = probs[:, :rows]
            own = jnp.concatenate(
                [
                    jnp.concatenate([zeros, v_ref[:, lanes]], axis=0),
                    jnp.concatenate([ones, ones], axis=0),
                ],
                axis=1,
            )
            total = jnp.dot(probs, own, preferred_element_type=F32)
            inverse = 1.0 / total[:, LANES:]
            inverse_ref[:, lanes] = inverse
            out_ref[:, lanes] = total[:, :LANES] * inverse


def score(queries, keys, before, values, per):
    rows, channels = queries.shape
    flat = jax.ShapeDtypeStruct((rows, channels), F32)
    return pl.pallas_call(
        functools.partial(score_kernel, per),
        out_shape=(
            jax.ShapeDtypeStruct((channels // HD, rows, rows), BF16),
            flat,
            flat,
            jax.ShapeDtypeStruct((1, rows, LANES), F32),
        ),
        in_specs=[in_vmem()] * 4,
        out_specs=(in_vmem(),) * 4,
        scratch_shapes=[pltpu.VMEM((rows, 2 * rows), F32)],
        compiler_params=params(),
        cost_estimate=cost(
            8 * rows * rows * channels, 14 * rows * channels, 4 * rows * rows * channels // HD
        ),
        name="score",
    )(queries, keys, before, values)


def value_kernel(first, probs_ref, before_ref, own_ref, inverse_ref, square_in_ref, out_ref, square_ref):
    square = square_in_ref[0]
    for k in range(before_ref.shape[1] // LANES):
        lanes = slice((first + k) * LANES, (first + k + 1) * LANES)
        total = own_ref[:, lanes] + inverse_ref[:, lanes] * jnp.dot(
            probs_ref[first + k],
            before_ref[:, k * LANES : (k + 1) * LANES],
            preferred_element_type=F32,
        )
        out_ref[:, lanes] = total
        square = square + total * total
    square_ref[0] = square


def value_mix(first, probs, before, own, inverse, square):
    rows, channels = before.shape
    return pl.pallas_call(
        functools.partial(value_kernel, first),
        out_shape=(
            jax.ShapeDtypeStruct(own.shape, F32),
            jax.ShapeDtypeStruct((1, rows, LANES), F32),
        ),
        in_specs=[in_vmem()] * 5,
        out_specs=(in_vmem(),) * 2,
        input_output_aliases={2: 0},
        compiler_params=params(),
        cost_estimate=cost(1, 1),
        name="value_mix",
    )(probs, before, own, inverse, square)


def normalize_kernel(count, panels, pieces, with_head, *refs):
    square_refs, refs = refs[:panels], refs[panels:]
    mixed_refs, refs = refs[:count], refs[count:]
    if with_head:
        head_ref, refs = refs[0], refs[1:]
    out_refs, (held_ref, sems) = refs[:count], refs[count:]
    rows = mixed_refs[0].shape[0]
    piece = rows // pieces
    copies = []
    for n in range(count):
        square = square_refs[0][n]
        for ref in square_refs[1:]:
            square = square + ref[n]
        scale = lax.rsqrt(jnp.sum(square, axis=-1, keepdims=True) * (1.0 / CHANNELS) + 1e-06)
        for m in range(pieces):
            at = slice(m * piece, (m + 1) * piece)
            value = mixed_refs[n][at, :]
            if with_head and n == 0 and m == 0:
                value = jnp.concatenate([head_ref[...], value[8:]], axis=0)
            held_ref[n, at, :] = (value * scale[at]).astype(BF16)
            copy = pltpu.make_async_copy(
                held_ref.at[n, pl.ds(m * piece, piece)],
                out_refs[n].at[pl.ds(m * piece, piece)],
                sems.at[n, m],
            )
            copy.start()
            copies.append(copy)
    for copy in copies:
        copy.wait()


def normalize(squares, mixed, head=None, pieces=3):
    rows, channels = mixed[0].shape
    count = len(mixed)
    operands = (*squares, *mixed) + (() if head is None else (head,))
    return pl.pallas_call(
        functools.partial(normalize_kernel, count, len(squares), pieces, head is not None),
        out_shape=(jax.ShapeDtypeStruct((rows, channels), BF16),) * count,
        in_specs=[in_vmem()] * len(operands),
        out_specs=(pl.BlockSpec(memory_space=pl.ANY),) * count,
        scratch_shapes=[
            pltpu.VMEM((count, rows, channels), BF16),
            pltpu.SemaphoreType.DMA((count, pieces)),
        ],
        compiler_params=params(),
        cost_estimate=cost(1, 1),
        name="normalize",
    )(*operands)


def from_behind(value):
    count = lax.axis_size("ctx")
    return lax.ppermute(value, "ctx", [(source, source + 1) for source in range(count - 1)])


def of_panels(square):
    count = lax.axis_size("panel")
    return [square] + [
        lax.ppermute(square, "panel", [(n, (n + shift) % count) for n in range(count)])
        for shift in range(1, count)
    ]


def body(se, se_short, se_filter, mr, mr_short, raw, decay, queries, keys, values):
    last_heads = 3 * (queries.shape[1] // HD) // 8
    key_before = from_behind(keys)
    packet, mr_taps, se_taps, decay, filter_taps, most, rest = pack(
        se, mr, se_short, mr_short, decay[None, :], se_filter, values, last_heads, 4
    )
    packet = from_behind(packet)
    own, z0, se_mix, se_square, taps, heads = own_part(
        mr, se, mr_taps, se_taps, raw, decay, filter_taps, 4
    )
    most, own = lax.optimization_barrier((most, own))
    most_before = from_behind(most)
    probs, attended, inverse, square = score(queries, keys, key_before, values, 4)
    rest, attended = lax.optimization_barrier((rest, attended))
    rest_before = from_behind(rest)
    packet, attended = lax.optimization_barrier((packet, attended))
    head, mr_mix, mixed_square = mix(
        packet, own, z0, se_square, taps, heads, mr_taps, se_taps, filter_taps
    )
    se_out, mr_out = normalize(of_panels(mixed_square), (se_mix, mr_mix), head)
    most_before, se_out, mr_out = lax.optimization_barrier((most_before, se_out, mr_out))
    attended, square = value_mix(0, probs, most_before, attended, inverse, square)
    rest_before, attended = lax.optimization_barrier((rest_before, attended))
    first = most.shape[1] // HD
    attended, square = value_mix(first, probs, rest_before, attended, inverse, square)
    (attn_out,) = normalize(of_panels(square), (attended,))
    return se_out, mr_out, attn_out


def solution(mesh):
    placed = (
        P(None, "ctx", "panel"),
        P(None, None, "panel"),
        P(None, "panel"),
        P(None, "ctx", "panel"),
        P(None, None, "panel"),
        P(None, "panel"),
        P("panel"),
        P("ctx", "panel"),
        P("ctx", "panel"),
        P("ctx", "panel"),
    )
    return jax.shard_map(
        body,
        mesh=mesh,
        in_specs=placed,
        out_specs=(P("ctx", "panel"), P("ctx", "panel"), P("ctx", "panel")),
        check_vma=False,
    )
```

```python
import functools
import math

import jax
import jax.numpy as jnp
from jax import lax
from jax.experimental import pallas as pl
from jax.experimental.pallas import tpu as pltpu
from jax.sharding import PartitionSpec as P

CHANNELS = 4096
HD = 128
LSE = 7
MEDIUM_TAPS = 128
LANES = 128
F32 = jnp.float32
BF16 = jnp.bfloat16


def params(mebibytes=6):
    return pltpu.CompilerParams(vmem_limit_bytes=mebibytes * 1024 * 1024)


def in_vmem():
    return pl.BlockSpec(memory_space=pltpu.VMEM)


def cost(flops, nbytes, trans=0):
    return pl.CostEstimate(flops=int(flops), bytes_accessed=int(nbytes), transcendentals=int(trans))


def roll(value, shift):
    shift = shift % value.shape[0]
    return pltpu.roll(value, shift, 0) if shift else value


def row_is(rows, at):
    return lax.broadcasted_iota(jnp.int32, (rows, LANES), 0) == at


def features(u, front, taps):
    ext = jnp.concatenate([front, u], axis=0)
    total = taps[0] * ext
    for j in range(1, len(taps)):
        total = total + taps[j] * roll(ext, j)
    return total[8:]


def tap_rows(ref, stream, lanes):
    return [ref[stream, j : j + 1, lanes] for j in range(ref.shape[1])]


def lane_block(k):
    return pl.ds(pl.multiple_of(k * LANES, LANES), LANES)


def tap_tile(held_ref, j):
    return jnp.broadcast_to(held_ref[j : j + 1, :], (8, LANES))


def pack_kernel(
    per,
    mr_ref,
    se_ref,
    mr_short_ref,
    se_short_ref,
    decay_hbm_ref,
    filter_hbm_ref,
    values_ref,
    out_ref,
    mw_ref,
    sw_ref,
    decay_ref,
    filter_ref,
    most_ref,
    rest_ref,
    m_ref,
    tail_ref,
    last_ref,
    sems,
    late_sems,
):
    _, rows, channels = mr_ref.shape
    width = per * LANES
    chunk = MEDIUM_TAPS + 16
    nothing = jnp.zeros((8, LANES), F32)
    end = pl.ds(rows - 16, 16)
    copies = [
        pltpu.make_async_copy(mr_short_ref, mw_ref, sems.at[0]),
        pltpu.make_async_copy(se_short_ref, sw_ref, sems.at[1]),
        pltpu.make_async_copy(mr_ref.at[pl.ds(0, 1), end], tail_ref.at[pl.ds(0, 1)], sems.at[2]),
        pltpu.make_async_copy(se_ref.at[:, end], tail_ref.at[pl.ds(1, 3)], sems.at[3]),
    ]
    first = len(copies)
    for n in range(channels // width):
        at = pl.ds(n * width, width)
        copies.append(
            pltpu.make_async_copy(
                mr_ref.at[pl.ds(1, 2), :, at], m_ref.at[:, :, at], sems.at[first + n]
            )
        )
    most = most_ref.shape[1]
    late = [
        pltpu.make_async_copy(values_ref.at[:, pl.ds(0, most)], most_ref, late_sems.at[0]),
        pltpu.make_async_copy(
            values_ref.at[:, pl.ds(most, channels - most)], rest_ref, late_sems.at[1]
        ),
        pltpu.make_async_copy(decay_hbm_ref, decay_ref, late_sems.at[2]),
        pltpu.make_async_copy(filter_hbm_ref, filter_ref, late_sems.at[3]),
    ]
    for copy in copies + late:
        copy.start()
    for copy in copies[:first]:
        copy.wait()
    last_ref[...] = jnp.zeros_like(last_ref)

    def one(block):
        lanes = lane_block(block)
        m1 = m_ref[0, :, lanes].astype(F32)
        m2 = m_ref[1, :, lanes].astype(F32)
        z1 = features(m1, nothing, tap_rows(mw_ref, 1, lanes))
        z2 = features(m2, nothing, tap_rows(mw_ref, 2, lanes))
        product = (z1 * z2)[rows - MEDIUM_TAPS :]
        tail_m0 = tail_ref[0, :, lanes].astype(F32)[8:]
        tail_m1, tail_m2 = m1[rows - 8 :], m2[rows - 8 :]
        head = jnp.where(row_is(8, 0), roll(tail_m2, 2), product[:8])
        product = jnp.concatenate([head, product[8:]], axis=0)
        s0 = tail_ref[1, :, lanes].astype(F32)[8:]
        s1 = tail_ref[2, :, lanes].astype(F32)
        s2 = tail_ref[3, :, lanes].astype(F32)
        y1 = features(s1, nothing, tap_rows(sw_ref, 1, lanes))[8:]
        y2 = features(s2, nothing, tap_rows(sw_ref, 2, lanes))[8:]
        at = lax.broadcasted_iota(jnp.int32, (8, LANES), 0)
        x1 = jnp.where(at < 2, roll(s0, 2), y1 * y2)
        x2 = jnp.where(
            at < 2,
            roll(s1[8:], 2),
            jnp.where(at < 4, roll(s2[8:], 4), jnp.where(at < 6, roll(tail_m0, 6), tail_m1)),
        )
        start = pl.multiple_of(block * chunk, 16)
        out_ref[pl.ds(start, MEDIUM_TAPS), :] = product.astype(BF16)
        out_ref[pl.ds(start + MEDIUM_TAPS, 16), :] = jnp.concatenate([x1, x2], axis=0).astype(BF16)
        last_ref[pl.ds(block, 1), :] = tail_m2[7:8]

    for n in range(channels // width):
        copies[first + n].wait()
        pl.loop(n * per, (n + 1) * per)(one)

    out_ref[out_ref.shape[0] - 16 :, :] = last_ref[...].astype(BF16)
    for copy in late:
        copy.wait()


def pack(se, mr, se_short, mr_short, decay, se_filter, values, last_heads, per):
    _, rows, channels = se.shape
    blocks = channels // LANES
    total = blocks * (MEDIUM_TAPS + 16) + 16
    rest = last_heads * HD
    operands = (mr, se, mr_short, se_short, decay, se_filter, values)
    return pl.pallas_call(
        functools.partial(pack_kernel, per),
        out_shape=(
            jax.ShapeDtypeStruct((total, LANES), BF16),
            jax.ShapeDtypeStruct(mr_short.shape, F32),
            jax.ShapeDtypeStruct(se_short.shape, F32),
            jax.ShapeDtypeStruct(decay.shape, F32),
            jax.ShapeDtypeStruct(se_filter.shape, F32),
            jax.ShapeDtypeStruct((rows, channels - rest), BF16),
            jax.ShapeDtypeStruct((rows, rest), BF16),
        ),
        in_specs=[pl.BlockSpec(memory_space=pltpu.HBM)] * 7,
        out_specs=(in_vmem(),) * 7,
        scratch_shapes=[
            pltpu.VMEM((2, rows, channels), BF16),
            pltpu.VMEM((4, 16, channels), BF16),
            pltpu.VMEM((16, LANES), F32),
            pltpu.SemaphoreType.DMA((4 + blocks // per,)),
            pltpu.SemaphoreType.DMA((4,)),
        ],
        compiler_params=params(),
        cost_estimate=cost(20 * rows * channels, 10 * rows * channels),
        name="pack",
    )(*(pltpu.with_memory_space_constraint(x, pltpu.HBM) for x in operands))


def own_kernel(
    per,
    m_hbm_ref,
    s_hbm_ref,
    raw_hbm_ref,
    mw_ref,
    sw_ref,
    decay_ref,
    filter_ref,
    own_ref,
    z0_ref,
    se_ref,
    square_ref,
    taps_ref,
    heads_ref,
    m_ref,
    s_ref,
    raw_ref,
    held_ref,
    sems,
):
    rows, channels = own_ref.shape
    tiles = rows // 8
    width = per * LANES
    nothing = jnp.zeros((8, LANES), F32)

    def fetch(n):
        at = pl.ds(pl.multiple_of(n * width, width), width)
        return (
            pltpu.make_async_copy(s_hbm_ref.at[:, :, at], s_ref.at[:, :, at], sems.at[0, n]),
            pltpu.make_async_copy(m_hbm_ref.at[:, :, at], m_ref.at[:, :, at], sems.at[1, n]),
            pltpu.make_async_copy(raw_hbm_ref.at[:, at], raw_ref.at[:, at], sems.at[2, n]),
        )

    for n in range(channels // width):
        for copy in fetch(n):
            copy.start()
    square_ref[...] = jnp.zeros_like(square_ref)

    @pl.loop(0, channels // LANES)
    def _(k):
        @pl.when(k % per == 0)
        def _():
            for copy in fetch(k // per):
                copy.wait()

        lanes = lane_block(k)
        u = [s_ref[n, :, lanes].astype(F32) for n in range(3)]
        for n in range(3):
            heads_ref[n, :, lanes] = u[n][:8]
        s = [features(u[n], nothing, tap_rows(sw_ref, n, lanes)) for n in range(3)]
        ext = jnp.concatenate([nothing, (s[1] * s[2]).astype(BF16).astype(F32)], axis=0)
        total = filter_ref[0:1, lanes] * ext
        for j in range(1, LSE):
            total = total + filter_ref[j : j + 1, lanes] * roll(ext, j)
        mixed = s[0] * total[8:]
        se_ref[:, lanes] = mixed
        square_ref[8:, :] += mixed[8:] * mixed[8:]

        steps = lax.broadcasted_iota(jnp.int32, (MEDIUM_TAPS, LANES), 0).astype(F32)
        taps = raw_ref[:, lanes] * jnp.exp(-decay_ref[0:1, lanes] * steps)
        held_ref[...] = taps
        taps_ref[:, lanes] = taps
        u = [m_ref[n, :, lanes].astype(F32) for n in range(3)]
        for n in range(3):
            heads_ref[3 + n, :, lanes] = u[n][:8]
        z = [features(u[n], nothing, tap_rows(mw_ref, n, lanes)) for n in range(3)]
        z0_ref[:, lanes] = z[0]
        product = (z[1] * z[2]).astype(BF16).astype(F32)
        at = lax.broadcasted_iota(jnp.int32, (8, LANES), 0)
        head = jnp.where(at < 2, 0.0, product[:8])
        ext = jnp.concatenate([nothing, head, product[8:]], axis=0)
        total = [None] * tiles
        for r in range(8):
            shifted = roll(ext, r)
            tap = [tap_tile(held_ref, 8 * a + r) for a in range(MEDIUM_TAPS // 8)]
            for i in range(tiles):
                for a in range(min(i + 1, MEDIUM_TAPS // 8)):
                    at_tile = 8 * (i - a + 1)
                    term = tap[a] * shifted[at_tile : at_tile + 8]
                    total[i] = term if total[i] is None else total[i] + term
        own_ref[:, lanes] = jnp.concatenate(total, axis=0)


def own_part(mr, se, mr_short, se_short, raw, decay, se_filter, per):
    _, rows, channels = mr.shape
    mixed = jax.ShapeDtypeStruct((rows, channels), F32)
    mr, se, raw = (pltpu.with_memory_space_constraint(x, pltpu.HBM) for x in (mr, se, raw))
    return pl.pallas_call(
        functools.partial(own_kernel, per),
        out_shape=(
            mixed,
            mixed,
            mixed,
            jax.ShapeDtypeStruct((rows, LANES), F32),
            jax.ShapeDtypeStruct((MEDIUM_TAPS, channels), F32),
            jax.ShapeDtypeStruct((6, 8, channels), F32),
        ),
        in_specs=[pl.BlockSpec(memory_space=pltpu.HBM)] * 3 + [in_vmem()] * 4,
        out_specs=(in_vmem(),) * 6,
        scratch_shapes=[
            pltpu.VMEM(mr.shape, BF16),
            pltpu.VMEM(se.shape, BF16),
            pltpu.VMEM((MEDIUM_TAPS, channels), F32),
            pltpu.VMEM((MEDIUM_TAPS, LANES), F32),
            pltpu.SemaphoreType.DMA((3, channels // (per * LANES))),
        ],
        compiler_params=params(10),
        cost_estimate=cost(180 * rows * channels, 24 * rows * channels),
        name="own_part",
    )(mr, se, raw, mr_short, se_short, decay, se_filter)


def mix_kernel(
    packet_ref,
    own_ref,
    z0_ref,
    se_square_ref,
    taps_ref,
    heads_ref,
    mw_ref,
    sw_ref,
    filter_ref,
    head_ref,
    mr_ref,
    square_ref,
    last_ref,
    held_ref,
):
    rows, channels = own_ref.shape
    tiles = rows // 8
    chunk = MEDIUM_TAPS + 16
    nothing = jnp.zeros((8, LANES), F32)
    last_ref[...] = packet_ref[packet_ref.shape[0] - 16 :, :].astype(F32)
    square_ref[0] = se_square_ref[...]
    square_ref[1] = jnp.zeros((rows, LANES), F32)

    @pl.loop(0, channels // LANES)
    def _(k):
        lanes = lane_block(k)
        start = pl.multiple_of(k * chunk, 16)
        before = packet_ref[pl.ds(start, MEDIUM_TAPS), :].astype(F32)
        x = packet_ref[pl.ds(start + MEDIUM_TAPS, 16), :].astype(F32)
        x1, x2 = x[:8], x[8:]
        last = last_ref[pl.ds(k, 1), :]

        fronts = (roll(x1, 6), roll(x2, 6), roll(x2, 4))
        s = [
            features(heads_ref[n, :, lanes], fronts[n], tap_rows(sw_ref, n, lanes))
            for n in range(3)
        ]
        ext = jnp.concatenate([x1, (s[1] * s[2]).astype(BF16).astype(F32)], axis=0)
        total = filter_ref[0:1, lanes] * ext
        for j in range(1, LSE):
            total = total + filter_ref[j : j + 1, lanes] * roll(ext, j)
        mixed = s[0] * total[8:]
        head_ref[:, lanes] = mixed
        square_ref[0, :8, :] += mixed * mixed

        taps = taps_ref[:, lanes]
        held_ref[...] = taps
        front2 = jnp.where(row_is(8, 7), last, roll(before[:8], 6))
        fronts = (roll(x2, 2), x2, front2)
        z = [
            features(heads_ref[3 + n, :, lanes], fronts[n], tap_rows(mw_ref, n, lanes))
            for n in range(3)
        ]
        first = (z[1] * z[2]).astype(BF16).astype(F32)
        padded = jnp.concatenate([taps, jnp.zeros((rows - MEDIUM_TAPS, LANES), F32)], axis=0)
        base = own_ref[:, lanes] + padded * first[0:1] + roll(padded, 1) * first[1:2]
        total = [base[8 * i : 8 * i + 8] for i in range(tiles)]
        ext = jnp.concatenate([before, nothing], axis=0)
        count = MEDIUM_TAPS // 8
        for r in range(8):
            shifted = roll(ext, r)
            tap = [tap_tile(held_ref, 8 * a + r) for a in range(count)]
            for i in range(count):
                for a in range(i if r else i + 1, count):
                    at_tile = 8 * (i - a + count)
                    total[i] = total[i] + tap[a] * shifted[at_tile : at_tile + 8]
        z0 = jnp.concatenate([z[0], z0_ref[8:, lanes]], axis=0)
        mixed = z0 * jnp.concatenate(total, axis=0)
        mr_ref[:, lanes] = mixed
        square_ref[1] += mixed * mixed


def mix(packet, own, z0, se_square, taps, heads, mr_short, se_short, se_filter):
    rows, channels = own.shape
    return pl.pallas_call(
        mix_kernel,
        out_shape=(
            jax.ShapeDtypeStruct((8, channels), F32),
            jax.ShapeDtypeStruct((rows, channels), F32),
            jax.ShapeDtypeStruct((2, rows, LANES), F32),
        ),
        in_specs=[in_vmem()] * 9,
        out_specs=(in_vmem(),) * 3,
        scratch_shapes=[pltpu.VMEM((16, LANES), F32), pltpu.VMEM((MEDIUM_TAPS, LANES), F32)],
        compiler_params=params(),
        cost_estimate=cost(1, 1),
        name="mix",
    )(packet, own, z0, se_square, taps, heads, mr_short, se_short, se_filter)


def score_kernel(
    per, q_ref, k_ref, before_ref, v_ref, probs_ref, out_ref, inverse_ref, square_ref, bias_ref
):
    rows, channels = q_ref.shape
    at = lax.broadcasted_iota(jnp.int32, (rows, 2 * rows), 0)
    key = lax.broadcasted_iota(jnp.int32, (rows, 2 * rows), 1)
    valid = (key <= at + rows) & ((key >= rows) | (lax.axis_index("ctx") > 0))
    bias_ref[...] = jnp.where(valid, 0.0, -1e30)
    square_ref[...] = jnp.zeros_like(square_ref)
    factor = math.log2(math.e) / math.sqrt(HD)
    zeros, ones = jnp.zeros((rows, LANES), BF16), jnp.ones((rows, LANES), BF16)

    @pl.loop(0, channels // (LANES * per))
    def _(group):
        for n in range(per):
            head = group * per + n
            lanes = lane_block(head)
            both = jnp.concatenate([before_ref[:, lanes], k_ref[:, lanes]], axis=0)
            scores = lax.dot_general(
                q_ref[:, lanes], both, (((1,), (1,)), ((), ())), preferred_element_type=F32
            )
            scores = scores + bias_ref[...]
            top = jnp.max(scores, axis=-1, keepdims=True)
            probs = jnp.exp2((scores - top) * factor).astype(BF16)
            probs_ref[head] = probs[:, :rows]
            own = jnp.concatenate(
                [
                    jnp.concatenate([zeros, v_ref[:, lanes]], axis=0),
                    jnp.concatenate([ones, ones], axis=0),
                ],
                axis=1,
            )
            total = jnp.dot(probs, own, preferred_element_type=F32)
            inverse = 1.0 / total[:, LANES:]
            inverse_ref[:, lanes] = inverse
            out_ref[:, lanes] = total[:, :LANES] * inverse


def score(queries, keys, before, values, per):
    rows, channels = queries.shape
    flat = jax.ShapeDtypeStruct((rows, channels), F32)
    return pl.pallas_call(
        functools.partial(score_kernel, per),
        out_shape=(
            jax.ShapeDtypeStruct((channels // HD, rows, rows), BF16),
            flat,
            flat,
            jax.ShapeDtypeStruct((1, rows, LANES), F32),
        ),
        in_specs=[in_vmem()] * 4,
        out_specs=(in_vmem(),) * 4,
        scratch_shapes=[pltpu.VMEM((rows, 2 * rows), F32)],
        compiler_params=params(),
        cost_estimate=cost(
            8 * rows * rows * channels, 14 * rows * channels, 4 * rows * rows * channels // HD
        ),
        name="score",
    )(queries, keys, before, values)


def value_kernel(first, probs_ref, before_ref, own_ref, inverse_ref, square_in_ref, out_ref, square_ref):
    square = square_in_ref[0]
    for k in range(before_ref.shape[1] // LANES):
        lanes = slice((first + k) * LANES, (first + k + 1) * LANES)
        total = own_ref[:, lanes] + inverse_ref[:, lanes] * jnp.dot(
            probs_ref[first + k],
            before_ref[:, k * LANES : (k + 1) * LANES],
            preferred_element_type=F32,
        )
        out_ref[:, lanes] = total
        square = square + total * total
    square_ref[0] = square


def value_mix(first, probs, before, own, inverse, square):
    rows, channels = before.shape
    return pl.pallas_call(
        functools.partial(value_kernel, first),
        out_shape=(
            jax.ShapeDtypeStruct(own.shape, F32),
            jax.ShapeDtypeStruct((1, rows, LANES), F32),
        ),
        in_specs=[in_vmem()] * 5,
        out_specs=(in_vmem(),) * 2,
        input_output_aliases={2: 0},
        compiler_params=params(),
        cost_estimate=cost(1, 1),
        name="value_mix",
    )(probs, before, own, inverse, square)


def normalize_kernel(count, panels, with_head, *refs):
    square_refs, refs = refs[:panels], refs[panels:]
    mixed_refs, refs = refs[:count], refs[count:]
    if with_head:
        head_ref, refs = refs[0], refs[1:]
    out_refs, (held_ref, sems) = refs[:count], refs[count:]
    pieces = mixed_refs[0].shape[0] // 16

    def write(n, m):
        at = pl.ds(pl.multiple_of(m * 16, 16), 16)
        return pltpu.make_async_copy(held_ref.at[n, at], out_refs[n].at[at], sems.at[n, m])

    for n in range(count):

        @pl.loop(0, pieces)
        def _(m):
            at = pl.ds(pl.multiple_of(m * 16, 16), 16)
            square = square_refs[0][n, at, :]
            for ref in square_refs[1:]:
                square = square + ref[n, at, :]
            scale = lax.rsqrt(jnp.sum(square, axis=-1, keepdims=True) * (1.0 / CHANNELS) + 1e-06)
            value = mixed_refs[n][at, :]
            if with_head and n == 0:
                value = jnp.where(m == 0, jnp.concatenate([head_ref[...], value[8:]], axis=0), value)
            held_ref[n, at, :] = (value * scale).astype(BF16)
            write(n, m).start()

    for n in range(count):
        for m in range(pieces):
            write(n, m).wait()


def normalize(squares, mixed, head=None):
    rows, channels = mixed[0].shape
    count = len(mixed)
    operands = (*squares, *mixed) + (() if head is None else (head,))
    return pl.pallas_call(
        functools.partial(normalize_kernel, count, len(squares), head is not None),
        out_shape=(jax.ShapeDtypeStruct((rows, channels), BF16),) * count,
        in_specs=[in_vmem()] * len(operands),
        out_specs=(pl.BlockSpec(memory_space=pl.ANY),) * count,
        scratch_shapes=[
            pltpu.VMEM((count, rows, channels), BF16),
            pltpu.SemaphoreType.DMA((count, rows // 16)),
        ],
        compiler_params=params(),
        cost_estimate=cost(1, 1),
        name="normalize",
    )(*operands)


def from_behind(value):
    count = lax.axis_size("ctx")
    return lax.ppermute(value, "ctx", [(source, source + 1) for source in range(count - 1)])


def of_panels(square):
    count = lax.axis_size("panel")
    return [square] + [
        lax.ppermute(square, "panel", [(n, (n + shift) % count) for n in range(count)])
        for shift in range(1, count)
    ]


def body(se, se_short, se_filter, mr, mr_short, raw, decay, queries, keys, values):
    last_heads = 3 * (queries.shape[1] // HD) // 8
    key_before = from_behind(keys)
    packet, mr_taps, se_taps, decay, filter_taps, most, rest = pack(
        se, mr, se_short, mr_short, decay[None, :], se_filter, values, last_heads, 4
    )
    packet = from_behind(packet)
    own, z0, se_mix, se_square, taps, heads = own_part(
        mr, se, mr_taps, se_taps, raw, decay, filter_taps, 4
    )
    most, own = lax.optimization_barrier((most, own))
    most_before = from_behind(most)
    probs, attended, inverse, square = score(queries, keys, key_before, values, 4)
    rest, attended = lax.optimization_barrier((rest, attended))
    rest_before = from_behind(rest)
    packet, attended = lax.optimization_barrier((packet, attended))
    head, mr_mix, mixed_square = mix(
        packet, own, z0, se_square, taps, heads, mr_taps, se_taps, filter_taps
    )
    se_out, mr_out = normalize(of_panels(mixed_square), (se_mix, mr_mix), head)
    most_before, se_out, mr_out = lax.optimization_barrier((most_before, se_out, mr_out))
    attended, square = value_mix(0, probs, most_before, attended, inverse, square)
    rest_before, attended = lax.optimization_barrier((rest_before, attended))
    first = most.shape[1] // HD
    attended, square = value_mix(first, probs, rest_before, attended, inverse, square)
    (attn_out,) = normalize(of_panels(square), (attended,))
    return se_out, mr_out, attn_out


def solution(mesh):
    placed = (
        P(None, "ctx", "panel"),
        P(None, None, "panel"),
        P(None, "panel"),
        P(None, "ctx", "panel"),
        P(None, None, "panel"),
        P(None, "panel"),
        P("panel"),
        P("ctx", "panel"),
        P("ctx", "panel"),
        P("ctx", "panel"),
    )
    return jax.shard_map(
        body,
        mesh=mesh,
        in_specs=placed,
        out_specs=(P("ctx", "panel"), P("ctx", "panel"), P("ctx", "panel")),
        check_vma=False,
    )
```

```python
import functools
import math

import jax
import jax.numpy as jnp
from jax import lax
from jax.experimental import pallas as pl
from jax.experimental.pallas import tpu as pltpu
from jax.sharding import PartitionSpec as P

CHANNELS = 4096
HD = 128
LSE = 7
MEDIUM_TAPS = 128
LANES = 128
F32 = jnp.float32
BF16 = jnp.bfloat16


def params(mebibytes=6):
    return pltpu.CompilerParams(vmem_limit_bytes=mebibytes * 1024 * 1024)


def in_vmem():
    return pl.BlockSpec(memory_space=pltpu.VMEM)


def cost(flops, nbytes, trans=0):
    return pl.CostEstimate(flops=int(flops), bytes_accessed=int(nbytes), transcendentals=int(trans))


def roll(value, shift):
    shift = shift % value.shape[0]
    return pltpu.roll(value, shift, 0) if shift else value


def row_is(rows, at):
    return lax.broadcasted_iota(jnp.int32, (rows, LANES), 0) == at


def features(u, front, taps):
    ext = jnp.concatenate([front, u], axis=0)
    total = taps[0] * ext
    for j in range(1, len(taps)):
        total = total + taps[j] * roll(ext, j)
    return total[8:]


def tap_rows(ref, stream, lanes):
    return [ref[stream, j : j + 1, lanes] for j in range(ref.shape[1])]


def lane_block(k):
    return pl.ds(pl.multiple_of(k * LANES, LANES), LANES)


def tap_tile(held_ref, j):
    return jnp.broadcast_to(held_ref[j : j + 1, :], (8, LANES))


def pack_kernel(
    per,
    mr_ref,
    se_ref,
    mr_short_ref,
    se_short_ref,
    decay_hbm_ref,
    filter_hbm_ref,
    values_ref,
    out_ref,
    mw_ref,
    sw_ref,
    decay_ref,
    filter_ref,
    most_ref,
    rest_ref,
    m_ref,
    tail_ref,
    last_ref,
    sems,
    late_sems,
):
    _, rows, channels = mr_ref.shape
    width = per * LANES
    chunk = MEDIUM_TAPS + 16
    nothing = jnp.zeros((8, LANES), F32)
    end = pl.ds(rows - 16, 16)
    copies = [
        pltpu.make_async_copy(mr_short_ref, mw_ref, sems.at[0]),
        pltpu.make_async_copy(se_short_ref, sw_ref, sems.at[1]),
        pltpu.make_async_copy(mr_ref.at[pl.ds(0, 1), end], tail_ref.at[pl.ds(0, 1)], sems.at[2]),
        pltpu.make_async_copy(se_ref.at[:, end], tail_ref.at[pl.ds(1, 3)], sems.at[3]),
    ]
    first = len(copies)
    for n in range(channels // width):
        at = pl.ds(n * width, width)
        copies.append(
            pltpu.make_async_copy(
                mr_ref.at[pl.ds(1, 2), :, at], m_ref.at[:, :, at], sems.at[first + n]
            )
        )
    most = most_ref.shape[1]
    late = [
        pltpu.make_async_copy(values_ref.at[:, pl.ds(0, most)], most_ref, late_sems.at[0]),
        pltpu.make_async_copy(
            values_ref.at[:, pl.ds(most, channels - most)], rest_ref, late_sems.at[1]
        ),
        pltpu.make_async_copy(decay_hbm_ref, decay_ref, late_sems.at[2]),
        pltpu.make_async_copy(filter_hbm_ref, filter_ref, late_sems.at[3]),
    ]
    for copy in copies:
        copy.start()
    for copy in copies[:first]:
        copy.wait()
    last_ref[...] = jnp.zeros_like(last_ref)

    def one(block):
        lanes = lane_block(block)
        m1 = m_ref[0, :, lanes].astype(F32)
        m2 = m_ref[1, :, lanes].astype(F32)
        z1 = features(m1, nothing, tap_rows(mw_ref, 1, lanes))
        z2 = features(m2, nothing, tap_rows(mw_ref, 2, lanes))
        product = (z1 * z2)[rows - MEDIUM_TAPS :]
        tail_m0 = tail_ref[0, :, lanes].astype(F32)[8:]
        tail_m1, tail_m2 = m1[rows - 8 :], m2[rows - 8 :]
        head = jnp.where(row_is(8, 0), roll(tail_m2, 2), product[:8])
        product = jnp.concatenate([head, product[8:]], axis=0)
        s0 = tail_ref[1, :, lanes].astype(F32)[8:]
        s1 = tail_ref[2, :, lanes].astype(F32)
        s2 = tail_ref[3, :, lanes].astype(F32)
        y1 = features(s1, nothing, tap_rows(sw_ref, 1, lanes))[8:]
        y2 = features(s2, nothing, tap_rows(sw_ref, 2, lanes))[8:]
        at = lax.broadcasted_iota(jnp.int32, (8, LANES), 0)
        x1 = jnp.where(at < 2, roll(s0, 2), y1 * y2)
        x2 = jnp.where(
            at < 2,
            roll(s1[8:], 2),
            jnp.where(at < 4, roll(s2[8:], 4), jnp.where(at < 6, roll(tail_m0, 6), tail_m1)),
        )
        start = pl.multiple_of(block * chunk, 16)
        out_ref[pl.ds(start, MEDIUM_TAPS), :] = product.astype(BF16)
        out_ref[pl.ds(start + MEDIUM_TAPS, 16), :] = jnp.concatenate([x1, x2], axis=0).astype(BF16)
        last_ref[pl.ds(block, 1), :] = tail_m2[7:8]

    for n in range(channels // width):
        copies[first + n].wait()
        if n == 0:
            for copy in late:
                copy.start()
        pl.loop(n * per, (n + 1) * per)(one)

    out_ref[out_ref.shape[0] - 16 :, :] = last_ref[...].astype(BF16)
    for copy in late:
        copy.wait()


def pack(se, mr, se_short, mr_short, decay, se_filter, values, last_heads, per):
    _, rows, channels = se.shape
    blocks = channels // LANES
    total = blocks * (MEDIUM_TAPS + 16) + 16
    rest = last_heads * HD
    operands = (mr, se, mr_short, se_short, decay, se_filter, values)
    return pl.pallas_call(
        functools.partial(pack_kernel, per),
        out_shape=(
            jax.ShapeDtypeStruct((total, LANES), BF16),
            jax.ShapeDtypeStruct(mr_short.shape, F32),
            jax.ShapeDtypeStruct(se_short.shape, F32),
            jax.ShapeDtypeStruct(decay.shape, F32),
            jax.ShapeDtypeStruct(se_filter.shape, F32),
            jax.ShapeDtypeStruct((rows, channels - rest), BF16),
            jax.ShapeDtypeStruct((rows, rest), BF16),
        ),
        in_specs=[pl.BlockSpec(memory_space=pltpu.HBM)] * 7,
        out_specs=(in_vmem(),) * 7,
        scratch_shapes=[
            pltpu.VMEM((2, rows, channels), BF16),
            pltpu.VMEM((4, 16, channels), BF16),
            pltpu.VMEM((16, LANES), F32),
            pltpu.SemaphoreType.DMA((4 + blocks // per,)),
            pltpu.SemaphoreType.DMA((4,)),
        ],
        compiler_params=params(),
        cost_estimate=cost(20 * rows * channels, 10 * rows * channels),
        name="pack",
    )(*(pltpu.with_memory_space_constraint(x, pltpu.HBM) for x in operands))


def own_kernel(
    per,
    m_hbm_ref,
    s_hbm_ref,
    raw_hbm_ref,
    mw_ref,
    sw_ref,
    decay_ref,
    filter_ref,
    own_ref,
    z0_ref,
    se_ref,
    square_ref,
    taps_ref,
    heads_ref,
    m_ref,
    s_ref,
    raw_ref,
    held_ref,
    sems,
):
    rows, channels = own_ref.shape
    tiles = rows // 8
    width = per * LANES
    nothing = jnp.zeros((8, LANES), F32)

    def fetch(n):
        at = pl.ds(pl.multiple_of(n * width, width), width)
        return (
            pltpu.make_async_copy(s_hbm_ref.at[:, :, at], s_ref.at[:, :, at], sems.at[0, n]),
            pltpu.make_async_copy(m_hbm_ref.at[:, :, at], m_ref.at[:, :, at], sems.at[1, n]),
            pltpu.make_async_copy(raw_hbm_ref.at[:, at], raw_ref.at[:, at], sems.at[2, n]),
        )

    for n in range(channels // width):
        for copy in fetch(n):
            copy.start()
    square_ref[...] = jnp.zeros_like(square_ref)

    @pl.loop(0, channels // LANES)
    def _(k):
        @pl.when(k % per == 0)
        def _():
            for copy in fetch(k // per):
                copy.wait()

        lanes = lane_block(k)
        u = [s_ref[n, :, lanes].astype(F32) for n in range(3)]
        for n in range(3):
            heads_ref[n, :, lanes] = u[n][:8]
        s = [features(u[n], nothing, tap_rows(sw_ref, n, lanes)) for n in range(3)]
        ext = jnp.concatenate([nothing, (s[1] * s[2]).astype(BF16).astype(F32)], axis=0)
        total = filter_ref[0:1, lanes] * ext
        for j in range(1, LSE):
            total = total + filter_ref[j : j + 1, lanes] * roll(ext, j)
        mixed = s[0] * total[8:]
        se_ref[:, lanes] = mixed
        square_ref[8:, :] += mixed[8:] * mixed[8:]

        steps = lax.broadcasted_iota(jnp.int32, (MEDIUM_TAPS, LANES), 0).astype(F32)
        taps = raw_ref[:, lanes] * jnp.exp(-decay_ref[0:1, lanes] * steps)
        held_ref[...] = taps
        taps_ref[:, lanes] = taps
        u = [m_ref[n, :, lanes].astype(F32) for n in range(3)]
        for n in range(3):
            heads_ref[3 + n, :, lanes] = u[n][:8]
        z = [features(u[n], nothing, tap_rows(mw_ref, n, lanes)) for n in range(3)]
        z0_ref[:, lanes] = z[0]
        product = (z[1] * z[2]).astype(BF16).astype(F32)
        at = lax.broadcasted_iota(jnp.int32, (8, LANES), 0)
        head = jnp.where(at < 2, 0.0, product[:8])
        ext = jnp.concatenate([nothing, head, product[8:]], axis=0)
        total = [None] * tiles
        for r in range(8):
            shifted = roll(ext, r)
            tap = [tap_tile(held_ref, 8 * a + r) for a in range(MEDIUM_TAPS // 8)]
            for i in range(tiles):
                for a in range(min(i + 1, MEDIUM_TAPS // 8)):
                    at_tile = 8 * (i - a + 1)
                    term = tap[a] * shifted[at_tile : at_tile + 8]
                    total[i] = term if total[i] is None else total[i] + term
        own_ref[:, lanes] = jnp.concatenate(total, axis=0)


def own_part(mr, se, mr_short, se_short, raw, decay, se_filter, per):
    _, rows, channels = mr.shape
    mixed = jax.ShapeDtypeStruct((rows, channels), F32)
    mr, se, raw = (pltpu.with_memory_space_constraint(x, pltpu.HBM) for x in (mr, se, raw))
    return pl.pallas_call(
        functools.partial(own_kernel, per),
        out_shape=(
            mixed,
            mixed,
            mixed,
            jax.ShapeDtypeStruct((rows, LANES), F32),
            jax.ShapeDtypeStruct((MEDIUM_TAPS, channels), F32),
            jax.ShapeDtypeStruct((6, 8, channels), F32),
        ),
        in_specs=[pl.BlockSpec(memory_space=pltpu.HBM)] * 3 + [in_vmem()] * 4,
        out_specs=(in_vmem(),) * 6,
        scratch_shapes=[
            pltpu.VMEM(mr.shape, BF16),
            pltpu.VMEM(se.shape, BF16),
            pltpu.VMEM((MEDIUM_TAPS, channels), F32),
            pltpu.VMEM((MEDIUM_TAPS, LANES), F32),
            pltpu.SemaphoreType.DMA((3, channels // (per * LANES))),
        ],
        compiler_params=params(10),
        cost_estimate=cost(180 * rows * channels, 24 * rows * channels),
        name="own_part",
    )(mr, se, raw, mr_short, se_short, decay, se_filter)


def mix_kernel(
    packet_ref,
    own_ref,
    z0_ref,
    se_square_ref,
    taps_ref,
    heads_ref,
    mw_ref,
    sw_ref,
    filter_ref,
    head_ref,
    mr_ref,
    square_ref,
    last_ref,
    held_ref,
):
    rows, channels = own_ref.shape
    tiles = rows // 8
    chunk = MEDIUM_TAPS + 16
    nothing = jnp.zeros((8, LANES), F32)
    last_ref[...] = packet_ref[packet_ref.shape[0] - 16 :, :].astype(F32)
    square_ref[0] = se_square_ref[...]
    square_ref[1] = jnp.zeros((rows, LANES), F32)

    @pl.loop(0, channels // LANES)
    def _(k):
        lanes = lane_block(k)
        start = pl.multiple_of(k * chunk, 16)
        before = packet_ref[pl.ds(start, MEDIUM_TAPS), :].astype(F32)
        x = packet_ref[pl.ds(start + MEDIUM_TAPS, 16), :].astype(F32)
        x1, x2 = x[:8], x[8:]
        last = last_ref[pl.ds(k, 1), :]

        fronts = (roll(x1, 6), roll(x2, 6), roll(x2, 4))
        s = [
            features(heads_ref[n, :, lanes], fronts[n], tap_rows(sw_ref, n, lanes))
            for n in range(3)
        ]
        ext = jnp.concatenate([x1, (s[1] * s[2]).astype(BF16).astype(F32)], axis=0)
        total = filter_ref[0:1, lanes] * ext
        for j in range(1, LSE):
            total = total + filter_ref[j : j + 1, lanes] * roll(ext, j)
        mixed = s[0] * total[8:]
        head_ref[:, lanes] = mixed
        square_ref[0, :8, :] += mixed * mixed

        taps = taps_ref[:, lanes]
        held_ref[...] = taps
        front2 = jnp.where(row_is(8, 7), last, roll(before[:8], 6))
        fronts = (roll(x2, 2), x2, front2)
        z = [
            features(heads_ref[3 + n, :, lanes], fronts[n], tap_rows(mw_ref, n, lanes))
            for n in range(3)
        ]
        first = (z[1] * z[2]).astype(BF16).astype(F32)
        padded = jnp.concatenate([taps, jnp.zeros((rows - MEDIUM_TAPS, LANES), F32)], axis=0)
        base = own_ref[:, lanes] + padded * first[0:1] + roll(padded, 1) * first[1:2]
        total = [base[8 * i : 8 * i + 8] for i in range(tiles)]
        ext = jnp.concatenate([before, nothing], axis=0)
        count = MEDIUM_TAPS // 8
        for r in range(8):
            shifted = roll(ext, r)
            tap = [tap_tile(held_ref, 8 * a + r) for a in range(count)]
            for i in range(count):
                for a in range(i if r else i + 1, count):
                    at_tile = 8 * (i - a + count)
                    total[i] = total[i] + tap[a] * shifted[at_tile : at_tile + 8]
        z0 = jnp.concatenate([z[0], z0_ref[8:, lanes]], axis=0)
        mixed = z0 * jnp.concatenate(total, axis=0)
        mr_ref[:, lanes] = mixed
        square_ref[1] += mixed * mixed


def mix(packet, own, z0, se_square, taps, heads, mr_short, se_short, se_filter):
    rows, channels = own.shape
    return pl.pallas_call(
        mix_kernel,
        out_shape=(
            jax.ShapeDtypeStruct((8, channels), F32),
            jax.ShapeDtypeStruct((rows, channels), F32),
            jax.ShapeDtypeStruct((2, rows, LANES), F32),
        ),
        in_specs=[in_vmem()] * 9,
        out_specs=(in_vmem(),) * 3,
        scratch_shapes=[pltpu.VMEM((16, LANES), F32), pltpu.VMEM((MEDIUM_TAPS, LANES), F32)],
        compiler_params=params(),
        cost_estimate=cost(1, 1),
        name="mix",
    )(packet, own, z0, se_square, taps, heads, mr_short, se_short, se_filter)


def score_kernel(
    per, q_ref, k_ref, before_ref, v_ref, probs_ref, out_ref, inverse_ref, square_ref, bias_ref
):
    rows, channels = q_ref.shape
    at = lax.broadcasted_iota(jnp.int32, (rows, 2 * rows), 0)
    key = lax.broadcasted_iota(jnp.int32, (rows, 2 * rows), 1)
    valid = (key <= at + rows) & ((key >= rows) | (lax.axis_index("ctx") > 0))
    bias_ref[...] = jnp.where(valid, 0.0, -1e30)
    square_ref[...] = jnp.zeros_like(square_ref)
    factor = math.log2(math.e) / math.sqrt(HD)
    zeros, ones = jnp.zeros((rows, LANES), BF16), jnp.ones((rows, LANES), BF16)

    @pl.loop(0, channels // (LANES * per))
    def _(group):
        for n in range(per):
            head = group * per + n
            lanes = lane_block(head)
            both = jnp.concatenate([before_ref[:, lanes], k_ref[:, lanes]], axis=0)
            scores = lax.dot_general(
                q_ref[:, lanes], both, (((1,), (1,)), ((), ())), preferred_element_type=F32
            )
            scores = scores + bias_ref[...]
            top = jnp.max(scores, axis=-1, keepdims=True)
            probs = jnp.exp2((scores - top) * factor).astype(BF16)
            probs_ref[head] = probs[:, :rows]
            own = jnp.concatenate(
                [
                    jnp.concatenate([zeros, v_ref[:, lanes]], axis=0),
                    jnp.concatenate([ones, ones], axis=0),
                ],
                axis=1,
            )
            total = jnp.dot(probs, own, preferred_element_type=F32)
            inverse = 1.0 / total[:, LANES:]
            inverse_ref[:, lanes] = inverse
            out_ref[:, lanes] = total[:, :LANES] * inverse


def score(queries, keys, before, values, per):
    rows, channels = queries.shape
    flat = jax.ShapeDtypeStruct((rows, channels), F32)
    return pl.pallas_call(
        functools.partial(score_kernel, per),
        out_shape=(
            jax.ShapeDtypeStruct((channels // HD, rows, rows), BF16),
            flat,
            flat,
            jax.ShapeDtypeStruct((1, rows, LANES), F32),
        ),
        in_specs=[in_vmem()] * 4,
        out_specs=(in_vmem(),) * 4,
        scratch_shapes=[pltpu.VMEM((rows, 2 * rows), F32)],
        compiler_params=params(),
        cost_estimate=cost(
            8 * rows * rows * channels, 14 * rows * channels, 4 * rows * rows * channels // HD
        ),
        name="score",
    )(queries, keys, before, values)


def value_kernel(first, probs_ref, before_ref, own_ref, inverse_ref, square_in_ref, out_ref, square_ref):
    square = square_in_ref[0]
    for k in range(before_ref.shape[1] // LANES):
        lanes = slice((first + k) * LANES, (first + k + 1) * LANES)
        total = own_ref[:, lanes] + inverse_ref[:, lanes] * jnp.dot(
            probs_ref[first + k],
            before_ref[:, k * LANES : (k + 1) * LANES],
            preferred_element_type=F32,
        )
        out_ref[:, lanes] = total
        square = square + total * total
    square_ref[0] = square


def value_mix(first, probs, before, own, inverse, square):
    rows, channels = before.shape
    return pl.pallas_call(
        functools.partial(value_kernel, first),
        out_shape=(
            jax.ShapeDtypeStruct(own.shape, F32),
            jax.ShapeDtypeStruct((1, rows, LANES), F32),
        ),
        in_specs=[in_vmem()] * 5,
        out_specs=(in_vmem(),) * 2,
        input_output_aliases={2: 0},
        compiler_params=params(),
        cost_estimate=cost(1, 1),
        name="value_mix",
    )(probs, before, own, inverse, square)


def normalize_kernel(count, panels, pieces, with_head, *refs):
    square_refs, refs = refs[:panels], refs[panels:]
    mixed_refs, refs = refs[:count], refs[count:]
    if with_head:
        head_ref, refs = refs[0], refs[1:]
    out_refs, (held_ref, sems) = refs[:count], refs[count:]
    rows = mixed_refs[0].shape[0]
    piece = rows // pieces
    copies = []
    for n in range(count):
        square = square_refs[0][n]
        for ref in square_refs[1:]:
            square = square + ref[n]
        scale = lax.rsqrt(jnp.sum(square, axis=-1, keepdims=True) * (1.0 / CHANNELS) + 1e-06)
        for m in range(pieces):
            at = slice(m * piece, (m + 1) * piece)
            value = mixed_refs[n][at, :]
            if with_head and n == 0 and m == 0:
                value = jnp.concatenate([head_ref[...], value[8:]], axis=0)
            held_ref[n, at, :] = (value * scale[at]).astype(BF16)
            copy = pltpu.make_async_copy(
                held_ref.at[n, pl.ds(m * piece, piece)],
                out_refs[n].at[pl.ds(m * piece, piece)],
                sems.at[n, m],
            )
            copy.start()
            copies.append(copy)
    for copy in copies:
        copy.wait()


def normalize(squares, mixed, head=None, pieces=3):
    rows, channels = mixed[0].shape
    count = len(mixed)
    operands = (*squares, *mixed) + (() if head is None else (head,))
    return pl.pallas_call(
        functools.partial(normalize_kernel, count, len(squares), pieces, head is not None),
        out_shape=(jax.ShapeDtypeStruct((rows, channels), BF16),) * count,
        in_specs=[in_vmem()] * len(operands),
        out_specs=(pl.BlockSpec(memory_space=pl.ANY),) * count,
        scratch_shapes=[
            pltpu.VMEM((count, rows, channels), BF16),
            pltpu.SemaphoreType.DMA((count, pieces)),
        ],
        compiler_params=params(),
        cost_estimate=cost(1, 1),
        name="normalize",
    )(*operands)


def from_behind(value):
    count = lax.axis_size("ctx")
    return lax.ppermute(value, "ctx", [(source, source + 1) for source in range(count - 1)])


def of_panels(square):
    count = lax.axis_size("panel")
    return [square] + [
        lax.ppermute(square, "panel", [(n, (n + shift) % count) for n in range(count)])
        for shift in range(1, count)
    ]


def body(se, se_short, se_filter, mr, mr_short, raw, decay, queries, keys, values):
    last_heads = 5 * (queries.shape[1] // HD) // 16
    key_before = from_behind(keys)
    packet, mr_taps, se_taps, decay, filter_taps, most, rest = pack(
        se, mr, se_short, mr_short, decay[None, :], se_filter, values, last_heads, 4
    )
    packet = from_behind(packet)
    own, z0, se_mix, se_square, taps, heads = own_part(
        mr, se, mr_taps, se_taps, raw, decay, filter_taps, 4
    )
    most, own = lax.optimization_barrier((most, own))
    most_before = from_behind(most)
    probs, attended, inverse, square = score(queries, keys, key_before, values, 4)
    rest, attended = lax.optimization_barrier((rest, attended))
    rest_before = from_behind(rest)
    packet, attended = lax.optimization_barrier((packet, attended))
    head, mr_mix, mixed_square = mix(
        packet, own, z0, se_square, taps, heads, mr_taps, se_taps, filter_taps
    )
    se_out, mr_out = normalize(of_panels(mixed_square), (se_mix, mr_mix), head)
    most_before, se_out, mr_out = lax.optimization_barrier((most_before, se_out, mr_out))
    attended, square = value_mix(0, probs, most_before, attended, inverse, square)
    rest_before, attended = lax.optimization_barrier((rest_before, attended))
    first = most.shape[1] // HD
    attended, square = value_mix(first, probs, rest_before, attended, inverse, square)
    (attn_out,) = normalize(of_panels(square), (attended,))
    return se_out, mr_out, attn_out


def solution(mesh):
    placed = (
        P(None, "ctx", "panel"),
        P(None, None, "panel"),
        P(None, "panel"),
        P(None, "ctx", "panel"),
        P(None, None, "panel"),
        P(None, "panel"),
        P("panel"),
        P("ctx", "panel"),
        P("ctx", "panel"),
        P("ctx", "panel"),
    )
    return jax.shard_map(
        body,
        mesh=mesh,
        in_specs=placed,
        out_specs=(P("ctx", "panel"), P("ctx", "panel"), P("ctx", "panel")),
        check_vma=False,
    )
```

```python
import functools
import math

import jax
import jax.numpy as jnp
from jax import lax
from jax.experimental import pallas as pl
from jax.experimental.pallas import tpu as pltpu
from jax.sharding import PartitionSpec as P

CHANNELS = 4096
HD = 128
LSE = 7
MEDIUM_TAPS = 128
LANES = 128
F32 = jnp.float32
BF16 = jnp.bfloat16


def params(mebibytes=6):
    return pltpu.CompilerParams(vmem_limit_bytes=mebibytes * 1024 * 1024)


def in_vmem():
    return pl.BlockSpec(memory_space=pltpu.VMEM)


def cost(flops, nbytes, trans=0):
    return pl.CostEstimate(flops=int(flops), bytes_accessed=int(nbytes), transcendentals=int(trans))


def roll(value, shift):
    shift = shift % value.shape[0]
    return pltpu.roll(value, shift, 0) if shift else value


def row_is(rows, at):
    return lax.broadcasted_iota(jnp.int32, (rows, LANES), 0) == at


def features(u, front, taps):
    ext = jnp.concatenate([front, u], axis=0)
    total = taps[0] * ext
    for j in range(1, len(taps)):
        total = total + taps[j] * roll(ext, j)
    return total[8:]


def tap_rows(ref, stream, lanes):
    return [ref[stream, j : j + 1, lanes] for j in range(ref.shape[1])]


def lane_block(k):
    return pl.ds(pl.multiple_of(k * LANES, LANES), LANES)


def tap_tile(held_ref, j):
    return jnp.broadcast_to(held_ref[j : j + 1, :], (8, LANES))


def pack_kernel(
    per,
    mr_ref,
    se_ref,
    mr_short_ref,
    se_short_ref,
    decay_hbm_ref,
    filter_hbm_ref,
    values_ref,
    out_ref,
    mw_ref,
    sw_ref,
    decay_ref,
    filter_ref,
    most_ref,
    rest_ref,
    m_ref,
    tail_ref,
    last_ref,
    sems,
    late_sems,
):
    _, rows, channels = mr_ref.shape
    width = per * LANES
    chunk = MEDIUM_TAPS + 16
    nothing = jnp.zeros((8, LANES), F32)
    end = pl.ds(rows - 16, 16)
    copies = [
        pltpu.make_async_copy(mr_short_ref, mw_ref, sems.at[0]),
        pltpu.make_async_copy(se_short_ref, sw_ref, sems.at[1]),
        pltpu.make_async_copy(mr_ref.at[pl.ds(0, 1), end], tail_ref.at[pl.ds(0, 1)], sems.at[2]),
        pltpu.make_async_copy(se_ref.at[:, end], tail_ref.at[pl.ds(1, 3)], sems.at[3]),
    ]
    first = len(copies)
    for n in range(channels // width):
        at = pl.ds(n * width, width)
        copies.append(
            pltpu.make_async_copy(
                mr_ref.at[pl.ds(1, 2), :, at], m_ref.at[:, :, at], sems.at[first + n]
            )
        )
    most = most_ref.shape[1]
    late = [
        pltpu.make_async_copy(values_ref.at[:, pl.ds(0, most)], most_ref, late_sems.at[0]),
        pltpu.make_async_copy(
            values_ref.at[:, pl.ds(most, channels - most)], rest_ref, late_sems.at[1]
        ),
        pltpu.make_async_copy(decay_hbm_ref, decay_ref, late_sems.at[2]),
        pltpu.make_async_copy(filter_hbm_ref, filter_ref, late_sems.at[3]),
    ]
    for copy in copies:
        copy.start()
    for copy in copies[:first]:
        copy.wait()
    last_ref[...] = jnp.zeros_like(last_ref)

    def one(block):
        lanes = lane_block(block)
        m1 = m_ref[0, :, lanes].astype(F32)
        m2 = m_ref[1, :, lanes].astype(F32)
        z1 = features(m1, nothing, tap_rows(mw_ref, 1, lanes))
        z2 = features(m2, nothing, tap_rows(mw_ref, 2, lanes))
        product = (z1 * z2)[rows - MEDIUM_TAPS :]
        tail_m0 = tail_ref[0, :, lanes].astype(F32)[8:]
        tail_m1, tail_m2 = m1[rows - 8 :], m2[rows - 8 :]
        head = jnp.where(row_is(8, 0), roll(tail_m2, 2), product[:8])
        product = jnp.concatenate([head, product[8:]], axis=0)
        s0 = tail_ref[1, :, lanes].astype(F32)[8:]
        s1 = tail_ref[2, :, lanes].astype(F32)
        s2 = tail_ref[3, :, lanes].astype(F32)
        y1 = features(s1, nothing, tap_rows(sw_ref, 1, lanes))[8:]
        y2 = features(s2, nothing, tap_rows(sw_ref, 2, lanes))[8:]
        at = lax.broadcasted_iota(jnp.int32, (8, LANES), 0)
        x1 = jnp.where(at < 2, roll(s0, 2), y1 * y2)
        x2 = jnp.where(
            at < 2,
            roll(s1[8:], 2),
            jnp.where(at < 4, roll(s2[8:], 4), jnp.where(at < 6, roll(tail_m0, 6), tail_m1)),
        )
        start = pl.multiple_of(block * chunk, 16)
        out_ref[pl.ds(start, MEDIUM_TAPS), :] = product.astype(BF16)
        out_ref[pl.ds(start + MEDIUM_TAPS, 16), :] = jnp.concatenate([x1, x2], axis=0).astype(BF16)
        last_ref[pl.ds(block, 1), :] = tail_m2[7:8]

    for n in range(channels // width):
        copies[first + n].wait()
        if n == 0:
            for copy in late:
                copy.start()
        pl.loop(n * per, (n + 1) * per)(one)

    out_ref[out_ref.shape[0] - 16 :, :] = last_ref[...].astype(BF16)
    for copy in late:
        copy.wait()


def pack(se, mr, se_short, mr_short, decay, se_filter, values, last_heads, per):
    _, rows, channels = se.shape
    blocks = channels // LANES
    total = blocks * (MEDIUM_TAPS + 16) + 16
    rest = last_heads * HD
    operands = (mr, se, mr_short, se_short, decay, se_filter, values)
    return pl.pallas_call(
        functools.partial(pack_kernel, per),
        out_shape=(
            jax.ShapeDtypeStruct((total, LANES), BF16),
            jax.ShapeDtypeStruct(mr_short.shape, F32),
            jax.ShapeDtypeStruct(se_short.shape, F32),
            jax.ShapeDtypeStruct(decay.shape, F32),
            jax.ShapeDtypeStruct(se_filter.shape, F32),
            jax.ShapeDtypeStruct((rows, channels - rest), BF16),
            jax.ShapeDtypeStruct((rows, rest), BF16),
        ),
        in_specs=[pl.BlockSpec(memory_space=pltpu.HBM)] * 7,
        out_specs=(in_vmem(),) * 7,
        scratch_shapes=[
            pltpu.VMEM((2, rows, channels), BF16),
            pltpu.VMEM((4, 16, channels), BF16),
            pltpu.VMEM((16, LANES), F32),
            pltpu.SemaphoreType.DMA((4 + blocks // per,)),
            pltpu.SemaphoreType.DMA((4,)),
        ],
        compiler_params=params(),
        cost_estimate=cost(20 * rows * channels, 10 * rows * channels),
        name="pack",
    )(*(pltpu.with_memory_space_constraint(x, pltpu.HBM) for x in operands))


def own_kernel(
    per,
    m_hbm_ref,
    s_hbm_ref,
    raw_hbm_ref,
    mw_ref,
    sw_ref,
    decay_ref,
    filter_ref,
    own_ref,
    z0_ref,
    se_ref,
    square_ref,
    taps_ref,
    heads_ref,
    m_ref,
    s_ref,
    raw_ref,
    held_ref,
    sems,
):
    rows, channels = own_ref.shape
    tiles = rows // 8
    width = per * LANES
    nothing = jnp.zeros((8, LANES), F32)

    def fetch(n):
        at = pl.ds(pl.multiple_of(n * width, width), width)
        return (
            pltpu.make_async_copy(s_hbm_ref.at[:, :, at], s_ref.at[:, :, at], sems.at[0, n]),
            pltpu.make_async_copy(m_hbm_ref.at[:, :, at], m_ref.at[:, :, at], sems.at[1, n]),
            pltpu.make_async_copy(raw_hbm_ref.at[:, at], raw_ref.at[:, at], sems.at[2, n]),
        )

    for n in range(channels // width):
        for copy in fetch(n):
            copy.start()
    square_ref[...] = jnp.zeros_like(square_ref)

    @pl.loop(0, channels // LANES)
    def _(k):
        @pl.when(k % per == 0)
        def _():
            for copy in fetch(k // per):
                copy.wait()

        lanes = lane_block(k)
        u = [s_ref[n, :, lanes].astype(F32) for n in range(3)]
        for n in range(3):
            heads_ref[n, :, lanes] = u[n][:8]
        s = [features(u[n], nothing, tap_rows(sw_ref, n, lanes)) for n in range(3)]
        ext = jnp.concatenate([nothing, (s[1] * s[2]).astype(BF16).astype(F32)], axis=0)
        total = filter_ref[0:1, lanes] * ext
        for j in range(1, LSE):
            total = total + filter_ref[j : j + 1, lanes] * roll(ext, j)
        mixed = s[0] * total[8:]
        se_ref[:, lanes] = mixed
        square_ref[8:, :] += mixed[8:] * mixed[8:]

        steps = lax.broadcasted_iota(jnp.int32, (MEDIUM_TAPS, LANES), 0).astype(F32)
        taps = raw_ref[:, lanes] * jnp.exp(-decay_ref[0:1, lanes] * steps)
        held_ref[...] = taps
        taps_ref[:, lanes] = taps
        u = [m_ref[n, :, lanes].astype(F32) for n in range(3)]
        for n in range(3):
            heads_ref[3 + n, :, lanes] = u[n][:8]
        z = [features(u[n], nothing, tap_rows(mw_ref, n, lanes)) for n in range(3)]
        z0_ref[:, lanes] = z[0]
        product = (z[1] * z[2]).astype(BF16).astype(F32)
        at = lax.broadcasted_iota(jnp.int32, (8, LANES), 0)
        head = jnp.where(at < 2, 0.0, product[:8])
        ext = jnp.concatenate([nothing, head, product[8:]], axis=0)
        total = [None] * tiles
        for r in range(8):
            shifted = roll(ext, r)
            tap = [tap_tile(held_ref, 8 * a + r) for a in range(MEDIUM_TAPS // 8)]
            for i in range(tiles):
                for a in range(min(i + 1, MEDIUM_TAPS // 8)):
                    at_tile = 8 * (i - a + 1)
                    term = tap[a] * shifted[at_tile : at_tile + 8]
                    total[i] = term if total[i] is None else total[i] + term
        own_ref[:, lanes] = jnp.concatenate(total, axis=0)


def own_part(mr, se, mr_short, se_short, raw, decay, se_filter, per):
    _, rows, channels = mr.shape
    mixed = jax.ShapeDtypeStruct((rows, channels), F32)
    mr, se, raw = (pltpu.with_memory_space_constraint(x, pltpu.HBM) for x in (mr, se, raw))
    return pl.pallas_call(
        functools.partial(own_kernel, per),
        out_shape=(
            mixed,
            mixed,
            mixed,
            jax.ShapeDtypeStruct((rows, LANES), F32),
            jax.ShapeDtypeStruct((MEDIUM_TAPS, channels), F32),
            jax.ShapeDtypeStruct((6, 8, channels), F32),
        ),
        in_specs=[pl.BlockSpec(memory_space=pltpu.HBM)] * 3 + [in_vmem()] * 4,
        out_specs=(in_vmem(),) * 6,
        scratch_shapes=[
            pltpu.VMEM(mr.shape, BF16),
            pltpu.VMEM(se.shape, BF16),
            pltpu.VMEM((MEDIUM_TAPS, channels), F32),
            pltpu.VMEM((MEDIUM_TAPS, LANES), F32),
            pltpu.SemaphoreType.DMA((3, channels // (per * LANES))),
        ],
        compiler_params=params(10),
        cost_estimate=cost(180 * rows * channels, 24 * rows * channels),
        name="own_part",
    )(mr, se, raw, mr_short, se_short, decay, se_filter)


def mix_kernel(
    packet_ref,
    own_ref,
    z0_ref,
    se_square_ref,
    taps_ref,
    heads_ref,
    mw_ref,
    sw_ref,
    filter_ref,
    head_ref,
    mr_ref,
    square_ref,
    last_ref,
    held_ref,
):
    rows, channels = own_ref.shape
    tiles = rows // 8
    chunk = MEDIUM_TAPS + 16
    nothing = jnp.zeros((8, LANES), F32)
    last_ref[...] = packet_ref[packet_ref.shape[0] - 16 :, :].astype(F32)
    square_ref[0] = se_square_ref[...]
    square_ref[1] = jnp.zeros((rows, LANES), F32)

    @pl.loop(0, channels // LANES)
    def _(k):
        lanes = lane_block(k)
        start = pl.multiple_of(k * chunk, 16)
        before = packet_ref[pl.ds(start, MEDIUM_TAPS), :].astype(F32)
        x = packet_ref[pl.ds(start + MEDIUM_TAPS, 16), :].astype(F32)
        x1, x2 = x[:8], x[8:]
        last = last_ref[pl.ds(k, 1), :]

        fronts = (roll(x1, 6), roll(x2, 6), roll(x2, 4))
        s = [
            features(heads_ref[n, :, lanes], fronts[n], tap_rows(sw_ref, n, lanes))
            for n in range(3)
        ]
        ext = jnp.concatenate([x1, (s[1] * s[2]).astype(BF16).astype(F32)], axis=0)
        total = filter_ref[0:1, lanes] * ext
        for j in range(1, LSE):
            total = total + filter_ref[j : j + 1, lanes] * roll(ext, j)
        mixed = s[0] * total[8:]
        head_ref[:, lanes] = mixed
        square_ref[0, :8, :] += mixed * mixed

        taps = taps_ref[:, lanes]
        held_ref[...] = taps
        front2 = jnp.where(row_is(8, 7), last, roll(before[:8], 6))
        fronts = (roll(x2, 2), x2, front2)
        z = [
            features(heads_ref[3 + n, :, lanes], fronts[n], tap_rows(mw_ref, n, lanes))
            for n in range(3)
        ]
        first = (z[1] * z[2]).astype(BF16).astype(F32)
        padded = jnp.concatenate([taps, jnp.zeros((rows - MEDIUM_TAPS, LANES), F32)], axis=0)
        base = own_ref[:, lanes] + padded * first[0:1] + roll(padded, 1) * first[1:2]
        total = [base[8 * i : 8 * i + 8] for i in range(tiles)]
        ext = jnp.concatenate([before, nothing], axis=0)
        count = MEDIUM_TAPS // 8
        for r in range(8):
            shifted = roll(ext, r)
            tap = [tap_tile(held_ref, 8 * a + r) for a in range(count)]
            for i in range(count):
                for a in range(i if r else i + 1, count):
                    at_tile = 8 * (i - a + count)
                    total[i] = total[i] + tap[a] * shifted[at_tile : at_tile + 8]
        z0 = jnp.concatenate([z[0], z0_ref[8:, lanes]], axis=0)
        mixed = z0 * jnp.concatenate(total, axis=0)
        mr_ref[:, lanes] = mixed
        square_ref[1] += mixed * mixed


def mix(packet, own, z0, se_square, taps, heads, mr_short, se_short, se_filter):
    rows, channels = own.shape
    return pl.pallas_call(
        mix_kernel,
        out_shape=(
            jax.ShapeDtypeStruct((8, channels), F32),
            jax.ShapeDtypeStruct((rows, channels), F32),
            jax.ShapeDtypeStruct((2, rows, LANES), F32),
        ),
        in_specs=[in_vmem()] * 9,
        out_specs=(in_vmem(),) * 3,
        scratch_shapes=[pltpu.VMEM((16, LANES), F32), pltpu.VMEM((MEDIUM_TAPS, LANES), F32)],
        compiler_params=params(),
        cost_estimate=cost(1, 1),
        name="mix",
    )(packet, own, z0, se_square, taps, heads, mr_short, se_short, se_filter)


def score_kernel(
    per, q_ref, k_ref, before_ref, v_ref, probs_ref, out_ref, inverse_ref, square_ref, bias_ref
):
    rows, channels = q_ref.shape
    at = lax.broadcasted_iota(jnp.int32, (rows, 2 * rows), 0)
    key = lax.broadcasted_iota(jnp.int32, (rows, 2 * rows), 1)
    valid = (key <= at + rows) & ((key >= rows) | (lax.axis_index("ctx") > 0))
    bias_ref[...] = jnp.where(valid, 0.0, -1e30)
    square_ref[...] = jnp.zeros_like(square_ref)
    factor = math.log2(math.e) / math.sqrt(HD)
    zeros, ones = jnp.zeros((rows, LANES), BF16), jnp.ones((rows, LANES), BF16)

    @pl.loop(0, channels // (LANES * per))
    def _(group):
        for n in range(per):
            head = group * per + n
            lanes = lane_block(head)
            both = jnp.concatenate([before_ref[:, lanes], k_ref[:, lanes]], axis=0)
            scores = lax.dot_general(
                q_ref[:, lanes], both, (((1,), (1,)), ((), ())), preferred_element_type=F32
            )
            scores = scores + bias_ref[...]
            top = jnp.max(scores, axis=-1, keepdims=True)
            probs = jnp.exp2((scores - top) * factor).astype(BF16)
            probs_ref[head] = probs[:, :rows]
            own = jnp.concatenate(
                [
                    jnp.concatenate([zeros, v_ref[:, lanes]], axis=0),
                    jnp.concatenate([ones, ones], axis=0),
                ],
                axis=1,
            )
            total = jnp.dot(probs, own, preferred_element_type=F32)
            inverse = 1.0 / total[:, LANES:]
            inverse_ref[:, lanes] = inverse
            out_ref[:, lanes] = total[:, :LANES] * inverse


def score(queries, keys, before, values, per):
    rows, channels = queries.shape
    flat = jax.ShapeDtypeStruct((rows, channels), F32)
    return pl.pallas_call(
        functools.partial(score_kernel, per),
        out_shape=(
            jax.ShapeDtypeStruct((channels // HD, rows, rows), BF16),
            flat,
            flat,
            jax.ShapeDtypeStruct((1, rows, LANES), F32),
        ),
        in_specs=[in_vmem()] * 4,
        out_specs=(in_vmem(),) * 4,
        scratch_shapes=[pltpu.VMEM((rows, 2 * rows), F32)],
        compiler_params=params(),
        cost_estimate=cost(
            8 * rows * rows * channels, 14 * rows * channels, 4 * rows * rows * channels // HD
        ),
        name="score",
    )(queries, keys, before, values)


def value_kernel(first, probs_ref, before_ref, own_ref, inverse_ref, square_in_ref, out_ref, square_ref):
    square = square_in_ref[0]
    for k in range(before_ref.shape[1] // LANES):
        lanes = slice((first + k) * LANES, (first + k + 1) * LANES)
        total = own_ref[:, lanes] + inverse_ref[:, lanes] * jnp.dot(
            probs_ref[first + k],
            before_ref[:, k * LANES : (k + 1) * LANES],
            preferred_element_type=F32,
        )
        out_ref[:, lanes] = total
        square = square + total * total
    square_ref[0] = square


def value_mix(first, probs, before, own, inverse, square):
    rows, channels = before.shape
    return pl.pallas_call(
        functools.partial(value_kernel, first),
        out_shape=(
            jax.ShapeDtypeStruct(own.shape, F32),
            jax.ShapeDtypeStruct((1, rows, LANES), F32),
        ),
        in_specs=[in_vmem()] * 5,
        out_specs=(in_vmem(),) * 2,
        input_output_aliases={2: 0},
        compiler_params=params(),
        cost_estimate=cost(1, 1),
        name="value_mix",
    )(probs, before, own, inverse, square)


def normalize_kernel(count, panels, pieces, with_head, *refs):
    square_refs, refs = refs[:panels], refs[panels:]
    mixed_refs, refs = refs[:count], refs[count:]
    if with_head:
        head_ref, refs = refs[0], refs[1:]
    out_refs, (held_ref, sems) = refs[:count], refs[count:]
    rows = mixed_refs[0].shape[0]
    piece = rows // pieces
    copies = []
    for n in range(count):
        square = square_refs[0][n]
        for ref in square_refs[1:]:
            square = square + ref[n]
        scale = lax.rsqrt(jnp.sum(square, axis=-1, keepdims=True) * (1.0 / CHANNELS) + 1e-06)
        for m in range(pieces):
            at = slice(m * piece, (m + 1) * piece)
            value = mixed_refs[n][at, :]
            if with_head and n == 0 and m == 0:
                value = jnp.concatenate([head_ref[...], value[8:]], axis=0)
            held_ref[n, at, :] = (value * scale[at]).astype(BF16)
            copy = pltpu.make_async_copy(
                held_ref.at[n, pl.ds(m * piece, piece)],
                out_refs[n].at[pl.ds(m * piece, piece)],
                sems.at[n, m],
            )
            copy.start()
            copies.append(copy)
    for copy in copies:
        copy.wait()


def normalize(squares, mixed, head=None, pieces=3):
    rows, channels = mixed[0].shape
    count = len(mixed)
    operands = (*squares, *mixed) + (() if head is None else (head,))
    return pl.pallas_call(
        functools.partial(normalize_kernel, count, len(squares), pieces, head is not None),
        out_shape=(jax.ShapeDtypeStruct((rows, channels), BF16),) * count,
        in_specs=[in_vmem()] * len(operands),
        out_specs=(pl.BlockSpec(memory_space=pl.ANY),) * count,
        scratch_shapes=[
            pltpu.VMEM((count, rows, channels), BF16),
            pltpu.SemaphoreType.DMA((count, pieces)),
        ],
        compiler_params=params(),
        cost_estimate=cost(1, 1),
        name="normalize",
    )(*operands)


def from_behind(value):
    count = lax.axis_size("ctx")
    return lax.ppermute(value, "ctx", [(source, source + 1) for source in range(count - 1)])


def of_panels(square):
    count = lax.axis_size("panel")
    return [square] + [
        lax.ppermute(square, "panel", [(n, (n + shift) % count) for n in range(count)])
        for shift in range(1, count)
    ]


def body(se, se_short, se_filter, mr, mr_short, raw, decay, queries, keys, values):
    last_heads = 3 * (queries.shape[1] // HD) // 8
    key_before = from_behind(keys)
    packet, mr_taps, se_taps, decay, filter_taps, most, rest = pack(
        se, mr, se_short, mr_short, decay[None, :], se_filter, values, last_heads, 4
    )
    packet = from_behind(packet)
    own, z0, se_mix, se_square, taps, heads = own_part(
        mr, se, mr_taps, se_taps, raw, decay, filter_taps, 4
    )
    most, own = lax.optimization_barrier((most, own))
    most_before = from_behind(most)
    probs, attended, inverse, square = score(queries, keys, key_before, values, 4)
    rest, attended = lax.optimization_barrier((rest, attended))
    rest_before = from_behind(rest)
    packet, attended = lax.optimization_barrier((packet, attended))
    head, mr_mix, mixed_square = mix(
        packet, own, z0, se_square, taps, heads, mr_taps, se_taps, filter_taps
    )
    se_out, mr_out = normalize(of_panels(mixed_square), (se_mix, mr_mix), head)
    most_before, se_out, mr_out = lax.optimization_barrier((most_before, se_out, mr_out))
    attended, square = value_mix(0, probs, most_before, attended, inverse, square)
    rest_before, attended = lax.optimization_barrier((rest_before, attended))
    first = most.shape[1] // HD
    attended, square = value_mix(first, probs, rest_before, attended, inverse, square)
    (attn_out,) = normalize(of_panels(square), (attended,))
    return se_out, mr_out, attn_out


def solution(mesh):
    placed = (
        P(None, "ctx", "panel"),
        P(None, None, "panel"),
        P(None, "panel"),
        P(None, "ctx", "panel"),
        P(None, None, "panel"),
        P(None, "panel"),
        P("panel"),
        P("ctx", "panel"),
        P("ctx", "panel"),
        P("ctx", "panel"),
    )
    return jax.shard_map(
        body,
        mesh=mesh,
        in_specs=placed,
        out_specs=(P("ctx", "panel"), P("ctx", "panel"), P("ctx", "panel")),
        check_vma=False,
    )
```

```python
import functools
import math

import jax
import jax.numpy as jnp
from jax import lax
from jax.experimental import pallas as pl
from jax.experimental.pallas import tpu as pltpu
from jax.sharding import PartitionSpec as P

CHANNELS = 4096
HD = 128
LSE = 7
MEDIUM_TAPS = 128
LANES = 128
F32 = jnp.float32
BF16 = jnp.bfloat16


def params(mebibytes=6):
    return pltpu.CompilerParams(vmem_limit_bytes=mebibytes * 1024 * 1024)


def in_vmem():
    return pl.BlockSpec(memory_space=pltpu.VMEM)


def cost(flops, nbytes, trans=0):
    return pl.CostEstimate(flops=int(flops), bytes_accessed=int(nbytes), transcendentals=int(trans))


def roll(value, shift):
    shift = shift % value.shape[0]
    return pltpu.roll(value, shift, 0) if shift else value


def row_is(rows, at):
    return lax.broadcasted_iota(jnp.int32, (rows, LANES), 0) == at


def features(u, front, taps):
    ext = jnp.concatenate([front, u], axis=0)
    total = taps[0] * ext
    for j in range(1, len(taps)):
        total = total + taps[j] * roll(ext, j)
    return total[8:]


def tap_rows(ref, stream, lanes):
    return [ref[stream, j : j + 1, lanes] for j in range(ref.shape[1])]


def lane_block(k):
    return pl.ds(pl.multiple_of(k * LANES, LANES), LANES)


def tap_tile(held_ref, j):
    return jnp.broadcast_to(held_ref[j : j + 1, :], (8, LANES))


def pack_kernel(
    per,
    mr_ref,
    se_ref,
    mr_short_ref,
    se_short_ref,
    decay_hbm_ref,
    filter_hbm_ref,
    values_ref,
    out_ref,
    mw_ref,
    sw_ref,
    decay_ref,
    filter_ref,
    most_ref,
    rest_ref,
    m_ref,
    tail_ref,
    last_ref,
    sems,
    late_sems,
):
    _, rows, channels = mr_ref.shape
    width = per * LANES
    chunk = MEDIUM_TAPS + 16
    nothing = jnp.zeros((8, LANES), F32)
    end = pl.ds(rows - 16, 16)
    copies = [
        pltpu.make_async_copy(mr_short_ref, mw_ref, sems.at[0]),
        pltpu.make_async_copy(se_short_ref, sw_ref, sems.at[1]),
        pltpu.make_async_copy(mr_ref.at[pl.ds(0, 1), end], tail_ref.at[pl.ds(0, 1)], sems.at[2]),
        pltpu.make_async_copy(se_ref.at[:, end], tail_ref.at[pl.ds(1, 3)], sems.at[3]),
    ]
    first = len(copies)
    for n in range(channels // width):
        at = pl.ds(n * width, width)
        copies.append(
            pltpu.make_async_copy(
                mr_ref.at[pl.ds(1, 2), :, at], m_ref.at[:, :, at], sems.at[first + n]
            )
        )
    most = most_ref.shape[1]
    late = [
        pltpu.make_async_copy(values_ref.at[:, pl.ds(0, most)], most_ref, late_sems.at[0]),
        pltpu.make_async_copy(
            values_ref.at[:, pl.ds(most, channels - most)], rest_ref, late_sems.at[1]
        ),
        pltpu.make_async_copy(decay_hbm_ref, decay_ref, late_sems.at[2]),
        pltpu.make_async_copy(filter_hbm_ref, filter_ref, late_sems.at[3]),
    ]
    for copy in copies:
        copy.start()
    for copy in copies[:first]:
        copy.wait()
    last_ref[...] = jnp.zeros_like(last_ref)

    def one(block):
        lanes = lane_block(block)
        m1 = m_ref[0, :, lanes].astype(F32)
        m2 = m_ref[1, :, lanes].astype(F32)
        z1 = features(m1, nothing, tap_rows(mw_ref, 1, lanes))
        z2 = features(m2, nothing, tap_rows(mw_ref, 2, lanes))
        product = (z1 * z2)[rows - MEDIUM_TAPS :]
        tail_m0 = tail_ref[0, :, lanes].astype(F32)[8:]
        tail_m1, tail_m2 = m1[rows - 8 :], m2[rows - 8 :]
        head = jnp.where(row_is(8, 0), roll(tail_m2, 2), product[:8])
        product = jnp.concatenate([head, product[8:]], axis=0)
        s0 = tail_ref[1, :, lanes].astype(F32)[8:]
        s1 = tail_ref[2, :, lanes].astype(F32)
        s2 = tail_ref[3, :, lanes].astype(F32)
        y1 = features(s1, nothing, tap_rows(sw_ref, 1, lanes))[8:]
        y2 = features(s2, nothing, tap_rows(sw_ref, 2, lanes))[8:]
        at = lax.broadcasted_iota(jnp.int32, (8, LANES), 0)
        x1 = jnp.where(at < 2, roll(s0, 2), y1 * y2)
        x2 = jnp.where(
            at < 2,
            roll(s1[8:], 2),
            jnp.where(at < 4, roll(s2[8:], 4), jnp.where(at < 6, roll(tail_m0, 6), tail_m1)),
        )
        start = pl.multiple_of(block * chunk, 16)
        out_ref[pl.ds(start, MEDIUM_TAPS), :] = product.astype(BF16)
        out_ref[pl.ds(start + MEDIUM_TAPS, 16), :] = jnp.concatenate([x1, x2], axis=0).astype(BF16)
        last_ref[pl.ds(block, 1), :] = tail_m2[7:8]

    for n in range(channels // width):
        copies[first + n].wait()
        if n == 0:
            for copy in late:
                copy.start()
        pl.loop(n * per, (n + 1) * per)(one)

    out_ref[out_ref.shape[0] - 16 :, :] = last_ref[...].astype(BF16)
    for copy in late:
        copy.wait()


def pack(se, mr, se_short, mr_short, decay, se_filter, values, last_heads, per):
    _, rows, channels = se.shape
    blocks = channels // LANES
    total = blocks * (MEDIUM_TAPS + 16) + 16
    rest = last_heads * HD
    operands = (mr, se, mr_short, se_short, decay, se_filter, values)
    return pl.pallas_call(
        functools.partial(pack_kernel, per),
        out_shape=(
            jax.ShapeDtypeStruct((total, LANES), BF16),
            jax.ShapeDtypeStruct(mr_short.shape, F32),
            jax.ShapeDtypeStruct(se_short.shape, F32),
            jax.ShapeDtypeStruct(decay.shape, F32),
            jax.ShapeDtypeStruct(se_filter.shape, F32),
            jax.ShapeDtypeStruct((rows, channels - rest), BF16),
            jax.ShapeDtypeStruct((rows, rest), BF16),
        ),
        in_specs=[pl.BlockSpec(memory_space=pltpu.HBM)] * 7,
        out_specs=(in_vmem(),) * 7,
        scratch_shapes=[
            pltpu.VMEM((2, rows, channels), BF16),
            pltpu.VMEM((4, 16, channels), BF16),
            pltpu.VMEM((16, LANES), F32),
            pltpu.SemaphoreType.DMA((4 + blocks // per,)),
            pltpu.SemaphoreType.DMA((4,)),
        ],
        compiler_params=params(),
        cost_estimate=cost(20 * rows * channels, 10 * rows * channels),
        name="pack",
    )(*(pltpu.with_memory_space_constraint(x, pltpu.HBM) for x in operands))


def own_kernel(
    per,
    m_hbm_ref,
    s_hbm_ref,
    raw_hbm_ref,
    mw_ref,
    sw_ref,
    decay_ref,
    filter_ref,
    own_ref,
    z0_ref,
    se_ref,
    square_ref,
    taps_ref,
    heads_ref,
    m_ref,
    s_ref,
    raw_ref,
    held_ref,
    sems,
):
    rows, channels = own_ref.shape
    tiles = rows // 8
    width = per * LANES
    nothing = jnp.zeros((8, LANES), F32)

    def fetch(n):
        at = pl.ds(pl.multiple_of(n * width, width), width)
        return (
            pltpu.make_async_copy(s_hbm_ref.at[:, :, at], s_ref.at[:, :, at], sems.at[0, n]),
            pltpu.make_async_copy(m_hbm_ref.at[:, :, at], m_ref.at[:, :, at], sems.at[1, n]),
            pltpu.make_async_copy(raw_hbm_ref.at[:, at], raw_ref.at[:, at], sems.at[2, n]),
        )

    for n in range(channels // width):
        for copy in fetch(n):
            copy.start()
    square_ref[...] = jnp.zeros_like(square_ref)

    @pl.loop(0, channels // LANES)
    def _(k):
        @pl.when(k % per == 0)
        def _():
            for copy in fetch(k // per):
                copy.wait()

        lanes = lane_block(k)
        u = [s_ref[n, :, lanes].astype(F32) for n in range(3)]
        for n in range(3):
            heads_ref[n, :, lanes] = u[n][:8]
        s = [features(u[n], nothing, tap_rows(sw_ref, n, lanes)) for n in range(3)]
        ext = jnp.concatenate([nothing, (s[1] * s[2]).astype(BF16).astype(F32)], axis=0)
        total = filter_ref[0:1, lanes] * ext
        for j in range(1, LSE):
            total = total + filter_ref[j : j + 1, lanes] * roll(ext, j)
        mixed = s[0] * total[8:]
        se_ref[:, lanes] = mixed
        square_ref[8:, :] += mixed[8:] * mixed[8:]

        steps = lax.broadcasted_iota(jnp.int32, (MEDIUM_TAPS, LANES), 0).astype(F32)
        taps = raw_ref[:, lanes] * jnp.exp(-decay_ref[0:1, lanes] * steps)
        held_ref[...] = taps
        taps_ref[:, lanes] = taps
        u = [m_ref[n, :, lanes].astype(F32) for n in range(3)]
        for n in range(3):
            heads_ref[3 + n, :, lanes] = u[n][:8]
        z = [features(u[n], nothing, tap_rows(mw_ref, n, lanes)) for n in range(3)]
        z0_ref[:, lanes] = z[0]
        product = (z[1] * z[2]).astype(BF16).astype(F32)
        at = lax.broadcasted_iota(jnp.int32, (8, LANES), 0)
        head = jnp.where(at < 2, 0.0, product[:8])
        ext = jnp.concatenate([nothing, head, product[8:]], axis=0)
        total = [None] * tiles
        for r in range(8):
            shifted = roll(ext, r)
            tap = [tap_tile(held_ref, 8 * a + r) for a in range(MEDIUM_TAPS // 8)]
            for i in range(tiles):
                for a in range(min(i + 1, MEDIUM_TAPS // 8)):
                    at_tile = 8 * (i - a + 1)
                    term = tap[a] * shifted[at_tile : at_tile + 8]
                    total[i] = term if total[i] is None else total[i] + term
        own_ref[:, lanes] = jnp.concatenate(total, axis=0)


def own_part(mr, se, mr_short, se_short, raw, decay, se_filter, per):
    _, rows, channels = mr.shape
    mixed = jax.ShapeDtypeStruct((rows, channels), F32)
    mr, se, raw = (pltpu.with_memory_space_constraint(x, pltpu.HBM) for x in (mr, se, raw))
    return pl.pallas_call(
        functools.partial(own_kernel, per),
        out_shape=(
            mixed,
            mixed,
            mixed,
            jax.ShapeDtypeStruct((rows, LANES), F32),
            jax.ShapeDtypeStruct((MEDIUM_TAPS, channels), F32),
            jax.ShapeDtypeStruct((6, 8, channels), F32),
        ),
        in_specs=[pl.BlockSpec(memory_space=pltpu.HBM)] * 3 + [in_vmem()] * 4,
        out_specs=(in_vmem(),) * 6,
        scratch_shapes=[
            pltpu.VMEM(mr.shape, BF16),
            pltpu.VMEM(se.shape, BF16),
            pltpu.VMEM((MEDIUM_TAPS, channels), F32),
            pltpu.VMEM((MEDIUM_TAPS, LANES), F32),
            pltpu.SemaphoreType.DMA((3, channels // (per * LANES))),
        ],
        compiler_params=params(10),
        cost_estimate=cost(180 * rows * channels, 24 * rows * channels),
        name="own_part",
    )(mr, se, raw, mr_short, se_short, decay, se_filter)


def mix_kernel(
    packet_ref,
    own_ref,
    z0_ref,
    se_square_ref,
    taps_ref,
    heads_ref,
    mw_ref,
    sw_ref,
    filter_ref,
    head_ref,
    mr_ref,
    square_ref,
    last_ref,
    held_ref,
):
    rows, channels = own_ref.shape
    tiles = rows // 8
    chunk = MEDIUM_TAPS + 16
    nothing = jnp.zeros((8, LANES), F32)
    last_ref[...] = packet_ref[packet_ref.shape[0] - 16 :, :].astype(F32)
    square_ref[0] = se_square_ref[...]
    square_ref[1] = jnp.zeros((rows, LANES), F32)

    @pl.loop(0, channels // LANES)
    def _(k):
        lanes = lane_block(k)
        start = pl.multiple_of(k * chunk, 16)
        before = packet_ref[pl.ds(start, MEDIUM_TAPS), :].astype(F32)
        x = packet_ref[pl.ds(start + MEDIUM_TAPS, 16), :].astype(F32)
        x1, x2 = x[:8], x[8:]
        last = last_ref[pl.ds(k, 1), :]

        fronts = (roll(x1, 6), roll(x2, 6), roll(x2, 4))
        s = [
            features(heads_ref[n, :, lanes], fronts[n], tap_rows(sw_ref, n, lanes))
            for n in range(3)
        ]
        ext = jnp.concatenate([x1, (s[1] * s[2]).astype(BF16).astype(F32)], axis=0)
        total = filter_ref[0:1, lanes] * ext
        for j in range(1, LSE):
            total = total + filter_ref[j : j + 1, lanes] * roll(ext, j)
        mixed = s[0] * total[8:]
        head_ref[:, lanes] = mixed
        square_ref[0, :8, :] += mixed * mixed

        taps = taps_ref[:, lanes]
        held_ref[...] = taps
        front2 = jnp.where(row_is(8, 7), last, roll(before[:8], 6))
        fronts = (roll(x2, 2), x2, front2)
        z = [
            features(heads_ref[3 + n, :, lanes], fronts[n], tap_rows(mw_ref, n, lanes))
            for n in range(3)
        ]
        first = (z[1] * z[2]).astype(BF16).astype(F32)
        padded = jnp.concatenate([taps, jnp.zeros((rows - MEDIUM_TAPS, LANES), F32)], axis=0)
        base = own_ref[:, lanes] + padded * first[0:1] + roll(padded, 1) * first[1:2]
        total = [base[8 * i : 8 * i + 8] for i in range(tiles)]
        ext = jnp.concatenate([before, nothing], axis=0)
        count = MEDIUM_TAPS // 8
        for r in range(8):
            shifted = roll(ext, r)
            tap = [tap_tile(held_ref, 8 * a + r) for a in range(count)]
            for i in range(count):
                for a in range(i if r else i + 1, count):
                    at_tile = 8 * (i - a + count)
                    total[i] = total[i] + tap[a] * shifted[at_tile : at_tile + 8]
        z0 = jnp.concatenate([z[0], z0_ref[8:, lanes]], axis=0)
        mixed = z0 * jnp.concatenate(total, axis=0)
        mr_ref[:, lanes] = mixed
        square_ref[1] += mixed * mixed


def mix(packet, own, z0, se_square, taps, heads, mr_short, se_short, se_filter):
    rows, channels = own.shape
    return pl.pallas_call(
        mix_kernel,
        out_shape=(
            jax.ShapeDtypeStruct((8, channels), F32),
            jax.ShapeDtypeStruct((rows, channels), F32),
            jax.ShapeDtypeStruct((2, rows, LANES), F32),
        ),
        in_specs=[in_vmem()] * 9,
        out_specs=(in_vmem(),) * 3,
        scratch_shapes=[pltpu.VMEM((16, LANES), F32), pltpu.VMEM((MEDIUM_TAPS, LANES), F32)],
        compiler_params=params(),
        cost_estimate=cost(1, 1),
        name="mix",
    )(packet, own, z0, se_square, taps, heads, mr_short, se_short, se_filter)


def score_kernel(
    per, q_ref, k_ref, before_ref, v_ref, probs_ref, out_ref, inverse_ref, square_ref, bias_ref
):
    rows, channels = q_ref.shape
    at = lax.broadcasted_iota(jnp.int32, (rows, 2 * rows), 0)
    key = lax.broadcasted_iota(jnp.int32, (rows, 2 * rows), 1)
    valid = (key <= at + rows) & ((key >= rows) | (lax.axis_index("ctx") > 0))
    bias_ref[...] = jnp.where(valid, 0.0, -1e30)
    square_ref[...] = jnp.zeros_like(square_ref)
    factor = math.log2(math.e) / math.sqrt(HD)
    zeros, ones = jnp.zeros((rows, LANES), BF16), jnp.ones((rows, LANES), BF16)

    @pl.loop(0, channels // (LANES * per))
    def _(group):
        for n in range(per):
            head = group * per + n
            lanes = lane_block(head)
            both = jnp.concatenate([before_ref[:, lanes], k_ref[:, lanes]], axis=0)
            scores = lax.dot_general(
                q_ref[:, lanes], both, (((1,), (1,)), ((), ())), preferred_element_type=F32
            )
            scores = scores + bias_ref[...]
            top = jnp.max(scores, axis=-1, keepdims=True)
            probs = jnp.exp2((scores - top) * factor).astype(BF16)
            probs_ref[head] = probs[:, :rows]
            own = jnp.concatenate(
                [
                    jnp.concatenate([zeros, v_ref[:, lanes]], axis=0),
                    jnp.concatenate([ones, ones], axis=0),
                ],
                axis=1,
            )
            total = jnp.dot(probs, own, preferred_element_type=F32)
            inverse = 1.0 / total[:, LANES:]
            inverse_ref[:, lanes] = inverse
            out_ref[:, lanes] = total[:, :LANES] * inverse


def score(queries, keys, before, values, per):
    rows, channels = queries.shape
    flat = jax.ShapeDtypeStruct((rows, channels), F32)
    return pl.pallas_call(
        functools.partial(score_kernel, per),
        out_shape=(
            jax.ShapeDtypeStruct((channels // HD, rows, rows), BF16),
            flat,
            flat,
            jax.ShapeDtypeStruct((1, rows, LANES), F32),
        ),
        in_specs=[in_vmem()] * 4,
        out_specs=(in_vmem(),) * 4,
        scratch_shapes=[pltpu.VMEM((rows, 2 * rows), F32)],
        compiler_params=params(),
        cost_estimate=cost(
            8 * rows * rows * channels, 14 * rows * channels, 4 * rows * rows * channels // HD
        ),
        name="score",
    )(queries, keys, before, values)


def value_kernel(first, probs_ref, before_ref, own_ref, inverse_ref, square_in_ref, out_ref, square_ref):
    square = square_in_ref[0]
    for k in range(before_ref.shape[1] // LANES):
        lanes = slice((first + k) * LANES, (first + k + 1) * LANES)
        total = own_ref[:, lanes] + inverse_ref[:, lanes] * jnp.dot(
            probs_ref[first + k],
            before_ref[:, k * LANES : (k + 1) * LANES],
            preferred_element_type=F32,
        )
        out_ref[:, lanes] = total
        square = square + total * total
    square_ref[0] = square


def value_mix(first, probs, before, own, inverse, square):
    rows, channels = before.shape
    return pl.pallas_call(
        functools.partial(value_kernel, first),
        out_shape=(
            jax.ShapeDtypeStruct(own.shape, F32),
            jax.ShapeDtypeStruct((1, rows, LANES), F32),
        ),
        in_specs=[in_vmem()] * 5,
        out_specs=(in_vmem(),) * 2,
        input_output_aliases={2: 0},
        compiler_params=params(),
        cost_estimate=cost(1, 1),
        name="value_mix",
    )(probs, before, own, inverse, square)


def normalize_kernel(count, panels, pieces, with_head, *refs):
    square_refs, refs = refs[:panels], refs[panels:]
    mixed_refs, refs = refs[:count], refs[count:]
    if with_head:
        head_ref, refs = refs[0], refs[1:]
    out_refs, (held_ref, sems) = refs[:count], refs[count:]
    rows = mixed_refs[0].shape[0]
    piece = rows // pieces
    copies = []
    for n in range(count):
        square = square_refs[0][n]
        for ref in square_refs[1:]:
            square = square + ref[n]
        scale = lax.rsqrt(jnp.sum(square, axis=-1, keepdims=True) * (1.0 / CHANNELS) + 1e-06)
        for m in range(pieces):
            at = slice(m * piece, (m + 1) * piece)
            value = mixed_refs[n][at, :]
            if with_head and n == 0 and m == 0:
                value = jnp.concatenate([head_ref[...], value[8:]], axis=0)
            held_ref[n, at, :] = (value * scale[at]).astype(BF16)
            copy = pltpu.make_async_copy(
                held_ref.at[n, pl.ds(m * piece, piece)],
                out_refs[n].at[pl.ds(m * piece, piece)],
                sems.at[n, m],
            )
            copy.start()
            copies.append(copy)
    for copy in copies:
        copy.wait()


def normalize(squares, mixed, head=None, pieces=1):
    rows, channels = mixed[0].shape
    count = len(mixed)
    operands = (*squares, *mixed) + (() if head is None else (head,))
    return pl.pallas_call(
        functools.partial(normalize_kernel, count, len(squares), pieces, head is not None),
        out_shape=(jax.ShapeDtypeStruct((rows, channels), BF16),) * count,
        in_specs=[in_vmem()] * len(operands),
        out_specs=(pl.BlockSpec(memory_space=pl.ANY),) * count,
        scratch_shapes=[
            pltpu.VMEM((count, rows, channels), BF16),
            pltpu.SemaphoreType.DMA((count, pieces)),
        ],
        compiler_params=params(),
        cost_estimate=cost(1, 1),
        name="normalize",
    )(*operands)


def from_behind(value):
    count = lax.axis_size("ctx")
    return lax.ppermute(value, "ctx", [(source, source + 1) for source in range(count - 1)])


def of_panels(square):
    count = lax.axis_size("panel")
    return [square] + [
        lax.ppermute(square, "panel", [(n, (n + shift) % count) for n in range(count)])
        for shift in range(1, count)
    ]


def body(se, se_short, se_filter, mr, mr_short, raw, decay, queries, keys, values):
    last_heads = 3 * (queries.shape[1] // HD) // 8
    key_before = from_behind(keys)
    packet, mr_taps, se_taps, decay, filter_taps, most, rest = pack(
        se, mr, se_short, mr_short, decay[None, :], se_filter, values, last_heads, 4
    )
    packet = from_behind(packet)
    own, z0, se_mix, se_square, taps, heads = own_part(
        mr, se, mr_taps, se_taps, raw, decay, filter_taps, 4
    )
    most, own = lax.optimization_barrier((most, own))
    most_before = from_behind(most)
    probs, attended, inverse, square = score(queries, keys, key_before, values, 4)
    rest, attended = lax.optimization_barrier((rest, attended))
    rest_before = from_behind(rest)
    packet, attended = lax.optimization_barrier((packet, attended))
    head, mr_mix, mixed_square = mix(
        packet, own, z0, se_square, taps, heads, mr_taps, se_taps, filter_taps
    )
    se_out, mr_out = normalize(of_panels(mixed_square), (se_mix, mr_mix), head)
    most_before, se_out, mr_out = lax.optimization_barrier((most_before, se_out, mr_out))
    attended, square = value_mix(0, probs, most_before, attended, inverse, square)
    rest_before, attended = lax.optimization_barrier((rest_before, attended))
    first = most.shape[1] // HD
    attended, square = value_mix(first, probs, rest_before, attended, inverse, square)
    (attn_out,) = normalize(of_panels(square), (attended,))
    return se_out, mr_out, attn_out


def solution(mesh):
    placed = (
        P(None, "ctx", "panel"),
        P(None, None, "panel"),
        P(None, "panel"),
        P(None, "ctx", "panel"),
        P(None, None, "panel"),
        P(None, "panel"),
        P("panel"),
        P("ctx", "panel"),
        P("ctx", "panel"),
        P("ctx", "panel"),
    )
    return jax.shard_map(
        body,
        mesh=mesh,
        in_specs=placed,
        out_specs=(P("ctx", "panel"), P("ctx", "panel"), P("ctx", "panel")),
        check_vma=False,
    )
```

```python
import functools
import math

import jax
import jax.numpy as jnp
from jax import lax
from jax.experimental import pallas as pl
from jax.experimental.pallas import tpu as pltpu
from jax.sharding import PartitionSpec as P

CHANNELS = 4096
HD = 128
LSE = 7
MEDIUM_TAPS = 128
LANES = 128
F32 = jnp.float32
BF16 = jnp.bfloat16


def params(mebibytes=6):
    return pltpu.CompilerParams(vmem_limit_bytes=mebibytes * 1024 * 1024)


def in_vmem():
    return pl.BlockSpec(memory_space=pltpu.VMEM)


def cost(flops, nbytes, trans=0):
    return pl.CostEstimate(flops=int(flops), bytes_accessed=int(nbytes), transcendentals=int(trans))


def roll(value, shift):
    shift = shift % value.shape[0]
    return pltpu.roll(value, shift, 0) if shift else value


def row_is(rows, at):
    return lax.broadcasted_iota(jnp.int32, (rows, LANES), 0) == at


def features(u, front, taps):
    ext = jnp.concatenate([front, u], axis=0)
    total = taps[0] * ext
    for j in range(1, len(taps)):
        total = total + taps[j] * roll(ext, j)
    return total[8:]


def tap_rows(ref, stream, lanes):
    return [ref[stream, j : j + 1, lanes] for j in range(ref.shape[1])]


def lane_block(k):
    return pl.ds(pl.multiple_of(k * LANES, LANES), LANES)


def tap_tile(held_ref, j):
    return jnp.broadcast_to(held_ref[j : j + 1, :], (8, LANES))


def pack_kernel(
    per,
    mr_ref,
    se_ref,
    mr_short_ref,
    se_short_ref,
    decay_hbm_ref,
    filter_hbm_ref,
    values_ref,
    out_ref,
    mw_ref,
    sw_ref,
    decay_ref,
    filter_ref,
    most_ref,
    rest_ref,
    m_ref,
    tail_ref,
    last_ref,
    sems,
    late_sems,
):
    _, rows, channels = mr_ref.shape
    width = per * LANES
    chunk = MEDIUM_TAPS + 16
    nothing = jnp.zeros((8, LANES), F32)
    end = pl.ds(rows - 16, 16)
    copies = [
        pltpu.make_async_copy(mr_short_ref, mw_ref, sems.at[0]),
        pltpu.make_async_copy(se_short_ref, sw_ref, sems.at[1]),
        pltpu.make_async_copy(mr_ref.at[pl.ds(0, 1), end], tail_ref.at[pl.ds(0, 1)], sems.at[2]),
        pltpu.make_async_copy(se_ref.at[:, end], tail_ref.at[pl.ds(1, 3)], sems.at[3]),
    ]
    first = len(copies)
    for n in range(channels // width):
        at = pl.ds(n * width, width)
        copies.append(
            pltpu.make_async_copy(
                mr_ref.at[pl.ds(1, 2), :, at], m_ref.at[:, :, at], sems.at[first + n]
            )
        )
    most = most_ref.shape[1]
    late = [
        pltpu.make_async_copy(values_ref.at[:, pl.ds(0, most)], most_ref, late_sems.at[0]),
        pltpu.make_async_copy(
            values_ref.at[:, pl.ds(most, channels - most)], rest_ref, late_sems.at[1]
        ),
        pltpu.make_async_copy(decay_hbm_ref, decay_ref, late_sems.at[2]),
        pltpu.make_async_copy(filter_hbm_ref, filter_ref, late_sems.at[3]),
    ]
    for copy in copies:
        copy.start(priority=1)
    for copy in copies[:first]:
        copy.wait()
    last_ref[...] = jnp.zeros_like(last_ref)

    def one(block):
        lanes = lane_block(block)
        m1 = m_ref[0, :, lanes].astype(F32)
        m2 = m_ref[1, :, lanes].astype(F32)
        z1 = features(m1, nothing, tap_rows(mw_ref, 1, lanes))
        z2 = features(m2, nothing, tap_rows(mw_ref, 2, lanes))
        product = (z1 * z2)[rows - MEDIUM_TAPS :]
        tail_m0 = tail_ref[0, :, lanes].astype(F32)[8:]
        tail_m1, tail_m2 = m1[rows - 8 :], m2[rows - 8 :]
        head = jnp.where(row_is(8, 0), roll(tail_m2, 2), product[:8])
        product = jnp.concatenate([head, product[8:]], axis=0)
        s0 = tail_ref[1, :, lanes].astype(F32)[8:]
        s1 = tail_ref[2, :, lanes].astype(F32)
        s2 = tail_ref[3, :, lanes].astype(F32)
        y1 = features(s1, nothing, tap_rows(sw_ref, 1, lanes))[8:]
        y2 = features(s2, nothing, tap_rows(sw_ref, 2, lanes))[8:]
        at = lax.broadcasted_iota(jnp.int32, (8, LANES), 0)
        x1 = jnp.where(at < 2, roll(s0, 2), y1 * y2)
        x2 = jnp.where(
            at < 2,
            roll(s1[8:], 2),
            jnp.where(at < 4, roll(s2[8:], 4), jnp.where(at < 6, roll(tail_m0, 6), tail_m1)),
        )
        start = pl.multiple_of(block * chunk, 16)
        out_ref[pl.ds(start, MEDIUM_TAPS), :] = product.astype(BF16)
        out_ref[pl.ds(start + MEDIUM_TAPS, 16), :] = jnp.concatenate([x1, x2], axis=0).astype(BF16)
        last_ref[pl.ds(block, 1), :] = tail_m2[7:8]

    for n in range(channels // width):
        copies[first + n].wait()
        if n == 0:
            for copy in late:
                copy.start(priority=1)
        pl.loop(n * per, (n + 1) * per)(one)

    out_ref[out_ref.shape[0] - 16 :, :] = last_ref[...].astype(BF16)
    for copy in late:
        copy.wait()


def pack(se, mr, se_short, mr_short, decay, se_filter, values, last_heads, per):
    _, rows, channels = se.shape
    blocks = channels // LANES
    total = blocks * (MEDIUM_TAPS + 16) + 16
    rest = last_heads * HD
    operands = (mr, se, mr_short, se_short, decay, se_filter, values)
    return pl.pallas_call(
        functools.partial(pack_kernel, per),
        out_shape=(
            jax.ShapeDtypeStruct((total, LANES), BF16),
            jax.ShapeDtypeStruct(mr_short.shape, F32),
            jax.ShapeDtypeStruct(se_short.shape, F32),
            jax.ShapeDtypeStruct(decay.shape, F32),
            jax.ShapeDtypeStruct(se_filter.shape, F32),
            jax.ShapeDtypeStruct((rows, channels - rest), BF16),
            jax.ShapeDtypeStruct((rows, rest), BF16),
        ),
        in_specs=[pl.BlockSpec(memory_space=pltpu.HBM)] * 7,
        out_specs=(in_vmem(),) * 7,
        scratch_shapes=[
            pltpu.VMEM((2, rows, channels), BF16),
            pltpu.VMEM((4, 16, channels), BF16),
            pltpu.VMEM((16, LANES), F32),
            pltpu.SemaphoreType.DMA((4 + blocks // per,)),
            pltpu.SemaphoreType.DMA((4,)),
        ],
        compiler_params=params(),
        cost_estimate=cost(20 * rows * channels, 10 * rows * channels),
        name="pack",
    )(*(pltpu.with_memory_space_constraint(x, pltpu.HBM) for x in operands))


def own_kernel(
    per,
    m_hbm_ref,
    s_hbm_ref,
    raw_hbm_ref,
    mw_ref,
    sw_ref,
    decay_ref,
    filter_ref,
    own_ref,
    z0_ref,
    se_ref,
    square_ref,
    taps_ref,
    heads_ref,
    m_ref,
    s_ref,
    raw_ref,
    held_ref,
    sems,
):
    rows, channels = own_ref.shape
    tiles = rows // 8
    width = per * LANES
    nothing = jnp.zeros((8, LANES), F32)

    def fetch(n):
        at = pl.ds(pl.multiple_of(n * width, width), width)
        return (
            pltpu.make_async_copy(s_hbm_ref.at[:, :, at], s_ref.at[:, :, at], sems.at[0, n]),
            pltpu.make_async_copy(m_hbm_ref.at[:, :, at], m_ref.at[:, :, at], sems.at[1, n]),
            pltpu.make_async_copy(raw_hbm_ref.at[:, at], raw_ref.at[:, at], sems.at[2, n]),
        )

    for n in range(channels // width):
        for copy in fetch(n):
            copy.start()
    square_ref[...] = jnp.zeros_like(square_ref)

    @pl.loop(0, channels // LANES)
    def _(k):
        @pl.when(k % per == 0)
        def _():
            for copy in fetch(k // per):
                copy.wait()

        lanes = lane_block(k)
        u = [s_ref[n, :, lanes].astype(F32) for n in range(3)]
        for n in range(3):
            heads_ref[n, :, lanes] = u[n][:8]
        s = [features(u[n], nothing, tap_rows(sw_ref, n, lanes)) for n in range(3)]
        ext = jnp.concatenate([nothing, (s[1] * s[2]).astype(BF16).astype(F32)], axis=0)
        total = filter_ref[0:1, lanes] * ext
        for j in range(1, LSE):
            total = total + filter_ref[j : j + 1, lanes] * roll(ext, j)
        mixed = s[0] * total[8:]
        se_ref[:, lanes] = mixed
        square_ref[8:, :] += mixed[8:] * mixed[8:]

        steps = lax.broadcasted_iota(jnp.int32, (MEDIUM_TAPS, LANES), 0).astype(F32)
        taps = raw_ref[:, lanes] * jnp.exp(-decay_ref[0:1, lanes] * steps)
        held_ref[...] = taps
        taps_ref[:, lanes] = taps
        u = [m_ref[n, :, lanes].astype(F32) for n in range(3)]
        for n in range(3):
            heads_ref[3 + n, :, lanes] = u[n][:8]
        z = [features(u[n], nothing, tap_rows(mw_ref, n, lanes)) for n in range(3)]
        z0_ref[:, lanes] = z[0]
        product = (z[1] * z[2]).astype(BF16).astype(F32)
        at = lax.broadcasted_iota(jnp.int32, (8, LANES), 0)
        head = jnp.where(at < 2, 0.0, product[:8])
        ext = jnp.concatenate([nothing, head, product[8:]], axis=0)
        total = [None] * tiles
        for r in range(8):
            shifted = roll(ext, r)
            tap = [tap_tile(held_ref, 8 * a + r) for a in range(MEDIUM_TAPS // 8)]
            for i in range(tiles):
                for a in range(min(i + 1, MEDIUM_TAPS // 8)):
                    at_tile = 8 * (i - a + 1)
                    term = tap[a] * shifted[at_tile : at_tile + 8]
                    total[i] = term if total[i] is None else total[i] + term
        own_ref[:, lanes] = jnp.concatenate(total, axis=0)


def own_part(mr, se, mr_short, se_short, raw, decay, se_filter, per):
    _, rows, channels = mr.shape
    mixed = jax.ShapeDtypeStruct((rows, channels), F32)
    mr, se, raw = (pltpu.with_memory_space_constraint(x, pltpu.HBM) for x in (mr, se, raw))
    return pl.pallas_call(
        functools.partial(own_kernel, per),
        out_shape=(
            mixed,
            mixed,
            mixed,
            jax.ShapeDtypeStruct((rows, LANES), F32),
            jax.ShapeDtypeStruct((MEDIUM_TAPS, channels), F32),
            jax.ShapeDtypeStruct((6, 8, channels), F32),
        ),
        in_specs=[pl.BlockSpec(memory_space=pltpu.HBM)] * 3 + [in_vmem()] * 4,
        out_specs=(in_vmem(),) * 6,
        scratch_shapes=[
            pltpu.VMEM(mr.shape, BF16),
            pltpu.VMEM(se.shape, BF16),
            pltpu.VMEM((MEDIUM_TAPS, channels), F32),
            pltpu.VMEM((MEDIUM_TAPS, LANES), F32),
            pltpu.SemaphoreType.DMA((3, channels // (per * LANES))),
        ],
        compiler_params=params(10),
        cost_estimate=cost(180 * rows * channels, 24 * rows * channels),
        name="own_part",
    )(mr, se, raw, mr_short, se_short, decay, se_filter)


def mix_kernel(
    packet_ref,
    own_ref,
    z0_ref,
    se_square_ref,
    taps_ref,
    heads_ref,
    mw_ref,
    sw_ref,
    filter_ref,
    head_ref,
    mr_ref,
    square_ref,
    last_ref,
    held_ref,
):
    rows, channels = own_ref.shape
    tiles = rows // 8
    chunk = MEDIUM_TAPS + 16
    nothing = jnp.zeros((8, LANES), F32)
    last_ref[...] = packet_ref[packet_ref.shape[0] - 16 :, :].astype(F32)
    square_ref[0] = se_square_ref[...]
    square_ref[1] = jnp.zeros((rows, LANES), F32)

    @pl.loop(0, channels // LANES)
    def _(k):
        lanes = lane_block(k)
        start = pl.multiple_of(k * chunk, 16)
        before = packet_ref[pl.ds(start, MEDIUM_TAPS), :].astype(F32)
        x = packet_ref[pl.ds(start + MEDIUM_TAPS, 16), :].astype(F32)
        x1, x2 = x[:8], x[8:]
        last = last_ref[pl.ds(k, 1), :]

        fronts = (roll(x1, 6), roll(x2, 6), roll(x2, 4))
        s = [
            features(heads_ref[n, :, lanes], fronts[n], tap_rows(sw_ref, n, lanes))
            for n in range(3)
        ]
        ext = jnp.concatenate([x1, (s[1] * s[2]).astype(BF16).astype(F32)], axis=0)
        total = filter_ref[0:1, lanes] * ext
        for j in range(1, LSE):
            total = total + filter_ref[j : j + 1, lanes] * roll(ext, j)
        mixed = s[0] * total[8:]
        head_ref[:, lanes] = mixed
        square_ref[0, :8, :] += mixed * mixed

        taps = taps_ref[:, lanes]
        held_ref[...] = taps
        front2 = jnp.where(row_is(8, 7), last, roll(before[:8], 6))
        fronts = (roll(x2, 2), x2, front2)
        z = [
            features(heads_ref[3 + n, :, lanes], fronts[n], tap_rows(mw_ref, n, lanes))
            for n in range(3)
        ]
        first = (z[1] * z[2]).astype(BF16).astype(F32)
        padded = jnp.concatenate([taps, jnp.zeros((rows - MEDIUM_TAPS, LANES), F32)], axis=0)
        base = own_ref[:, lanes] + padded * first[0:1] + roll(padded, 1) * first[1:2]
        total = [base[8 * i : 8 * i + 8] for i in range(tiles)]
        ext = jnp.concatenate([before, nothing], axis=0)
        count = MEDIUM_TAPS // 8
        for r in range(8):
            shifted = roll(ext, r)
            tap = [tap_tile(held_ref, 8 * a + r) for a in range(count)]
            for i in range(count):
                for a in range(i if r else i + 1, count):
                    at_tile = 8 * (i - a + count)
                    total[i] = total[i] + tap[a] * shifted[at_tile : at_tile + 8]
        z0 = jnp.concatenate([z[0], z0_ref[8:, lanes]], axis=0)
        mixed = z0 * jnp.concatenate(total, axis=0)
        mr_ref[:, lanes] = mixed
        square_ref[1] += mixed * mixed


def mix(packet, own, z0, se_square, taps, heads, mr_short, se_short, se_filter):
    rows, channels = own.shape
    return pl.pallas_call(
        mix_kernel,
        out_shape=(
            jax.ShapeDtypeStruct((8, channels), F32),
            jax.ShapeDtypeStruct((rows, channels), F32),
            jax.ShapeDtypeStruct((2, rows, LANES), F32),
        ),
        in_specs=[in_vmem()] * 9,
        out_specs=(in_vmem(),) * 3,
        scratch_shapes=[pltpu.VMEM((16, LANES), F32), pltpu.VMEM((MEDIUM_TAPS, LANES), F32)],
        compiler_params=params(),
        cost_estimate=cost(1, 1),
        name="mix",
    )(packet, own, z0, se_square, taps, heads, mr_short, se_short, se_filter)


def score_kernel(
    per, q_ref, k_ref, before_ref, v_ref, probs_ref, out_ref, inverse_ref, square_ref, bias_ref
):
    rows, channels = q_ref.shape
    at = lax.broadcasted_iota(jnp.int32, (rows, 2 * rows), 0)
    key = lax.broadcasted_iota(jnp.int32, (rows, 2 * rows), 1)
    valid = (key <= at + rows) & ((key >= rows) | (lax.axis_index("ctx") > 0))
    bias_ref[...] = jnp.where(valid, 0.0, -1e30)
    square_ref[...] = jnp.zeros_like(square_ref)
    factor = math.log2(math.e) / math.sqrt(HD)
    zeros, ones = jnp.zeros((rows, LANES), BF16), jnp.ones((rows, LANES), BF16)

    @pl.loop(0, channels // (LANES * per))
    def _(group):
        for n in range(per):
            head = group * per + n
            lanes = lane_block(head)
            both = jnp.concatenate([before_ref[:, lanes], k_ref[:, lanes]], axis=0)
            scores = lax.dot_general(
                q_ref[:, lanes], both, (((1,), (1,)), ((), ())), preferred_element_type=F32
            )
            scores = scores + bias_ref[...]
            top = jnp.max(scores, axis=-1, keepdims=True)
            probs = jnp.exp2((scores - top) * factor).astype(BF16)
            probs_ref[head] = probs[:, :rows]
            own = jnp.concatenate(
                [
                    jnp.concatenate([zeros, v_ref[:, lanes]], axis=0),
                    jnp.concatenate([ones, ones], axis=0),
                ],
                axis=1,
            )
            total = jnp.dot(probs, own, preferred_element_type=F32)
            inverse = 1.0 / total[:, LANES:]
            inverse_ref[:, lanes] = inverse
            out_ref[:, lanes] = total[:, :LANES] * inverse


def score(queries, keys, before, values, per):
    rows, channels = queries.shape
    flat = jax.ShapeDtypeStruct((rows, channels), F32)
    return pl.pallas_call(
        functools.partial(score_kernel, per),
        out_shape=(
            jax.ShapeDtypeStruct((channels // HD, rows, rows), BF16),
            flat,
            flat,
            jax.ShapeDtypeStruct((1, rows, LANES), F32),
        ),
        in_specs=[in_vmem()] * 4,
        out_specs=(in_vmem(),) * 4,
        scratch_shapes=[pltpu.VMEM((rows, 2 * rows), F32)],
        compiler_params=params(),
        cost_estimate=cost(
            8 * rows * rows * channels, 14 * rows * channels, 4 * rows * rows * channels // HD
        ),
        name="score",
    )(queries, keys, before, values)


def value_kernel(first, probs_ref, before_ref, own_ref, inverse_ref, square_in_ref, out_ref, square_ref):
    square = square_in_ref[0]
    for k in range(before_ref.shape[1] // LANES):
        lanes = slice((first + k) * LANES, (first + k + 1) * LANES)
        total = own_ref[:, lanes] + inverse_ref[:, lanes] * jnp.dot(
            probs_ref[first + k],
            before_ref[:, k * LANES : (k + 1) * LANES],
            preferred_element_type=F32,
        )
        out_ref[:, lanes] = total
        square = square + total * total
    square_ref[0] = square


def value_mix(first, probs, before, own, inverse, square):
    rows, channels = before.shape
    return pl.pallas_call(
        functools.partial(value_kernel, first),
        out_shape=(
            jax.ShapeDtypeStruct(own.shape, F32),
            jax.ShapeDtypeStruct((1, rows, LANES), F32),
        ),
        in_specs=[in_vmem()] * 5,
        out_specs=(in_vmem(),) * 2,
        input_output_aliases={2: 0},
        compiler_params=params(),
        cost_estimate=cost(1, 1),
        name="value_mix",
    )(probs, before, own, inverse, square)


def normalize_kernel(count, panels, pieces, with_head, *refs):
    square_refs, refs = refs[:panels], refs[panels:]
    mixed_refs, refs = refs[:count], refs[count:]
    if with_head:
        head_ref, refs = refs[0], refs[1:]
    out_refs, (held_ref, sems) = refs[:count], refs[count:]
    rows = mixed_refs[0].shape[0]
    piece = rows // pieces
    copies = []
    for n in range(count):
        square = square_refs[0][n]
        for ref in square_refs[1:]:
            square = square + ref[n]
        scale = lax.rsqrt(jnp.sum(square, axis=-1, keepdims=True) * (1.0 / CHANNELS) + 1e-06)
        for m in range(pieces):
            at = slice(m * piece, (m + 1) * piece)
            value = mixed_refs[n][at, :]
            if with_head and n == 0 and m == 0:
                value = jnp.concatenate([head_ref[...], value[8:]], axis=0)
            held_ref[n, at, :] = (value * scale[at]).astype(BF16)
            copy = pltpu.make_async_copy(
                held_ref.at[n, pl.ds(m * piece, piece)],
                out_refs[n].at[pl.ds(m * piece, piece)],
                sems.at[n, m],
            )
            copy.start()
            copies.append(copy)
    for copy in copies:
        copy.wait()


def normalize(squares, mixed, head=None, pieces=1):
    rows, channels = mixed[0].shape
    count = len(mixed)
    operands = (*squares, *mixed) + (() if head is None else (head,))
    return pl.pallas_call(
        functools.partial(normalize_kernel, count, len(squares), pieces, head is not None),
        out_shape=(jax.ShapeDtypeStruct((rows, channels), BF16),) * count,
        in_specs=[in_vmem()] * len(operands),
        out_specs=(pl.BlockSpec(memory_space=pl.ANY),) * count,
        scratch_shapes=[
            pltpu.VMEM((count, rows, channels), BF16),
            pltpu.SemaphoreType.DMA((count, pieces)),
        ],
        compiler_params=params(),
        cost_estimate=cost(1, 1),
        name="normalize",
    )(*operands)


def from_behind(value):
    count = lax.axis_size("ctx")
    return lax.ppermute(value, "ctx", [(source, source + 1) for source in range(count - 1)])


def of_panels(square):
    count = lax.axis_size("panel")
    return [square] + [
        lax.ppermute(square, "panel", [(n, (n + shift) % count) for n in range(count)])
        for shift in range(1, count)
    ]


def body(se, se_short, se_filter, mr, mr_short, raw, decay, queries, keys, values):
    last_heads = 3 * (queries.shape[1] // HD) // 8
    key_before = from_behind(keys)
    packet, mr_taps, se_taps, decay, filter_taps, most, rest = pack(
        se, mr, se_short, mr_short, decay[None, :], se_filter, values, last_heads, 4
    )
    packet = from_behind(packet)
    own, z0, se_mix, se_square, taps, heads = own_part(
        mr, se, mr_taps, se_taps, raw, decay, filter_taps, 4
    )
    most, own = lax.optimization_barrier((most, own))
    most_before = from_behind(most)
    probs, attended, inverse, square = score(queries, keys, key_before, values, 4)
    rest, attended = lax.optimization_barrier((rest, attended))
    rest_before = from_behind(rest)
    packet, attended = lax.optimization_barrier((packet, attended))
    head, mr_mix, mixed_square = mix(
        packet, own, z0, se_square, taps, heads, mr_taps, se_taps, filter_taps
    )
    se_out, mr_out = normalize(of_panels(mixed_square), (se_mix, mr_mix), head)
    most_before, se_out, mr_out = lax.optimization_barrier((most_before, se_out, mr_out))
    attended, square = value_mix(0, probs, most_before, attended, inverse, square)
    rest_before, attended = lax.optimization_barrier((rest_before, attended))
    first = most.shape[1] // HD
    attended, square = value_mix(first, probs, rest_before, attended, inverse, square)
    (attn_out,) = normalize(of_panels(square), (attended,))
    return se_out, mr_out, attn_out


def solution(mesh):
    placed = (
        P(None, "ctx", "panel"),
        P(None, None, "panel"),
        P(None, "panel"),
        P(None, "ctx", "panel"),
        P(None, None, "panel"),
        P(None, "panel"),
        P("panel"),
        P("ctx", "panel"),
        P("ctx", "panel"),
        P("ctx", "panel"),
    )
    return jax.shard_map(
        body,
        mesh=mesh,
        in_specs=placed,
        out_specs=(P("ctx", "panel"), P("ctx", "panel"), P("ctx", "panel")),
        check_vma=False,
    )
```
